32 devices in a mesh: dp: 8 (over z, x), ctx: 4 (over y, core).
Axes of the slice: x: 2, y: 2, z: 4, core: 2. Of those that a mesh axis runs over, the one named last changes fastest.
Arguments:
- tokens: bfloat16 [8, 2048, 1152], P('dp', 'ctx'), may hold values from -6 to 6
- cotangent: bfloat16 [8, 2048, 1152], P('dp', 'ctx'), may hold values from -6 to 6
- lengths: int32 [8, 2], P('dp'), may hold values from 512 to 1536, as said below
- w_qkv: float32 [1152, 1536], P(('dp', 'ctx')), may hold values from -0.1875 to 0.1875
- w_out: float32 [1024, 1152], P(('dp', 'ctx')), may hold values from -0.1875 to 0.1875
- w_gate_up: float32 [1152, 13824], P(('dp', 'ctx')), may hold values from -0.1875 to 0.1875
- w_down: float32 [6912, 1152], P(('dp', 'ctx')), may hold values from -0.078125 to 0.078125
- gains: float32 [4, 1152], P(None, ('dp', 'ctx')), may hold values from 0.4 to 5
- head_gains: float32 [2, 256], P(None, ('dp', 'ctx')), may hold values from 0.5 to 1.5
- first_qkv: float32 [1152, 1536], P(('dp', 'ctx')), may hold values from -0.00012207031 to 0.00012207031
- first_out: float32 [1024, 1152], P(('dp', 'ctx')), may hold values from -0.00012207031 to 0.00012207031
- first_gate_up: float32 [1152, 13824], P(('dp', 'ctx')), may hold values from -0.00012207031 to 0.00012207031
- first_down: float32 [6912, 1152], P(('dp', 'ctx')), may hold values from -0.00012207031 to 0.00012207031
- first_gains: float32 [4, 1152], P(None, ('dp', 'ctx')), may hold values from -0.00048828125 to 0.00048828125
- first_head: float32 [2, 256], P(None, ('dp', 'ctx')), may hold values from -0.00048828125 to 0.00048828125
- second_qkv: float32 [1152, 1536], P(('dp', 'ctx')), may hold values from 1.9745092e-09 to 7.823528e-09
- second_out: float32 [1024, 1152], P(('dp', 'ctx')), may hold values from 1.9745092e-09 to 7.823528e-09
- second_gate_up: float32 [1152, 13824], P(('dp', 'ctx')), may hold values from 1.9745092e-09 to 7.823528e-09
- second_down: float32 [6912, 1152], P(('dp', 'ctx')), may hold values from 1.9745092e-09 to 7.823528e-09
- second_gains: float32 [4, 1152], P(None, ('dp', 'ctx')), may hold values from 3.129411e-08 to 1.2666663e-07
- second_head: float32 [2, 256], P(None, ('dp', 'ctx')), may hold values from 3.129411e-08 to 1.2666663e-07
Outputs:
- output: bfloat16 [8, 2048, 1152], P('dp', 'ctx')
- input_grad: float32 [8, 2048, 1152], P('dp', 'ctx')
- new_qkv: float32 [1152, 1536], P(('dp', 'ctx'))
- new_out: float32 [1024, 1152], P(('dp', 'ctx'))
- new_gate_up: float32 [1152, 13824], P(('dp', 'ctx'))
- new_down: float32 [6912, 1152], P(('dp', 'ctx'))
- new_gains: float32 [4, 1152], P(None, ('dp', 'ctx'))
- new_head_gains: float32 [2, 256], P(None, ('dp', 'ctx'))
- new_first_qkv: float32 [1152, 1536], P(('dp', 'ctx'))
- new_first_out: float32 [1024, 1152], P(('dp', 'ctx'))
- new_first_gate_up: float32 [1152, 13824], P(('dp', 'ctx'))
- new_first_down: float32 [6912, 1152], P(('dp', 'ctx'))
- new_first_gains: float32 [4, 1152], P(None, ('dp', 'ctx'))
- new_first_head: float32 [2, 256], P(None, ('dp', 'ctx'))
- new_second_qkv: float32 [1152, 1536], P(('dp', 'ctx'))
- new_second_out: float32 [1024, 1152], P(('dp', 'ctx'))
- new_second_gate_up: float32 [1152, 13824], P(('dp', 'ctx'))
- new_second_down: float32 [6912, 1152], P(('dp', 'ctx'))
- new_second_gains: float32 [4, 1152], P(None, ('dp', 'ctx'))
- new_second_head: float32 [2, 256], P(None, ('dp', 'ctx'))
- grad_norm: float32 [], replicated
The draws below stay inside these ranges and needn't reach their ends.
Inputs may be any that keep to these rules, and one draw needn't show every extreme that they name: `lengths`: each row holds 1536 and 512 in either order, so it sums to 2048.
All inputs are finite; a program needn't handle non-finite values.
Results may differ from the reference program's by a relative error of at most 0.019.
The reference program's roundings to bfloat16 on the way count: a program that leaves them out, or rounds other values in their place, can miss the bound.
Values may be sent and summed in bfloat16 or wider, within the bound.
No kernel may reach another device: no remote copies, remote signals or barrier semaphores. Data moves between devices by JAX's collectives and lax.ppermute only.
A program may use at most 384 MiB of HBM per device.

```python
import math
import jax
import jax.numpy as jnp
from jax import lax

D = 1152
H = 4
HD = 256
FF = 6912
STEP = 10
SEQ = 2048
GROUPS = 8
MOST = 1536
PARAMS = 26842112
N_CTX = 4


def draw_gains(key, part):
    key = jax.random.fold_in(key, 7)
    place = jnp.arange(D, dtype=jnp.float32) / (D - 1)
    rise = 0.6 * jnp.exp(jnp.log(3.0) * place)
    factor = jax.random.uniform(key, (4, D), jnp.float32, 0.85, 1.15)
    return (rise[None, :] * factor).astype(jnp.float32)


def draw_lengths(key, part):
    key = jax.random.fold_in(key, 11)
    order_bit = jax.random.randint(key, (GROUPS,), 0, 2, dtype=jnp.int32)
    first_len = jnp.where(order_bit == 1, MOST, SEQ - MOST).astype(jnp.int32)
    return jnp.stack([first_len, (SEQ - first_len).astype(jnp.int32)], axis=1).astype(jnp.int32)


def block_scale(rng, shape, cuts, least, largest):
    loudness = 1.0
    for dim, parts in cuts:
        steps = jax.random.uniform(jax.random.fold_in(jax.random.fold_in(rng, 6), dim), (parts,), jnp.float32, least / len(cuts), largest / len(cuts))
        loudness = loudness * jnp.repeat(jnp.exp(steps), shape[dim] // parts).reshape((-1,) + (1,) * (len(shape) - 1 - dim))
    return loudness


def bell_draw(rng, dims, deviation, limit, split=(), held_as=jnp.bfloat16):
    factor_of = block_scale(rng, dims, split, -0.22, 0.18) if split else 1.0
    values = jax.random.normal(rng, dims, jnp.float32) * deviation * factor_of
    return jnp.minimum(jnp.maximum(values, -limit), limit).astype(held_as)


def setup_inputs(seed: int = 0) -> dict:
    key_of = jax.random.split(jax.random.key(seed), 22)
    return {
        "tokens": bell_draw(key_of[0], (GROUPS, SEQ, D), 1.0, 6.0, ((0, 8), (1, 4))),
        "cotangent": bell_draw(key_of[1], (GROUPS, SEQ, D), 1.0, 6.0, ((0, 8), (1, 4))),
        "lengths": draw_lengths(jax.random.fold_in(key_of[21], 71), 0),
        "w_qkv": bell_draw(key_of[3], (D, (H + 2) * HD), D ** -0.5, 0.1875, ((0, 32),), jnp.float32),
        "w_out": bell_draw(key_of[4], (H * HD, D), (H * HD) ** -0.5, 0.1875, ((0, 32),), jnp.float32),
        "w_gate_up": bell_draw(key_of[5], (D, 2 * FF), D ** -0.5, 0.1875, ((0, 32),), jnp.float32),
        "w_down": bell_draw(key_of[6], (FF, D), FF ** -0.5, 0.078125, ((0, 32),), jnp.float32),
        "gains": draw_gains(jax.random.fold_in(key_of[21], 71), 0),
        "head_gains": jnp.clip(1.0 + 0.1 * jax.random.normal(key_of[8], (2, HD), jnp.float32), 0.5, 1.5),
        "first_qkv": bell_draw(key_of[9], (D, (H + 2) * HD), (0.11 * PARAMS ** -0.5), 0.00012207031, ((0, 32),), jnp.float32),
        "first_out": bell_draw(key_of[10], (H * HD, D), (0.11 * PARAMS ** -0.5), 0.00012207031, ((0, 32),), jnp.float32),
        "first_gate_up": bell_draw(key_of[11], (D, 2 * FF), (0.11 * PARAMS ** -0.5), 0.00012207031, ((0, 32),), jnp.float32),
        "first_down": bell_draw(key_of[12], (FF, D), (0.11 * PARAMS ** -0.5), 0.00012207031, ((0, 32),), jnp.float32),
        "first_gains": bell_draw(key_of[13], (4, D), (0.44 * PARAMS ** -0.5), 0.00048828125, ((1, 32),), jnp.float32),
        "first_head": bell_draw(key_of[14], (2, HD), (0.44 * PARAMS ** -0.5), 0.00048828125, ((1, 32),), jnp.float32),
        "second_qkv": jnp.clip(jnp.exp(math.log(7.82352760353433e-09) - 1.3768157 * jax.random.uniform(key_of[15], (D, (H + 2) * HD), jnp.float32) ** block_scale(key_of[15], (D, (H + 2) * HD), ((0, 32),), -0.2, 0.2)), 1.9745092227907435e-09, 7.82352760353433e-09),
        "second_out": jnp.clip(jnp.exp(math.log(7.82352760353433e-09) - 1.3768157 * jax.random.uniform(key_of[16], (H * HD, D), jnp.float32) ** block_scale(key_of[16], (H * HD, D), ((0, 32),), -0.2, 0.2)), 1.9745092227907435e-09, 7.82352760353433e-09),
        "second_gate_up": jnp.clip(jnp.exp(math.log(7.82352760353433e-09) - 1.3768157 * jax.random.uniform(key_of[17], (D, 2 * FF), jnp.float32) ** block_scale(key_of[17], (D, 2 * FF), ((0, 32),), -0.2, 0.2)), 1.9745092227907435e-09, 7.82352760353433e-09),
        "second_down": jnp.clip(jnp.exp(math.log(7.82352760353433e-09) - 1.3768157 * jax.random.uniform(key_of[18], (FF, D), jnp.float32) ** block_scale(key_of[18], (FF, D), ((0, 32),), -0.2, 0.2)), 1.9745092227907435e-09, 7.82352760353433e-09),
        "second_gains": jnp.clip(jnp.exp(math.log(1.2666663451454951e-07) - 1.3981288 * jax.random.uniform(key_of[19], (4, D), jnp.float32) ** block_scale(key_of[19], (4, D), ((1, 32),), -0.2, 0.2)), 3.129411041413732e-08, 1.2666663451454951e-07),
        "second_head": jnp.clip(jnp.exp(math.log(1.2666663451454951e-07) - 1.3981288 * jax.random.uniform(key_of[20], (2, HD), jnp.float32) ** block_scale(key_of[20], (2, HD), ((1, 32),), -0.2, 0.2)), 3.129411041413732e-08, 1.2666663451454951e-07),
    }


EPSILON = 1e-06
ROPE_BASE = 1000000.0
BETA_ONE = 0.9
BETA_TWO = 0.95
ADAM_EPSILON = 1e-08
WEIGHT_DECAY = 0.1
GAIN_RATE = 1.0
HIGHEST = lax.Precision.HIGHEST

@jax.custom_vjp
def low(v):
    return lax.optimization_barrier(v.astype(jnp.bfloat16)).astype(jnp.float32)

@jax.custom_vjp
def low_back(v):
    return v

def low_keep(v):
    return (low(v), None)

def low_pass(kept, grad):
    return (grad,)

def back_keep(v):
    return (v, None)

def back_low(kept, grad):
    return (low(grad),)
low.defvjp(low_keep, low_pass)
low_back.defvjp(back_keep, back_low)

def stored_positions(stored, count, per_device):
    half = per_device // 2
    device = stored // per_device
    within = stored % per_device
    block = jnp.where(within < half, device, 2 * count - 1 - device)
    return (block * half + within % half).astype(jnp.int32)

def document_of(positions, doc_lengths):
    ends = jnp.cumsum(doc_lengths).astype(jnp.int32)
    starts = (ends - doc_lengths).astype(jnp.int32)
    inside = (positions[:, None] >= starts[None, :]) & (positions[:, None] < ends[None, :])
    numbers = jnp.arange(doc_lengths.shape[0], dtype=jnp.int32)
    doc_ids = lax.optimization_barrier(jnp.sum(jnp.where(inside, numbers[None, :], 0), axis=1)).astype(jnp.int32)
    doc_starts = lax.optimization_barrier(jnp.sum(jnp.where(inside, starts[None, :], 0), axis=1)).astype(jnp.int32)
    return (doc_ids, doc_starts)

def rope_tables(offsets, width):
    half = width // 2
    freq = jnp.exp(-jnp.log(ROPE_BASE) * jnp.arange(half, dtype=jnp.float32) * (2.0 / width))
    angle = offsets.astype(jnp.float32)[:, None] * freq[None, :]
    return (jnp.cos(angle), jnp.sin(angle))

def rotate(field, cos_t, sin_t):
    half = field.shape[-1] // 2
    first_half = field[..., :half]
    second_half = field[..., half:]
    return jnp.concatenate([first_half * cos_t - second_half * sin_t, second_half * cos_t + first_half * sin_t], axis=-1)

def rms_norm(field, gain):
    return field * lax.rsqrt(lax.optimization_barrier(jnp.mean(field * field, axis=-1, keepdims=True)) + EPSILON) * gain

def layer_group(inputs, doc_lengths, w_qkv, w_out, w_gate_up, w_down, gains, head_gains):
    seq_len = inputs.shape[0]
    stored = jnp.arange(seq_len, dtype=jnp.int32)
    positions = stored_positions(stored, N_CTX, seq_len // N_CTX)
    doc_ids, doc_starts = document_of(positions, doc_lengths)
    allowed = (doc_ids[:, None] == doc_ids[None, :]) & (positions[None, :] <= positions[:, None])
    cos_t, sin_t = rope_tables(positions - doc_starts, HD)
    normed = low(rms_norm(inputs, gains[0]))
    qkv = low_back(jnp.dot(normed, w_qkv, precision=HIGHEST, preferred_element_type=jnp.float32))
    query = qkv[:, :H * HD].reshape(seq_len, H, HD)
    key_part = qkv[:, H * HD:(H + 1) * HD]
    value_part = low(qkv[:, (H + 1) * HD:])
    query_low = low(rotate(rms_norm(query, head_gains[0]), cos_t[:, None, :], sin_t[:, None, :]))
    key_low = low(rotate(rms_norm(key_part, head_gains[1]), cos_t, sin_t))
    scores = low_back(jnp.einsum('qhd,kd->hqk', query_low, key_low, precision=HIGHEST) * HD ** (-0.5))
    probs = jax.nn.softmax(jnp.where(allowed[None], scores, -1e+30), axis=-1)
    mixed = jnp.einsum('hqk,kd->qhd', low(probs), value_part, precision=HIGHEST)
    mixed = low(low_back(mixed.reshape(seq_len, H * HD)))
    proj = low_back(jnp.dot(mixed, w_out, precision=HIGHEST, preferred_element_type=jnp.float32))
    resid = inputs + rms_norm(proj, gains[1])
    pre_ff = low(rms_norm(resid, gains[2]))
    gate_up = low_back(jnp.dot(pre_ff, w_gate_up, precision=HIGHEST, preferred_element_type=jnp.float32))
    hidden = low(jax.nn.gelu(gate_up[:, :FF], approximate=True) * gate_up[:, FF:])
    ffn = low_back(jnp.dot(hidden, w_down, precision=HIGHEST, preferred_element_type=jnp.float32))
    return resid + rms_norm(ffn, gains[3])

def adam_update(weight, first, second, grad, rate, decay):
    first_new = BETA_ONE * first + (1.0 - BETA_ONE) * grad
    second_new = BETA_TWO * second + (1.0 - BETA_TWO) * grad * grad
    first_hat = first_new / (1.0 - BETA_ONE ** STEP)
    second_hat = second_new / (1.0 - BETA_TWO ** STEP)
    updated = weight - rate * (first_hat / (jnp.sqrt(second_hat) + ADAM_EPSILON) + decay * weight)
    return (updated, first_new, second_new)

def reference(tokens, cotangent, lengths, w_qkv, w_out, w_gate_up, w_down, gains, head_gains, first_qkv, first_out, first_gate_up, first_down, first_gains, first_head, second_qkv, second_out, second_gate_up, second_down, second_gains, second_head):

    def forward(inputs, a_qkv, a_out, a_gate_up, a_down, a_gains, a_head):
        r_qkv, r_out, r_gate_up, r_down = (low(a_qkv), low(a_out), low(a_gate_up), low(a_down))
        r_gains, r_head = (low(a_gains), low(a_head))

        def one_group(pair):
            return layer_group(pair[0], pair[1], r_qkv, r_out, r_gate_up, r_down, r_gains, r_head)
        return lax.map(jax.checkpoint(one_group), (inputs, lengths))
    inputs = tokens.astype(jnp.float32)
    result, pull = jax.vjp(forward, inputs, w_qkv, w_out, w_gate_up, w_down, gains, head_gains)
    grads = pull(cotangent.astype(jnp.float32))
    weight_grads = grads[1:]
    squares = jnp.float32(0.0)
    for grad in weight_grads:
        squares = squares + jnp.sum(grad * grad)
    grad_norm = jnp.sqrt(squares)
    factor = 1.0 / jnp.maximum(grad_norm, 1.0)
    weights = (w_qkv, w_out, w_gate_up, w_down, gains, head_gains)
    firsts = (first_qkv, first_out, first_gate_up, first_down, first_gains, first_head)
    seconds = (second_qkv, second_out, second_gate_up, second_down, second_gains, second_head)
    rates = (D ** (-0.5), (H * HD) ** (-0.5), D ** (-0.5), FF ** (-0.5), GAIN_RATE, GAIN_RATE)
    decays = (WEIGHT_DECAY, WEIGHT_DECAY, WEIGHT_DECAY, WEIGHT_DECAY, 0.0, 0.0)
    updates = [adam_update(weights[i], firsts[i], seconds[i], weight_grads[i] * factor, rates[i], decays[i]) for i in range(6)]
    return (result.astype(jnp.bfloat16), grads[0], updates[0][0], updates[1][0], updates[2][0], updates[3][0], updates[4][0], updates[5][0], updates[0][1], updates[1][1], updates[2][1], updates[3][1], updates[4][1], updates[5][1], updates[0][2], updates[1][2], updates[2][2], updates[3][2], updates[4][2], updates[5][2], grad_norm)
```

```python
from functools import partial

import jax
import jax.numpy as jnp
from jax import lax
from jax.experimental import pallas as pl
from jax.experimental.pallas import tpu as pltpu
from jax.sharding import PartitionSpec as P

D = 1152
H = 4
HD = 256
FF = 6912
STEP = 10

EPSILON = 1e-06
ROPE_BASE = 1000000.0
BETA_ONE = 0.9
BETA_TWO = 0.95
ADAM_EPSILON = 1e-08
WEIGHT_DECAY = 0.1
GAIN_RATE = 1.0


def rope_tables(offsets, width):
    half = width // 2
    freq = jnp.exp(-jnp.log(ROPE_BASE) * jnp.arange(half, dtype=jnp.float32) * (2.0 / width))
    angle = offsets.astype(jnp.float32)[:, None] * freq[None, :]
    return (jnp.cos(angle), jnp.sin(angle))


def adam_update(weight, first, second, grad, rate, decay):
    first_new = BETA_ONE * first + (1.0 - BETA_ONE) * grad
    second_new = BETA_TWO * second + (1.0 - BETA_TWO) * grad * grad
    first_hat = first_new / (1.0 - BETA_ONE**STEP)
    second_hat = second_new / (1.0 - BETA_TWO**STEP)
    updated = weight - rate * (first_hat / (jnp.sqrt(second_hat) + ADAM_EPSILON) + decay * weight)
    return (updated, first_new, second_new)


def exchange(parts, axis):
    return lax.all_to_all(parts, axis, split_axis=0, concat_axis=0, tiled=True)


def swap(value, bit):
    count = lax.axis_size("ctx")
    return lax.ppermute(value, "ctx", [(i, i ^ bit) for i in range(count)])


def swap_dp(value, bit):
    count = lax.axis_size("dp")
    return lax.ppermute(value, "dp", [(i, i ^ bit) for i in range(count)])


def gather_ctx(block):
    far = swap(block, 2)
    return [block, swap(block, 1), far, swap(far, 1)]


def add_low(a, b):
    return a + b


def reduce_ctx(blocks):
    near, far = jnp.concatenate([blocks[1], blocks[3]]), None
    near = swap(near, 1)
    size = blocks[0].shape[0]
    far = swap(add_low(blocks[2], near[size:]), 2)
    mine = blocks[0].astype(jnp.float32) + near[:size].astype(jnp.float32)
    return mine + far.astype(jnp.float32)


def reorder(value, bit, rows):
    parts = [value[j * rows : (j + 1) * rows] for j in range(value.shape[0] // rows)]
    return jnp.concatenate([parts[j ^ bit] for j in range(len(parts))])


def sum_all(value):
    bit = 1
    while bit < lax.axis_size("ctx"):
        value = value + swap(value, bit)
        bit *= 2
    bit = 1
    while bit < lax.axis_size("dp"):
        value = value + swap_dp(value, bit)
        bit *= 2
    return value


def tie(value, *tokens):
    return lax.optimization_barrier((value, *tokens))[0]


class Ring:
    def __init__(self):
        count = self.count = lax.axis_size("dp")
        self.ctx = lax.axis_size("ctx")
        self.order = list(range(0, count, 2)) + list(range(count - 1, 0, -2))
        self.hops = (count // 2, count - 1 - count // 2)
        table = [
            [self.order[(self.order.index(i) + sense * step) % count] for step in range(count)]
            for sense in (1, -1)
            for i in range(count)
        ]
        row = (lax.axis_index("ctx") % 2) * count + lax.axis_index("dp")
        self.places = lax.dynamic_slice(
            jnp.array(table, jnp.int32), (row, 0), (1, count), allow_negative_indices=False
        )[0]

    def send(self, value, way):
        pairs = []
        for place, source in enumerate(self.order):
            for c in range(self.ctx):
                target = self.order[(place + (way if c % 2 == 0 else -way)) % self.count]
                pairs.append((source * self.ctx + c, target * self.ctx + c))
        return lax.ppermute(value, ("dp", "ctx"), pairs)

    def ways(self, hop):
        return [way for way, last in zip((1, -1), self.hops) if hop <= last]


class Gather:
    def __init__(self, ring, block):
        self.ring, self.hop = ring, 0
        self.held = {1: block, -1: block}
        self.parts, self.steps = [block], [0]

    def advance(self, *tokens):
        self.hop += 1
        for way in self.ring.ways(self.hop):
            self.held[way] = self.ring.send(tie(self.held[way], *tokens), way)
            self.parts.append(self.held[way])
            self.steps.append(-way * self.hop % self.ring.count)
        return list(self.held.values())

    def finish(self):
        while self.hop < self.ring.hops[0]:
            self.advance()
        return self

    def whole(self):
        block = self.parts[0]
        rows = block.shape[0]
        found = jnp.zeros((rows * self.ring.count, block.shape[1]), block.dtype)
        starts = self.ring.places * rows
        for step, part in zip(self.steps, self.parts):
            found = lax.dynamic_update_slice(
                found, part, (starts[step], 0), allow_negative_indices=False
            )
        return found


class Reduce:
    def __init__(self, ring, whole):
        self.ring, self.source, self.hop = ring, whole, ring.hops[0]
        self.rows = whole.shape[0] // ring.count
        self.starts = ring.places * self.rows
        self.held = {way: self.piece(way * last) for way, last in zip((1, -1), ring.hops)}
        self.total = None

    def piece(self, step):
        return lax.dynamic_slice(
            self.source,
            (self.starts[step % self.ring.count], 0),
            (self.rows, self.source.shape[1]),
            allow_negative_indices=False,
        )

    def tokens(self):
        return list(self.held.values())

    def send(self, *tokens):
        self.came = {
            way: self.ring.send(tie(self.held[way], *tokens), way) for way in self.ring.ways(self.hop)
        }
        return self

    def absorb(self, *tokens):
        for way, came in self.came.items():
            came = tie(came, *tokens) if tokens else came
            if self.hop > 1:
                self.held[way] = add_low(came, self.piece(way * (self.hop - 1)))
            else:
                mine = self.piece(0) if self.total is None else self.total
                self.total = mine.astype(jnp.float32) + came.astype(jnp.float32)
        self.hop -= 1
        return self.tokens() if self.total is None else [self.total]

    def finish(self):
        while self.hop > 0:
            self.send().absorb()
        return self.total


LOW = jnp.bfloat16
F32 = jnp.float32
TILE = 256
LONG = 6
SHORT = 2
GELU_A = 0.7978845608028654
GELU_B = 0.044715
VMEM = 56 * 2**20


def mm(a, b):
    return jnp.dot(a, b, preferred_element_type=F32)


def mm_nt(a, b):
    return lax.dot_general(a, b, (((1,), (1,)), ((), ())), preferred_element_type=F32)


def mm_tn(a, b):
    return lax.dot_general(a, b, (((0,), (0,)), ((), ())), preferred_element_type=F32)


def call(body, out_shape, in_specs, out_specs, args, grid=(1,), flops=0, scratch=(), into=(), prefetch=()):
    given = len(prefetch)
    used = len(in_specs)

    def kernel(*refs):
        body(*refs[: given + used], *refs[given + used + len(into) :])

    nbytes = sum(a.size * a.dtype.itemsize for a in args)
    nbytes += sum(o.size * o.dtype.itemsize for o in jax.tree.leaves(out_shape))
    return pl.pallas_call(
        kernel,
        out_shape=out_shape,
        grid_spec=pltpu.PrefetchScalarGridSpec(
            num_scalar_prefetch=given,
            grid=grid,
            in_specs=list(in_specs) + [pl.BlockSpec(memory_space=pl.ANY)] * len(into),
            out_specs=out_specs,
            scratch_shapes=list(scratch),
        ),
        compiler_params=pltpu.CompilerParams(vmem_limit_bytes=VMEM),
        cost_estimate=pl.CostEstimate(flops=flops // 16, bytes_accessed=nbytes // 16, transcendentals=0),
        input_output_aliases={given + used + i: i for i in range(len(into))},
    )(*prefetch, *args, *into)


def held(shape):
    return pl.BlockSpec(shape, lambda *_: (0,) * len(shape), pipeline_mode=pl.Buffered(1))


def like(shape, dtype):
    return jax.ShapeDtypeStruct(shape, dtype)


def scale_of(v):
    return lax.rsqrt(jnp.mean(v * v, axis=-1, keepdims=True) + EPSILON)


def norm_pull(v, s, g, dy):
    w = dy * g
    return s * w - v * (s * s * s) * jnp.mean(w * v, axis=-1, keepdims=True)


def turn(v, cos_t, sin_t, sign):
    half = v.shape[-1] // 2
    a, b = v[:, :half], v[:, half:]
    return jnp.concatenate([a * cos_t - sign * (b * sin_t), b * cos_t + sign * (a * sin_t)], axis=-1)


def stored_block(p):
    return jnp.where(p < 4, 2 * p, 2 * (7 - p) + 1)


def hidden_room(rows, dp):
    unit = max(16, 256 // dp)
    return -(-rows // unit) * unit


def pack_columns(w_gate_up, dp, ctx):
    rows, wide = w_gate_up.shape
    ff = wide // 2
    step = ff // (dp * ctx)
    room = hidden_room(step, dp)
    part = dp * room

    def body(w, out):
        zeros = [jnp.zeros((rows, room - step), F32)] if room > step else []
        for c in range(ctx):
            for side in range(2):
                cut = []
                for d in range(dp):
                    at = side * ff + (d * ctx + c) * step
                    cut += [w[:, at : at + step]] + zeros
                out[c, :, side * part : (side + 1) * part] = jnp.concatenate(cut, axis=1).astype(LOW)

    return call(
        body,
        like((ctx, rows, 2 * part), LOW),
        [held((rows, wide))],
        held((ctx, rows, 2 * part)),
        (w_gate_up,),
    )


def unpack_columns(parts, dp, ctx, step):
    rows, wide = parts.shape[1], parts.shape[2]
    part = wide // 2
    room = part // dp
    ff = dp * ctx * step

    def body(p, out):
        for c in range(ctx):
            own = p[c].astype(F32)
            for side in range(2):
                for d in range(dp):
                    at = side * ff + (d * ctx + c) * step
                    start = side * part + d * room
                    out[:, at : at + step] = own[:, start : start + step]

    return call(
        body,
        like((rows, 2 * ff), F32),
        [held(parts.shape)],
        held((rows, 2 * ff)),
        (parts,),
    )


class Blocks:
    def __init__(self, gathered, rows=None):
        block, self.cols = gathered.parts[0].shape
        self.rows = rows = rows or block
        count = gathered.ring.count
        self.height = rows * count
        if rows % 16:
            whole = gathered.whole().reshape(count, block, self.cols)[:, :rows]
            self.parts, self.steps = [whole.reshape(self.height, self.cols)], [0]
            self.rows = self.height
        else:
            self.parts, self.steps = gathered.parts, gathered.steps

    def specs(self):
        return [pl.BlockSpec(memory_space=pl.ANY)] * len(self.parts)

    def scratch(self):
        return [
            pltpu.VMEM((self.height, self.cols), LOW),
            pltpu.SemaphoreType.DMA((len(self.parts),)),
        ]

    def load(self, places, refs, room, sems):
        @pl.when(pl.program_id(0) == 0)
        def _():
            copies = []
            for i, (step, ref) in enumerate(zip(self.steps, refs)):
                at = pl.multiple_of(places[step] * self.rows, 16) if len(refs) > 1 else 0
                copies.append(
                    pltpu.make_async_copy(
                        ref.at[pl.ds(0, self.rows), :], room.at[pl.ds(at, self.rows), :], sems.at[i]
                    )
                )
            for copy in copies:
                copy.start()
            for copy in copies:
                copy.wait()


def unpack_small(gathered, first, dp, ctx, out_rows, gain_cols, head_cols):
    block, wide = gathered.parts[0].shape
    rows = block - first
    direct = first % 16 == 0 and rows % 16 == 0
    if direct:
        parts, steps = gathered.parts, gathered.steps
    else:
        parts, steps = [gathered.whole().reshape(dp, block, wide)[:, first:]], [0]
    half = out_rows // 2
    count = len(parts)

    def body(places, *refs):
        gain, head, out, room, sems = refs[count:]
        copies = []
        for i, ref in enumerate(refs[:count]):
            if direct:
                source, target = ref.at[pl.ds(first, rows), :], room.at[places[steps[i]]]
            else:
                source, target = ref, room
            copies.append(pltpu.make_async_copy(source, target, sems.at[i]))
        for copy in copies:
            copy.start()
        for copy in copies:
            copy.wait()
        lines = []
        for d in range(dp):
            extra = room[d, : 4 * ctx, :].astype(F32)
            lines += [extra[4 * c : 4 * c + 1] for c in range(ctx)]
            at, own = d * out_rows, room[d, 4 * ctx :, :]
            out[at : at + out_rows, :wide] = own[:out_rows]
            out[at : at + half, wide:] = own[out_rows:, : D - wide]
            out[at + half : at + out_rows, wide:] = own[out_rows:, D - wide :]
        for g in range(4):
            cut = [line[:, g * gain_cols : (g + 1) * gain_cols] for line in lines]
            gain[g : g + 1, :] = jnp.concatenate(cut, axis=1)
        for g in range(2):
            at = 4 * gain_cols + g * head_cols
            cut = [line[:, at : at + head_cols] for line in lines]
            head[g : g + 1, :] = jnp.concatenate(cut, axis=1)

    return call(
        body,
        [like((4, D), F32), like((2, HD), F32), like((HD, D), LOW)],
        [pl.BlockSpec(memory_space=pl.ANY)] * count,
        [held((4, D)), held((2, HD)), held((HD, D))],
        tuple(parts),
        scratch=[pltpu.VMEM((dp, rows, wide), LOW), pltpu.SemaphoreType.DMA((count,))],
        prefetch=(gathered.ring.places,),
    )


def input_stage(x, w_in, gain, head_rows, cos_t, sin_t, row_map, places):
    seq = x.shape[0]
    count = len(w_in.parts)

    def body(_, pl_ref, x0, x1, g, hg, cos, sin, *refs):
        q, k, v, raw, n_ref, w, sems = refs[count:]
        w_in.load(pl_ref, refs[:count], w, sems)
        for i, x_ref in enumerate((x0, x1)):
            at = slice(i * TILE, (i + 1) * TILE)
            xf = x_ref[...].astype(F32)
            n = (xf * scale_of(xf) * g[...]).astype(LOW)
            n_ref[at, :] = n
            y = mm(n, w[...])
            qy, ky = y[:, :HD], y[:, HD : 2 * HD]
            raw[at, :] = y[:, : 2 * HD]
            c, s = cos[at, :], sin[at, :]
            q[at, :] = turn(qy * scale_of(qy) * hg[0:1], c, s, 1.0).astype(LOW)
            k[at, :] = turn(ky * scale_of(ky) * hg[1:2], c, s, 1.0).astype(LOW)
            v[at, :] = y[:, 2 * HD :].astype(LOW)

    def block(cols):
        return pl.BlockSpec((2 * TILE, cols), lambda p, m, s: (p, 0))

    return call(
        body,
        [like((seq, HD), LOW)] * 3 + [like((seq, 2 * HD), F32), like((seq, D), LOW)],
        [
            pl.BlockSpec((TILE, D), lambda p, m, s: (m[2 * p], 0)),
            pl.BlockSpec((TILE, D), lambda p, m, s: (m[2 * p + 1], 0)),
            held((1, D)),
            held((2, HD)),
            block(HD // 2),
            block(HD // 2),
        ]
        + w_in.specs(),
        [block(HD)] * 3 + [block(2 * HD), block(D)],
        (x, x, gain, head_rows, cos_t, sin_t, *w_in.parts),
        grid=(seq // TILE // 2,),
        flops=2 * seq * D * 3 * HD,
        scratch=w_in.scratch(),
        prefetch=(row_map, places),
    )


def scores_of(q, k, doc_step):
    s = mm_nt(q, k) * HD ** (-0.5)
    row = lax.broadcasted_iota(jnp.int32, s.shape, 0) + doc_step * TILE
    col = lax.broadcasted_iota(jnp.int32, s.shape, 1)
    return jnp.where(col <= row, s, -1e30)


def attention(q, k, v, base):
    seq = q.shape[0]

    def body(b, q_ref, k_ref, v_ref, mixed, lse):
        for doc, count in enumerate((LONG, SHORT)):
            first = b[doc]
            for i in range(count):
                p = first + i
                at = pl.ds(pl.multiple_of(p * TILE, TILE), TILE)
                keys = pl.ds(pl.multiple_of(first * TILE, TILE), (i + 1) * TILE)
                s = scores_of(q_ref[at, :], k_ref[keys, :], i)
                peak = jnp.max(s, axis=-1, keepdims=True)
                e = jnp.exp(s - peak)
                total = jnp.sum(e, axis=-1, keepdims=True)
                lse[at, :] = peak + jnp.log(total)
                probs = (e * (1.0 / total)).astype(LOW)
                to = pl.ds(pl.multiple_of(stored_block(p) * TILE, TILE), TILE)
                mixed[to, :] = mm(probs, v_ref[keys, :]).astype(LOW)

    return call(
        body,
        [like((seq, HD), LOW), like((seq, 1), F32)],
        [held((seq, HD))] * 3,
        [held((seq, HD)), held((seq, 1))],
        (q, k, v),
        flops=4 * 24 * TILE * TILE * HD,
        prefetch=(base,),
    )


def attention_back(q, k, v, raw, lse, grads, head_rows, cos_t, sin_t, base):
    seq = q.shape[0]
    chip = seq // 2

    def pull_head(v_raw, g, dy, cos, sin):
        dy = turn(dy, cos, sin, -1.0)
        s = scale_of(v_raw)
        return norm_pull(v_raw, s, g, dy), jnp.sum(dy * v_raw * s, axis=0, keepdims=True)

    def body(b, q_ref, k_ref, v_ref, raw_ref, l_ref, *refs):
        hg, cos, sin, out, head_out, dk, dv, mixed_grad = refs[6:]
        for i in range(2):
            mine, near, far = refs[3 * i : 3 * i + 3]
            rows = pl.ds(pl.multiple_of((b[2] if i == 0 else 1 - b[2]) * chip, chip), chip)
            mixed_grad[rows, :] = (
                mine[0].astype(F32) + near[0].astype(F32) + far[...].astype(F32)
            ).astype(LOW)
        dk[...] = jnp.zeros_like(dk)
        dv[...] = jnp.zeros_like(dv)
        head_q = jnp.zeros((1, HD), F32)
        for doc, count in enumerate((LONG, SHORT)):
            first = b[doc]
            for i in range(count):
                p = first + i
                at = pl.ds(pl.multiple_of(p * TILE, TILE), TILE)
                keys = pl.ds(pl.multiple_of(first * TILE, TILE), (i + 1) * TILE)
                src = pl.ds(pl.multiple_of(stored_block(p) * TILE, TILE), TILE)
                do = mixed_grad[src, :]
                qs = q_ref[at, :]
                probs = jnp.exp(scores_of(qs, k_ref[keys, :], i) - l_ref[at, :])
                dp = mm_nt(do, v_ref[keys, :])
                inner = jnp.sum(probs * dp, axis=-1, keepdims=True)
                ds = (probs * (dp - inner)).astype(LOW)
                dq = mm(ds, k_ref[keys, :]) * HD ** (-0.5)
                dk[keys, :] += mm_tn(ds, qs)
                dv[keys, :] += mm_tn(probs.astype(LOW), do)
                dq, part = pull_head(raw_ref[at, :HD], hg[0:1], dq, cos[at, :], sin[at, :])
                head_q += part
                out[at, :HD] = dq.astype(LOW)
        head_k = jnp.zeros((1, HD), F32)
        for p in range(seq // TILE):
            at = slice(p * TILE, (p + 1) * TILE)
            dkp, part = pull_head(
                raw_ref[at, HD:], hg[1:2], dk[at, :] * HD ** (-0.5), cos[at, :], sin[at, :]
            )
            head_k += part
            out[at, HD : 2 * HD] = dkp.astype(LOW)
            out[at, 2 * HD :] = dv[at, :].astype(LOW)
        head_out[0:1, :] = head_q
        head_out[1:2, :] = head_k

    pair = pl.BlockSpec((1, chip, HD), lambda *_: (0, 0, 0), pipeline_mode=pl.Buffered(1))
    return call(
        body,
        [like((seq, 3 * HD), LOW), like((2, HD), F32)],
        [held((seq, HD))] * 3
        + [held((seq, 2 * HD)), held((seq, 1))]
        + [pair, pair, held((chip, HD))] * 2
        + [held((2, HD))]
        + [held((seq, HD // 2))] * 2,
        [held((seq, 3 * HD)), held((2, HD))],
        (q, k, v, raw, lse, *grads, head_rows, cos_t, sin_t),
        flops=10 * 24 * TILE * TILE * HD,
        scratch=[pltpu.VMEM((seq, HD), F32)] * 2 + [pltpu.VMEM((seq, HD), LOW)],
        prefetch=(base,),
    )


def project(mixed, outs, x, gains, stored_map):
    seq = x.shape[0]

    def body(_, m0, m1, m2, m3, w0, w1, w2, w3, x_ref, g, proj, pre):
        for i in range(2):
            at = slice(i * TILE, (i + 1) * TILE)
            y = mm(m0[at, :], w0[...]) + mm(m1[at, :], w1[...])
            y = y + mm(m2[at, :], w2[...]) + mm(m3[at, :], w3[...])
            proj[at, :] = y
            r = x_ref[at, :].astype(F32) + y * scale_of(y) * g[1:2]
            pre[at, :] = (r * scale_of(r) * g[2:3]).astype(LOW)

    def block(cols):
        return pl.BlockSpec((2 * TILE, cols), lambda r, m: (r, 0))

    return call(
        body,
        [like((seq, D), F32), like((seq, D), LOW)],
        [pl.BlockSpec((2 * TILE, HD), lambda r, m: (m[2 * r] // 2, 0))] * 4
        + [held((HD, D))] * 4
        + [block(D), held((4, D))],
        [block(D), block(D)],
        (*mixed, *outs, x, gains),
        grid=(seq // TILE // 2,),
        flops=2 * seq * D * H * HD,
        prefetch=(stored_map,),
    )


def gate_stage(pre, w, places, half, into=()):
    seq, part = pre.shape[0], w.cols // 2
    rows = 512
    first = half * (seq // 2 // rows)
    count = len(w.parts)

    def pieces(g, u):
        t = jnp.tanh(GELU_A * (g + GELU_B * (g * g * g)))
        a = 0.5 * g * (1.0 + t)
        slope = 0.5 * (1.0 + t) + (0.5 * g) * (1.0 - t * t) * (GELU_A * (1.0 + 3.0 * GELU_B * (g * g)))
        return a * u, u * slope, a

    def body(pl_ref, p_ref, *refs):
        hidden, ab, room, sems = refs[count:]
        w.load(pl_ref, refs[:count], room, sems)
        @pl.loop(0, part // 256)
        def _(i):
            at = pl.multiple_of(i * 256, 256)
            gate, up = pl.ds(at, 256), pl.ds(pl.multiple_of(part + at, 256), 256)
            h, b, a = pieces(mm(p_ref[...], room[:, gate]), mm(p_ref[...], room[:, up]))
            hidden[:, gate] = h.astype(LOW)
            ab[:, gate] = b.astype(LOW)
            ab[:, up] = a.astype(LOW)

    def block(cols):
        return pl.BlockSpec((rows, cols), lambda r, m: (first + r, 0))

    return call(
        body,
        [like((seq, part), LOW), like((seq, 2 * part), LOW)],
        [block(D)] + w.specs(),
        [block(part), block(2 * part)],
        (pre, *w.parts),
        grid=(seq // 2 // rows,),
        flops=2 * seq * D * part,
        scratch=w.scratch(),
        into=into,
        prefetch=(places,),
    )


def down_stage(hidden, w, places, half):
    seq, part = hidden.shape
    rows = seq // 4
    count = len(w.parts)

    def body(pl_ref, h, *refs):
        even, odd, room, sems = refs[count:]
        w.load(pl_ref, refs[:count], room, sems)
        odd[...] = mm(h[rows:, :], room[...]).astype(LOW)
        even[...] = mm(h[:rows, :], room[...]).astype(LOW)

    return call(
        body,
        [like((rows, D), LOW)] * 2,
        [
            pl.BlockSpec(
                (2 * rows, part), lambda r, m: (half, 0), pipeline_mode=pl.Buffered(1)
            )
        ]
        + w.specs(),
        [held((rows, D))] * 2,
        (hidden, *w.parts),
        flops=4 * rows * D * part,
        scratch=w.scratch(),
        prefetch=(places,),
    )


def ffn_stage(parts, near, far, proj, x, cot, gains):
    rows = cot.shape[0]

    def body(p, n, f, proj_ref, x_ref, c_ref, g, out, grad, gain):
        y = p[...].astype(F32) + n[...].astype(F32) + f[...].astype(F32)
        pr = proj_ref[...]
        s = scale_of(y)
        r = x_ref[...].astype(F32) + pr * scale_of(pr) * g[1:2]
        out[...] = (r + y * s * g[3:4]).astype(LOW)
        dy = c_ref[...].astype(F32)
        grad[...] = norm_pull(y, s, g[3:4], dy).astype(LOW)
        part = jnp.sum(dy * y * s, axis=0, keepdims=True)

        @pl.when(pl.program_id(0) == 0)
        def _():
            gain[...] = part

        @pl.when(pl.program_id(0) > 0)
        def _():
            gain[...] += part

    block = pl.BlockSpec((TILE, D), lambda r: (r, 0))
    return call(
        body,
        [like((rows, D), LOW), like((rows, D), LOW), like((1, D), F32)],
        [block] * 6 + [held((4, D))],
        [block, block, held((1, D))],
        (parts, near, far, proj, x, cot, gains),
        grid=(rows // TILE,),
    )


def hidden_back(grad, w, ab, places, half, into=()):
    seq, part = ab.shape[0], ab.shape[1] // 2
    rows = 512
    first = half * (seq // 2 // rows)
    count = len(w.parts)

    def body(pl_ref, g_ref, ab_ref, *refs):
        out, room, sems = refs[count:]
        w.load(pl_ref, refs[:count], room, sems)
        @pl.loop(0, part // 256)
        def _(i):
            at = pl.multiple_of(i * 256, 256)
            hg = mm_nt(g_ref[...], room[pl.ds(at, 256), :])
            for side in (pl.ds(at, 256), pl.ds(pl.multiple_of(part + at, 256), 256)):
                out[:, side] = (hg * ab_ref[:, side].astype(F32)).astype(LOW)

    def block(cols):
        return pl.BlockSpec((rows, cols), lambda r, m: (first + r, 0))

    return call(
        body,
        [like((seq, 2 * part), LOW)],
        [pl.BlockSpec((rows, D), lambda r, m: (r, 0)), block(2 * part)] + w.specs(),
        [block(2 * part)],
        (grad, ab, *w.parts),
        grid=(seq // 2 // rows,),
        flops=seq * D * part,
        scratch=w.scratch(),
        into=into,
        prefetch=(places,),
    )[0]


def residual_back(gu, w, outs, proj, x, cot, gains, stored_map, places, half, into=()):
    seq, wide = gu.shape
    own = cot.shape[0] // TILE
    steps = seq // 2 // TILE
    first = half * steps
    count = len(w.parts)

    def body(_, pl_ref, gu_ref, w0, w1, w2, w3, proj_ref, x_ref, c_ref, g, *refs):
        rg, pg, even, odd, gain, room, sems, *made = refs[count:]
        w.load(pl_ref, refs[:count], room, sems)
        step = pl.program_id(0)

        def multiply(turn):
            made[turn][...] = mm_nt(gu_ref[...], room[...])

        def finish(turn):
            dy = made[turn][...]
            pr = proj_ref[...]
            sp = scale_of(pr)
            r = x_ref[...].astype(F32) + pr * sp * g[1:2]
            s = scale_of(r)
            dr = norm_pull(r, s, g[2:3], dy)
            if half == 0:
                dr = dr + jnp.where(step <= own, 1.0, 0.0) * c_ref[...].astype(F32)
            rg[...] = dr.astype(LOW)
            low = norm_pull(pr, sp, g[1:2], dr).astype(LOW)
            pg[...] = low
            even[0] = mm_nt(low, w0[...]).astype(LOW)
            odd[0] = mm_nt(low, w1[...]).astype(LOW)
            even[1] = mm_nt(low, w2[...]).astype(LOW)
            odd[1] = mm_nt(low, w3[...]).astype(LOW)
            before = jnp.where(step == 1, 0.0, gain[...])
            gain[0:1, :] = before[0:1] + jnp.sum(dr * pr * sp, axis=0, keepdims=True)
            gain[1:2, :] = before[1:2] + jnp.sum(dy * r * s, axis=0, keepdims=True)

        @pl.when(step == 0)
        def _():
            multiply(0)

        for turn in range(2):

            @pl.when((step > 0) & (step < steps) & (step % 2 == turn))
            def _():
                multiply(turn)
                finish(1 - turn)

        @pl.when(step == steps)
        def _():
            finish((steps - 1) % 2)

    def last(i):
        return jnp.maximum(i - 1, 0)

    def block(cols):
        return pl.BlockSpec((TILE, cols), lambda i, m, p: (first + last(i), 0))

    heads = pl.BlockSpec((2, TILE, HD), lambda i, m, p: (0, m[first + last(i)] % steps, 0))
    return call(
        body,
        [like((seq, D), LOW), like((seq, D), LOW)]
        + [like((2, seq // 2, HD), LOW)] * 2
        + [like((2, D), F32)],
        [pl.BlockSpec((TILE, wide), lambda i, m, p: (first + jnp.minimum(i, steps - 1), 0))]
        + [held((HD, D))] * 4
        + [block(D), block(D)]
        + [pl.BlockSpec((TILE, D), lambda i, m, p: (jnp.minimum(last(i), own - 1), 0)), held((4, D))]
        + w.specs(),
        [
            block(D),
            pl.BlockSpec((TILE, D), lambda i, m, p: (m[first + last(i)], 0)),
            heads,
            heads,
            held((2, D)),
        ],
        (gu, *outs, proj, x, cot, gains, *w.parts),
        grid=(steps + 1,),
        flops=seq * D * (wide + H * HD),
        scratch=w.scratch() + [pltpu.VMEM((TILE, D), F32)] * 2,
        into=into,
        prefetch=(stored_map, places),
    )


def input_back(qkv, w_in, x, rg, gain, pos_map, places):
    seq = x.shape[0]
    rows = 2 * TILE
    count = len(w_in.parts)

    def body(_, pl_ref, q0, q1, x_ref, rg_ref, g, *refs):
        even, odd, gain_out, w, sems = refs[count:]
        w_in.load(pl_ref, refs[:count], w, sems)
        step = pl.program_id(0)
        total = jnp.zeros((1, D), F32)
        made = []
        for i, q_ref in enumerate((q0, q1)):
            at = slice(i * TILE, (i + 1) * TILE)
            dy = mm_nt(q_ref[...], w[...])
            xf = x_ref[at, :].astype(F32)
            s = scale_of(xf)
            made.append((rg_ref[at, :].astype(F32) + norm_pull(xf, s, g[...], dy)).astype(LOW))
            total += jnp.sum(dy * xf * s, axis=0, keepdims=True)
        gain_out[...] = jnp.where(step == 0, 0.0, gain_out[...]) + total

        @pl.when(step % 2 == 0)
        def _():
            even[:TILE, :], even[TILE:, :] = made

        @pl.when(step % 2 == 1)
        def _():
            odd[:TILE, :], odd[TILE:, :] = made

    block = pl.BlockSpec((rows, D), lambda i, m, s: (i, 0))
    out = pl.BlockSpec((rows, D), lambda i, m, s: (i // 2, 0))
    return call(
        body,
        [like((seq // 2, D), LOW)] * 2 + [like((1, D), F32)],
        [
            pl.BlockSpec((TILE, 3 * HD), lambda i, m, s: (m[2 * i], 0)),
            pl.BlockSpec((TILE, 3 * HD), lambda i, m, s: (m[2 * i + 1], 0)),
            block,
            block,
            held((1, D)),
        ]
        + w_in.specs(),
        [out, out, held((1, D))],
        (qkv, qkv, x, rg, gain, *w_in.parts),
        grid=(seq // rows,),
        flops=2 * seq * D * 3 * HD,
        scratch=w_in.scratch(),
        prefetch=(pos_map, places),
    )


def local(
    tokens,
    cotangent,
    lengths,
    w_qkv,
    w_out,
    w_gate_up,
    w_down,
    gains,
    head_gains,
    first_qkv,
    first_out,
    first_gate_up,
    first_down,
    first_gains,
    first_head,
    second_qkv,
    second_out,
    second_gate_up,
    second_down,
    second_gains,
    second_head,
):
    low = jnp.bfloat16
    f32 = jnp.float32
    rows = tokens.shape[1]
    dp = lax.axis_size("dp")
    ctx = lax.axis_size("ctx")
    place = lax.axis_index("ctx")
    seq = rows * ctx
    in_rows = w_qkv.shape[0]
    out_rows = w_out.shape[0]
    ff_rows = w_down.shape[0]
    gain_cols = gains.shape[1]
    head_cols = head_gains.shape[1]
    qkv_cols = 3 * HD
    ring = Ring()

    q_cols = w_qkv[:, : H * HD].astype(low).reshape(in_rows, ctx, HD).transpose(1, 0, 2)
    kv_cols = jnp.broadcast_to(w_qkv[:, H * HD :].astype(low)[None], (ctx, in_rows, 2 * HD))
    extra = jnp.concatenate(
        [gains.astype(low).reshape(-1), head_gains.astype(low).reshape(-1)]
    )
    extra = jnp.pad(extra, (0, 4 * qkv_cols - extra.shape[0])).reshape(4, qkv_cols)
    small_sent = jnp.concatenate(
        [
            jnp.concatenate([q_cols, kv_cols], axis=2),
            jnp.broadcast_to(extra[None], (ctx, 4, qkv_cols)),
        ],
        axis=1,
    )
    to_user = [((dp * c + d), d * ctx + c) for d in range(dp) for c in range(ctx)]
    to_owner = [(b, a) for a, b in to_user]
    out_mine = lax.ppermute(w_out.astype(low), ("dp", "ctx"), to_user)
    half = out_rows // 2
    small = exchange(small_sent, "ctx")
    packed = pack_columns(tie(w_gate_up, small_sent), dp, ctx)
    own_rows = ctx * in_rows
    small_ring = Gather(
        ring,
        jnp.concatenate(
            [
                small[:, :in_rows].reshape(own_rows, qkv_cols),
                small[:, in_rows:].reshape(4 * ctx, qkv_cols),
                out_mine[:, :qkv_cols],
                jnp.concatenate([out_mine[:half, qkv_cols:], out_mine[half:, qkv_cols:]], axis=1),
            ]
        ),
    )
    down_block = jnp.pad(w_down.astype(low), ((0, hidden_room(ff_rows, dp) - ff_rows), (0, 0)))
    down_ring = Gather(ring, down_block)
    down_first = down_ring.advance()
    tokens_far = swap(tie(tokens[0], small), 2)
    tokens_near = swap(tie(tokens[0], small), 1)
    gate_up_cols = exchange(packed, "ctx").reshape(own_rows, -1)
    first_len = lengths[0, 0]
    pos = tie(jnp.arange(seq, dtype=jnp.int32), packed)
    cos_t, sin_t = rope_tables(pos - jnp.where(pos < first_len, 0, first_len), HD)
    small_ring.advance(*down_first)
    small_ring.advance(cos_t, sin_t)
    small_ring.advance(gate_up_cols, tokens_near)
    tokens_last = swap(tie(tokens_far, *small_ring.held.values()), 1)
    tokens_all = jnp.concatenate([tokens[0], tokens_near, tokens_far, tokens_last])
    while small_ring.hop < ring.hops[0]:
        small_ring.advance()
    small_seen = list(small_ring.held.values())
    gate_ring = Gather(ring, gate_up_cols)
    gate_seen = gate_ring.advance(*small_seen, tokens_last)
    w_in = Blocks(small_ring, own_rows)
    places = ring.places
    gain_rows, head_rows, out_mine = unpack_small(
        small_ring, own_rows, dp, ctx, out_rows, gain_cols, head_cols
    )
    out_far, out_near = swap(out_mine, 2), swap(out_mine, 1)

    blocks = seq // TILE
    split = first_len // TILE
    base = jnp.where(split == LONG, jnp.array([0, LONG, 0]), jnp.array([SHORT, 0, 0]))
    base = (base + jnp.array([0, 0, 1]) * (place // 2)).astype(jnp.int32)
    tiles = jnp.arange(blocks, dtype=jnp.int32)
    stored_map = 2 * (place ^ (tiles // 2)) + tiles % 2
    owner = jnp.where(tiles < ctx, tiles, 2 * ctx - 1 - tiles)
    row_map = 2 * (place ^ owner) + (tiles >= ctx)
    pos_map = jnp.where(tiles % 2 == 0, stored_map // 2, 2 * ctx - 1 - stored_map // 2)

    q, k, v, raw, normed = input_stage(
        tokens_all, w_in, gain_rows[0:1], head_rows, cos_t, sin_t, row_map, places
    )
    gate_ring.advance(q)
    mixed, lse = attention(tie(q, *gate_seen, out_far, out_near), k, v, base)
    mixed_far, mixed_near = swap(mixed, 2), swap(mixed, 1)
    out_parts = [out_mine, out_near, out_far, swap(tie(out_far, mixed), 1)]
    down_ring.advance(mixed)
    gate_ring.advance(mixed)
    mixed_parts = [mixed, mixed_near, mixed_far, swap(mixed_far, 1)]
    proj, pre_low = project(mixed_parts, out_parts, tokens_all, gain_rows, stored_map)
    while gate_ring.hop < ring.hops[0]:
        gate_ring.advance(pre_low)
        if down_ring.hop < ring.hops[0]:
            down_ring.advance(pre_low)
    down_ring.finish()
    full_gate_up = Blocks(gate_ring)
    full_down = Blocks(down_ring)
    buffers = gate_stage(pre_low, full_gate_up, places, 1)
    even, odd = down_stage(buffers[0], full_down, places, 1)
    summed = add_low(even, swap(odd, 1))
    far = swap(summed, 2)
    hidden_low, slopes = gate_stage(tie(pre_low, summed), full_gate_up, places, 0, buffers)
    even, odd = down_stage(tie(hidden_low, far), full_down, places, 0)
    near = swap(odd, 1)
    result, ffn_grad, gain_grad_d = ffn_stage(
        even, near, far, proj, tokens[0], cotangent[0], gain_rows
    )

    far = swap(ffn_grad, 2)
    ffn_here = jnp.concatenate([ffn_grad, swap(ffn_grad, 1)])
    residual = partial(
        residual_back,
        w=full_gate_up,
        outs=out_parts,
        proj=proj,
        x=tokens_all,
        cot=cotangent[0],
        gains=gain_rows,
        stored_map=stored_map,
        places=places,
    )
    gate_up_low = hidden_back(ffn_here, full_down, slopes, places, 0)
    resid_grad, proj_low, even, odd, gain_grad_here = residual(gate_up_low, half=0)
    far = tie(far, resid_grad)
    ffn_there = jnp.concatenate([far, swap(far, 1)])
    near = swap(odd, 1)
    parts_here = (even, near)
    far_there = swap(tie(add_low(even[1], near[1]), ffn_there), 2)
    ffn_low = jnp.concatenate([ffn_here, ffn_there])
    grad_down = mm_tn(hidden_low, ffn_low).astype(low)
    down_sum = Reduce(ring, grad_down).send()
    gate_up_low = hidden_back(
        tie(ffn_there, *down_sum.tokens()), full_down, slopes, places, 1, (gate_up_low,)
    )
    held_down = down_sum.absorb(gate_up_low)
    grad_gate_up = mm_tn(tie(pre_low, *held_down), gate_up_low).astype(low)
    gate_sum = Reduce(ring, grad_gate_up)
    held_down = down_sum.send().absorb(grad_gate_up)
    resid_grad, proj_low, even, odd, gain_grad_there = residual(
        tie(gate_up_low, *held_down, *gate_sum.tokens()), half=1, into=(resid_grad, proj_low)
    )
    held_gate = gate_sum.send().absorb(odd)
    held_down = down_sum.send().absorb(odd)
    near = swap(tie(odd, *held_gate, *held_down), 1)
    summed = add_low(even[1], near[1])
    far_here = swap(summed, 2)
    gate_sum.send(summed)
    down_sum.send(summed)
    proj_low = tie(proj_low, summed)
    grad_out = [mm_tn(m, proj_low).astype(low) for m in mixed_parts]
    far_here = tie(far_here, *grad_out)
    grad_out = reduce_ctx(grad_out).astype(low)
    qkv_low, head_grads = attention_back(
        q,
        k,
        v,
        raw,
        lse,
        parts_here + (far_here,) + (even, near, far_there),
        head_rows,
        cos_t,
        sin_t,
        base,
    )
    held_gate = gate_sum.absorb(qkv_low)
    down_sum.absorb(qkv_low)
    down_own = down_sum.finish()
    gate_sum.send()
    grad_in = mm_tn(tie(normed, down_own, *held_gate), qkv_low).astype(low)
    down_own = down_own[:ff_rows]
    grad_out = grad_out.reshape(dp, out_rows, D)
    in_blocks = jnp.concatenate(
        [
            grad_in.reshape(dp, own_rows, qkv_cols),
            grad_out[:, :, :qkv_cols],
            jnp.concatenate(
                [grad_out[:, :half, qkv_cols:], grad_out[:, half:, qkv_cols:]], axis=2
            ),
        ],
        axis=1,
    )
    in_sum = Reduce(ring, in_blocks.reshape(-1, qkv_cols)).send()
    input_even, input_odd, gain_grad_a = input_back(
        tie(qkv_low, *in_sum.tokens(), *held_gate),
        w_in,
        tokens_all,
        resid_grad,
        gain_rows[0:1],
        pos_map,
        places,
    )
    in_sum.absorb(input_odd)
    held_gate = gate_sum.absorb(input_odd)
    in_sum.send(*held_gate)
    gate_up_own = gate_sum.finish().astype(low)
    gate_up_own = exchange(gate_up_own.reshape(ctx, in_rows, -1), "ctx")
    near = swap(input_odd, 1)
    gain_grad_bc = gain_grad_here + gain_grad_there
    in_sum.absorb()

    in_own = in_sum.finish().astype(low)
    gate_up_own = unpack_columns(gate_up_own, dp, ctx, ff_rows)
    out_own = in_own[own_rows:]
    out_own = jnp.concatenate(
        [
            out_own[:out_rows],
            jnp.concatenate(
                [out_own[out_rows:, : D - qkv_cols], out_own[out_rows:, D - qkv_cols :]], axis=0
            ),
        ],
        axis=1,
    )
    out_own = lax.ppermute(out_own, ("dp", "ctx"), to_owner).astype(f32)
    in_own = exchange(in_own[:own_rows].reshape(ctx, in_rows, qkv_cols), "ctx").astype(f32)
    summed = tie(add_low(input_even[rows:], near[rows:]), gate_up_own, in_own)
    far = swap(summed, 2)
    input_grad = (
        input_even[:rows].astype(f32) + near[:rows].astype(f32) + far.astype(f32)
    )
    qkv_own = jnp.concatenate(
        [
            in_own[:, :, :HD].transpose(1, 0, 2).reshape(in_rows, H * HD),
            jnp.sum(in_own[:, :, HD:], axis=0),
        ],
        axis=1,
    )
    gain_grads = jnp.concatenate([gain_grad_a, gain_grad_bc, gain_grad_d], axis=0)
    local_squares = jnp.float32(0.0)
    for piece in (qkv_own, out_own, gate_up_own, down_own):
        local_squares = local_squares + jnp.sum(piece * piece)
    lines = jnp.concatenate([gain_grads.reshape(-1, 128), head_grads.reshape(-1, 128)])
    squares = jnp.pad(local_squares.reshape(1, 1), ((0, 7), (0, 127)))
    sums = sum_all(tie(jnp.concatenate([lines, squares]), summed))
    small_grads = sums[: lines.shape[0]]
    index = lax.axis_index("dp") * ctx + place
    gains_own = lax.dynamic_slice_in_dim(
        small_grads[: 4 * D // 128].reshape(4, D), index * gain_cols, gain_cols, axis=1
    )
    head_own = lax.dynamic_slice_in_dim(
        small_grads[4 * D // 128 :].reshape(2, HD), index * head_cols, head_cols, axis=1
    )
    reduced = (qkv_own, out_own, gate_up_own, down_own, gains_own, head_own)
    total_squares = sums[lines.shape[0], 0] + jnp.sum(small_grads * small_grads)
    total_squares = tie(total_squares, far)
    grad_norm = jnp.sqrt(total_squares)
    factor = 1.0 / jnp.maximum(grad_norm, 1.0)
    weights = (w_qkv, w_out, w_gate_up, w_down, gains, head_gains)
    firsts = (first_qkv, first_out, first_gate_up, first_down, first_gains, first_head)
    seconds = (second_qkv, second_out, second_gate_up, second_down, second_gains, second_head)
    rates = (D ** (-0.5), (H * HD) ** (-0.5), D ** (-0.5), FF ** (-0.5), GAIN_RATE, GAIN_RATE)
    decays = (WEIGHT_DECAY, WEIGHT_DECAY, WEIGHT_DECAY, WEIGHT_DECAY, 0.0, 0.0)
    updates = [
        adam_update(
            weights[index],
            firsts[index],
            seconds[index],
            reduced[index] * factor,
            rates[index],
            decays[index],
        )
        for index in range(6)
    ]
    return (
        result[None],
        input_grad[None],
        updates[0][0],
        updates[1][0],
        updates[2][0],
        updates[3][0],
        updates[4][0],
        updates[5][0],
        updates[0][1],
        updates[1][1],
        updates[2][1],
        updates[3][1],
        updates[4][1],
        updates[5][1],
        updates[0][2],
        updates[1][2],
        updates[2][2],
        updates[3][2],
        updates[4][2],
        updates[5][2],
        grad_norm,
    )


def solution(mesh):
    in_specs = (
        P("dp", "ctx", None),
        P("dp", "ctx", None),
        P("dp", None),
        P(("dp", "ctx"), None),
        P(("dp", "ctx"), None),
        P(("dp", "ctx"), None),
        P(("dp", "ctx"), None),
        P(None, ("dp", "ctx")),
        P(None, ("dp", "ctx")),
        P(("dp", "ctx"), None),
        P(("dp", "ctx"), None),
        P(("dp", "ctx"), None),
        P(("dp", "ctx"), None),
        P(None, ("dp", "ctx")),
        P(None, ("dp", "ctx")),
        P(("dp", "ctx"), None),
        P(("dp", "ctx"), None),
        P(("dp", "ctx"), None),
        P(("dp", "ctx"), None),
        P(None, ("dp", "ctx")),
        P(None, ("dp", "ctx")),
    )
    out_specs = (
        P("dp", "ctx", None),
        P("dp", "ctx", None),
        P(("dp", "ctx"), None),
        P(("dp", "ctx"), None),
        P(("dp", "ctx"), None),
        P(("dp", "ctx"), None),
        P(None, ("dp", "ctx")),
        P(None, ("dp", "ctx")),
        P(("dp", "ctx"), None),
        P(("dp", "ctx"), None),
        P(("dp", "ctx"), None),
        P(("dp", "ctx"), None),
        P(None, ("dp", "ctx")),
        P(None, ("dp", "ctx")),
        P(("dp", "ctx"), None),
        P(("dp", "ctx"), None),
        P(("dp", "ctx"), None),
        P(("dp", "ctx"), None),
        P(None, ("dp", "ctx")),
        P(None, ("dp", "ctx")),
        P(),
    )
    return jax.shard_map(local, mesh=mesh, in_specs=in_specs, out_specs=out_specs, check_vma=False)
```

```python
from functools import partial

import jax
import jax.numpy as jnp
from jax import lax
from jax.experimental import pallas as pl
from jax.experimental.pallas import tpu as pltpu
from jax.sharding import PartitionSpec as P

D = 1152
H = 4
HD = 256
FF = 6912
STEP = 10

EPSILON = 1e-06
ROPE_BASE = 1000000.0
BETA_ONE = 0.9
BETA_TWO = 0.95
ADAM_EPSILON = 1e-08
WEIGHT_DECAY = 0.1
GAIN_RATE = 1.0


def rope_tables(offsets, width):
    half = width // 2
    freq = jnp.exp(-jnp.log(ROPE_BASE) * jnp.arange(half, dtype=jnp.float32) * (2.0 / width))
    angle = offsets.astype(jnp.float32)[:, None] * freq[None, :]
    return (jnp.cos(angle), jnp.sin(angle))


def adam_update(weight, first, second, grad, rate, decay):
    first_new = BETA_ONE * first + (1.0 - BETA_ONE) * grad
    second_new = BETA_TWO * second + (1.0 - BETA_TWO) * grad * grad
    first_hat = first_new / (1.0 - BETA_ONE**STEP)
    second_hat = second_new / (1.0 - BETA_TWO**STEP)
    updated = weight - rate * (first_hat / (jnp.sqrt(second_hat) + ADAM_EPSILON) + decay * weight)
    return (updated, first_new, second_new)


def exchange(parts, axis):
    return lax.all_to_all(parts, axis, split_axis=0, concat_axis=0, tiled=True)


def swap(value, bit):
    count = lax.axis_size("ctx")
    return lax.ppermute(value, "ctx", [(i, i ^ bit) for i in range(count)])


def swap_dp(value, bit):
    count = lax.axis_size("dp")
    return lax.ppermute(value, "dp", [(i, i ^ bit) for i in range(count)])


def gather_ctx(block):
    far = swap(block, 2)
    return [block, swap(block, 1), far, swap(far, 1)]


def add_low(a, b):
    return a + b


def reduce_ctx(blocks):
    near, far = jnp.concatenate([blocks[1], blocks[3]]), None
    near = swap(near, 1)
    size = blocks[0].shape[0]
    far = swap(add_low(blocks[2], near[size:]), 2)
    mine = blocks[0].astype(jnp.float32) + near[:size].astype(jnp.float32)
    return mine + far.astype(jnp.float32)


def reorder(value, bit, rows):
    parts = [value[j * rows : (j + 1) * rows] for j in range(value.shape[0] // rows)]
    return jnp.concatenate([parts[j ^ bit] for j in range(len(parts))])


def sum_rest(value):
    value = value + swap(value, 1)
    bit = 1
    while bit < lax.axis_size("dp"):
        value = value + swap_dp(value, bit)
        bit *= 2
    return value


def tie(value, *tokens):
    return lax.optimization_barrier((value, *tokens))[0]


class Ring:
    def __init__(self):
        count = self.count = lax.axis_size("dp")
        self.ctx = lax.axis_size("ctx")
        self.order = list(range(0, count, 2)) + list(range(count - 1, 0, -2))
        self.hops = (count // 2, count - 1 - count // 2)
        table = [
            [self.order[(self.order.index(i) + sense * step) % count] for step in range(count)]
            for sense in (1, -1)
            for i in range(count)
        ]
        row = (lax.axis_index("ctx") % 2) * count + lax.axis_index("dp")
        self.places = lax.dynamic_slice(
            jnp.array(table, jnp.int32), (row, 0), (1, count), allow_negative_indices=False
        )[0]

    def send(self, value, way):
        pairs = []
        for place, source in enumerate(self.order):
            for c in range(self.ctx):
                target = self.order[(place + (way if c % 2 == 0 else -way)) % self.count]
                pairs.append((source * self.ctx + c, target * self.ctx + c))
        return lax.ppermute(value, ("dp", "ctx"), pairs)

    def ways(self, hop):
        return [way for way, last in zip((1, -1), self.hops) if hop <= last]


class Gather:
    def __init__(self, ring, block):
        self.ring, self.hop = ring, 0
        self.held = {1: block, -1: block}
        self.parts, self.steps = [block], [0]

    def advance(self, *tokens):
        self.hop += 1
        for way in self.ring.ways(self.hop):
            self.held[way] = self.ring.send(tie(self.held[way], *tokens), way)
            self.parts.append(self.held[way])
            self.steps.append(-way * self.hop % self.ring.count)
        return list(self.held.values())

    def finish(self):
        while self.hop < self.ring.hops[0]:
            self.advance()
        return self

    def whole(self):
        block = self.parts[0]
        rows = block.shape[0]
        found = jnp.zeros((rows * self.ring.count, block.shape[1]), block.dtype)
        starts = self.ring.places * rows
        for step, part in zip(self.steps, self.parts):
            found = lax.dynamic_update_slice(
                found, part, (starts[step], 0), allow_negative_indices=False
            )
        return found


class Reduce:
    def __init__(self, ring, whole):
        self.ring, self.source, self.hop = ring, whole, ring.hops[0]
        self.rows = whole.shape[0] // ring.count
        self.starts = ring.places * self.rows
        self.held = {way: self.piece(way * last) for way, last in zip((1, -1), ring.hops)}
        self.total = None

    def piece(self, step):
        return lax.dynamic_slice(
            self.source,
            (self.starts[step % self.ring.count], 0),
            (self.rows, self.source.shape[1]),
            allow_negative_indices=False,
        )

    def tokens(self):
        return list(self.held.values())

    def send(self, *tokens):
        self.came = {
            way: self.ring.send(tie(self.held[way], *tokens), way) for way in self.ring.ways(self.hop)
        }
        return self

    def absorb(self, *tokens):
        for way, came in self.came.items():
            came = tie(came, *tokens) if tokens else came
            if self.hop > 1:
                self.held[way] = add_low(came, self.piece(way * (self.hop - 1)))
            else:
                mine = self.piece(0) if self.total is None else self.total
                self.total = mine.astype(jnp.float32) + came.astype(jnp.float32)
        self.hop -= 1
        return self.tokens() if self.total is None else [self.total]

    def finish(self):
        while self.hop > 0:
            self.send().absorb()
        return self.total


LOW = jnp.bfloat16
F32 = jnp.float32
TILE = 256
LONG = 6
SHORT = 2
GELU_A = 0.7978845608028654
GELU_B = 0.044715
VMEM = 56 * 2**20


def mm(a, b):
    return jnp.dot(a, b, preferred_element_type=F32)


def mm_nt(a, b):
    return lax.dot_general(a, b, (((1,), (1,)), ((), ())), preferred_element_type=F32)


def mm_tn(a, b):
    return lax.dot_general(a, b, (((0,), (0,)), ((), ())), preferred_element_type=F32)


def call(body, out_shape, in_specs, out_specs, args, grid=(1,), flops=0, scratch=(), into=(), prefetch=()):
    given = len(prefetch)
    used = len(in_specs)

    def kernel(*refs):
        body(*refs[: given + used], *refs[given + used + len(into) :])

    nbytes = sum(a.size * a.dtype.itemsize for a in args)
    nbytes += sum(o.size * o.dtype.itemsize for o in jax.tree.leaves(out_shape))
    return pl.pallas_call(
        kernel,
        out_shape=out_shape,
        grid_spec=pltpu.PrefetchScalarGridSpec(
            num_scalar_prefetch=given,
            grid=grid,
            in_specs=list(in_specs) + [pl.BlockSpec(memory_space=pl.ANY)] * len(into),
            out_specs=out_specs,
            scratch_shapes=list(scratch),
        ),
        compiler_params=pltpu.CompilerParams(vmem_limit_bytes=VMEM),
        cost_estimate=pl.CostEstimate(flops=flops // 16, bytes_accessed=nbytes // 16, transcendentals=0),
        input_output_aliases={given + used + i: i for i in range(len(into))},
    )(*prefetch, *args, *into)


def held(shape):
    return pl.BlockSpec(shape, lambda *_: (0,) * len(shape), pipeline_mode=pl.Buffered(1))


def like(shape, dtype):
    return jax.ShapeDtypeStruct(shape, dtype)


def scale_of(v):
    return lax.rsqrt(jnp.mean(v * v, axis=-1, keepdims=True) + EPSILON)


def norm_pull(v, s, g, dy):
    w = dy * g
    return s * w - v * (s * s * s) * jnp.mean(w * v, axis=-1, keepdims=True)


def turn(v, cos_t, sin_t, sign):
    half = v.shape[-1] // 2
    a, b = v[:, :half], v[:, half:]
    return jnp.concatenate([a * cos_t - sign * (b * sin_t), b * cos_t + sign * (a * sin_t)], axis=-1)


def stored_block(p):
    return jnp.where(p < 4, 2 * p, 2 * (7 - p) + 1)


def padded(rows):
    return -(-rows // 16) * 16


def pack_columns(w_gate_up, dp, ctx):
    rows, wide = w_gate_up.shape
    ff = wide // 2
    step = ff // (dp * ctx)
    room = padded(step)
    part = dp * room

    def body(w, out):
        zeros = [jnp.zeros((rows, room - step), F32)] if room > step else []
        for c in range(ctx):
            for side in range(2):
                cut = []
                for d in range(dp):
                    at = side * ff + (d * ctx + c) * step
                    cut += [w[:, at : at + step]] + zeros
                out[c, :, side * part : (side + 1) * part] = jnp.concatenate(cut, axis=1).astype(LOW)

    return call(
        body,
        like((ctx, rows, 2 * part), LOW),
        [held((rows, wide))],
        held((ctx, rows, 2 * part)),
        (w_gate_up,),
    )


def unpack_columns(parts, dp, ctx, step):
    rows, wide = parts.shape[1], parts.shape[2]
    part = wide // 2
    room = part // dp
    ff = dp * ctx * step

    def body(p, out):
        for c in range(ctx):
            own = p[c].astype(F32)
            for side in range(2):
                for d in range(dp):
                    at = side * ff + (d * ctx + c) * step
                    start = side * part + d * room
                    out[:, at : at + step] = own[:, start : start + step]

    return call(
        body,
        like((rows, 2 * ff), F32),
        [held(parts.shape)],
        held((rows, 2 * ff)),
        (parts,),
    )


class Blocks:
    def __init__(self, gathered, rows=None):
        block, self.cols = gathered.parts[0].shape
        self.rows = rows = rows or block
        count = gathered.ring.count
        self.height = rows * count
        if rows % 16:
            whole = gathered.whole().reshape(count, block, self.cols)[:, :rows]
            self.parts, self.steps = [whole.reshape(self.height, self.cols)], [0]
            self.rows = self.height
        else:
            self.parts, self.steps = gathered.parts, gathered.steps

    def specs(self):
        return [pl.BlockSpec(memory_space=pl.ANY)] * len(self.parts)

    def scratch(self):
        return [
            pltpu.VMEM((self.height, self.cols), LOW),
            pltpu.SemaphoreType.DMA((len(self.parts),)),
        ]

    def load(self, places, refs, room, sems):
        @pl.when(pl.program_id(0) == 0)
        def _():
            copies = []
            for i, (step, ref) in enumerate(zip(self.steps, refs)):
                at = pl.multiple_of(places[step] * self.rows, 16) if len(refs) > 1 else 0
                copies.append(
                    pltpu.make_async_copy(
                        ref.at[pl.ds(0, self.rows), :], room.at[pl.ds(at, self.rows), :], sems.at[i]
                    )
                )
            for copy in copies:
                copy.start()
            for copy in copies:
                copy.wait()


def unpack_small(gathered, first, dp, ctx, out_rows, gain_cols, head_cols):
    block, wide = gathered.parts[0].shape
    rows = block - first
    direct = first % 16 == 0 and rows % 16 == 0
    if direct:
        parts, steps = gathered.parts, gathered.steps
    else:
        parts, steps = [gathered.whole().reshape(dp, block, wide)[:, first:]], [0]
    half = out_rows // 2
    count = len(parts)

    def body(places, *refs):
        gain, head, out, room, sems = refs[count:]
        copies = []
        for i, ref in enumerate(refs[:count]):
            if direct:
                source, target = ref.at[pl.ds(first, rows), :], room.at[places[steps[i]]]
            else:
                source, target = ref, room
            copies.append(pltpu.make_async_copy(source, target, sems.at[i]))
        for copy in copies:
            copy.start()
        for copy in copies:
            copy.wait()
        lines = []
        for d in range(dp):
            extra = room[d, : 4 * ctx, :].astype(F32)
            lines += [extra[4 * c : 4 * c + 1] for c in range(ctx)]
            at, own = d * out_rows, room[d, 4 * ctx :, :]
            out[at : at + out_rows, :wide] = own[:out_rows]
            out[at : at + half, wide:] = own[out_rows:, : D - wide]
            out[at + half : at + out_rows, wide:] = own[out_rows:, D - wide :]
        for g in range(4):
            cut = [line[:, g * gain_cols : (g + 1) * gain_cols] for line in lines]
            gain[g : g + 1, :] = jnp.concatenate(cut, axis=1)
        for g in range(2):
            at = 4 * gain_cols + g * head_cols
            cut = [line[:, at : at + head_cols] for line in lines]
            head[g : g + 1, :] = jnp.concatenate(cut, axis=1)

    return call(
        body,
        [like((4, D), F32), like((2, HD), F32), like((HD, D), LOW)],
        [pl.BlockSpec(memory_space=pl.ANY)] * count,
        [held((4, D)), held((2, HD)), held((HD, D))],
        tuple(parts),
        scratch=[pltpu.VMEM((dp, rows, wide), LOW), pltpu.SemaphoreType.DMA((count,))],
        prefetch=(gathered.ring.places,),
    )


def input_stage(x, w_in, gain, head_rows, cos_t, sin_t, row_map, places):
    seq = x.shape[0]
    count = len(w_in.parts)

    def body(_, pl_ref, x0, x1, g, hg, cos, sin, *refs):
        q, k, v, raw, n_ref, w, sems = refs[count:]
        w_in.load(pl_ref, refs[:count], w, sems)
        for i, x_ref in enumerate((x0, x1)):
            at = slice(i * TILE, (i + 1) * TILE)
            xf = x_ref[...].astype(F32)
            n = (xf * scale_of(xf) * g[...]).astype(LOW)
            n_ref[at, :] = n
            y = mm(n, w[...])
            qy, ky = y[:, :HD], y[:, HD : 2 * HD]
            raw[at, :] = y[:, : 2 * HD]
            c, s = cos[at, :], sin[at, :]
            q[at, :] = turn(qy * scale_of(qy) * hg[0:1], c, s, 1.0).astype(LOW)
            k[at, :] = turn(ky * scale_of(ky) * hg[1:2], c, s, 1.0).astype(LOW)
            v[at, :] = y[:, 2 * HD :].astype(LOW)

    def block(cols):
        return pl.BlockSpec((2 * TILE, cols), lambda p, m, s: (p, 0))

    return call(
        body,
        [like((seq, HD), LOW)] * 3 + [like((seq, 2 * HD), F32), like((seq, D), LOW)],
        [
            pl.BlockSpec((TILE, D), lambda p, m, s: (m[2 * p], 0)),
            pl.BlockSpec((TILE, D), lambda p, m, s: (m[2 * p + 1], 0)),
            held((1, D)),
            held((2, HD)),
            block(HD // 2),
            block(HD // 2),
        ]
        + w_in.specs(),
        [block(HD)] * 3 + [block(2 * HD), block(D)],
        (x, x, gain, head_rows, cos_t, sin_t, *w_in.parts),
        grid=(seq // TILE // 2,),
        flops=2 * seq * D * 3 * HD,
        scratch=w_in.scratch(),
        prefetch=(row_map, places),
    )


def scores_of(q, k, doc_step):
    s = mm_nt(q, k) * HD ** (-0.5)
    row = lax.broadcasted_iota(jnp.int32, s.shape, 0) + doc_step * TILE
    col = lax.broadcasted_iota(jnp.int32, s.shape, 1)
    return jnp.where(col <= row, s, -1e30)


def attention(q, k, v, base):
    seq = q.shape[0]

    def body(b, q_ref, k_ref, v_ref, mixed, lse):
        for doc, count in enumerate((LONG, SHORT)):
            first = b[doc]
            for i in range(count):
                p = first + i
                at = pl.ds(pl.multiple_of(p * TILE, TILE), TILE)
                keys = pl.ds(pl.multiple_of(first * TILE, TILE), (i + 1) * TILE)
                s = scores_of(q_ref[at, :], k_ref[keys, :], i)
                peak = jnp.max(s, axis=-1, keepdims=True)
                e = jnp.exp(s - peak)
                total = jnp.sum(e, axis=-1, keepdims=True)
                lse[at, :] = peak + jnp.log(total)
                probs = (e * (1.0 / total)).astype(LOW)
                to = pl.ds(pl.multiple_of(stored_block(p) * TILE, TILE), TILE)
                mixed[to, :] = mm(probs, v_ref[keys, :]).astype(LOW)

    return call(
        body,
        [like((seq, HD), LOW), like((seq, 1), F32)],
        [held((seq, HD))] * 3,
        [held((seq, HD)), held((seq, 1))],
        (q, k, v),
        flops=4 * 24 * TILE * TILE * HD,
        prefetch=(base,),
    )


def attention_back(q, k, v, raw, lse, grads, head_rows, cos_t, sin_t, base):
    seq = q.shape[0]
    chip = seq // 2

    def pull_head(v_raw, g, dy, cos, sin):
        dy = turn(dy, cos, sin, -1.0)
        s = scale_of(v_raw)
        return norm_pull(v_raw, s, g, dy), jnp.sum(dy * v_raw * s, axis=0, keepdims=True)

    def body(b, q_ref, k_ref, v_ref, raw_ref, l_ref, *refs):
        hg, cos, sin, out, head_out, dk, dv, mixed_grad = refs[6:]
        for i in range(2):
            mine, near, far = refs[3 * i : 3 * i + 3]
            rows = pl.ds(pl.multiple_of((b[2] if i == 0 else 1 - b[2]) * chip, chip), chip)
            mixed_grad[rows, :] = (
                mine[0].astype(F32) + near[0].astype(F32) + far[...].astype(F32)
            ).astype(LOW)
        dk[...] = jnp.zeros_like(dk)
        dv[...] = jnp.zeros_like(dv)
        head_q = jnp.zeros((1, HD), F32)
        for doc, count in enumerate((LONG, SHORT)):
            first = b[doc]
            for i in range(count):
                p = first + i
                at = pl.ds(pl.multiple_of(p * TILE, TILE), TILE)
                keys = pl.ds(pl.multiple_of(first * TILE, TILE), (i + 1) * TILE)
                src = pl.ds(pl.multiple_of(stored_block(p) * TILE, TILE), TILE)
                do = mixed_grad[src, :]
                qs = q_ref[at, :]
                probs = jnp.exp(scores_of(qs, k_ref[keys, :], i) - l_ref[at, :])
                dp = mm_nt(do, v_ref[keys, :])
                inner = jnp.sum(probs * dp, axis=-1, keepdims=True)
                ds = (probs * (dp - inner)).astype(LOW)
                dq = mm(ds, k_ref[keys, :]) * HD ** (-0.5)
                dk[keys, :] += mm_tn(ds, qs)
                dv[keys, :] += mm_tn(probs.astype(LOW), do)
                dq, part = pull_head(raw_ref[at, :HD], hg[0:1], dq, cos[at, :], sin[at, :])
                head_q += part
                out[at, :HD] = dq.astype(LOW)
        head_k = jnp.zeros((1, HD), F32)
        for p in range(seq // TILE):
            at = slice(p * TILE, (p + 1) * TILE)
            dkp, part = pull_head(
                raw_ref[at, HD:], hg[1:2], dk[at, :] * HD ** (-0.5), cos[at, :], sin[at, :]
            )
            head_k += part
            out[at, HD : 2 * HD] = dkp.astype(LOW)
            out[at, 2 * HD :] = dv[at, :].astype(LOW)
        head_out[0:1, :] = head_q
        head_out[1:2, :] = head_k

    pair = pl.BlockSpec((1, chip, HD), lambda *_: (0, 0, 0), pipeline_mode=pl.Buffered(1))
    return call(
        body,
        [like((seq, 3 * HD), LOW), like((2, HD), F32)],
        [held((seq, HD))] * 3
        + [held((seq, 2 * HD)), held((seq, 1))]
        + [pair, pair, held((chip, HD))] * 2
        + [held((2, HD))]
        + [held((seq, HD // 2))] * 2,
        [held((seq, 3 * HD)), held((2, HD))],
        (q, k, v, raw, lse, *grads, head_rows, cos_t, sin_t),
        flops=10 * 24 * TILE * TILE * HD,
        scratch=[pltpu.VMEM((seq, HD), F32)] * 2 + [pltpu.VMEM((seq, HD), LOW)],
        prefetch=(base,),
    )


def project(mixed, outs, x, gains, stored_map):
    seq = x.shape[0]

    def body(_, m0, m1, m2, m3, w0, w1, w2, w3, x_ref, g, proj, pre):
        for i in range(2):
            at = slice(i * TILE, (i + 1) * TILE)
            y = mm(m0[at, :], w0[...]) + mm(m1[at, :], w1[...])
            y = y + mm(m2[at, :], w2[...]) + mm(m3[at, :], w3[...])
            proj[at, :] = y
            r = x_ref[at, :].astype(F32) + y * scale_of(y) * g[1:2]
            pre[at, :] = (r * scale_of(r) * g[2:3]).astype(LOW)

    def block(cols):
        return pl.BlockSpec((2 * TILE, cols), lambda r, m: (r, 0))

    return call(
        body,
        [like((seq, D), F32), like((seq, D), LOW)],
        [pl.BlockSpec((2 * TILE, HD), lambda r, m: (m[2 * r] // 2, 0))] * 4
        + [held((HD, D))] * 4
        + [block(D), held((4, D))],
        [block(D), block(D)],
        (*mixed, *outs, x, gains),
        grid=(seq // TILE // 2,),
        flops=2 * seq * D * H * HD,
        prefetch=(stored_map,),
    )


def column_cuts(main, width):
    return [(at, min(width, main - at)) for at in range(0, main, width)]


def gate_stage(pre, w, places, half, into=()):
    seq, part = pre.shape[0], w.cols // 2
    rows = 512
    first = half * (seq // 2 // rows)
    count = len(w.parts)

    def pieces(g, u):
        t = jnp.tanh(GELU_A * (g + GELU_B * (g * g * g)))
        a = 0.5 * g * (1.0 + t)
        slope = 0.5 * (1.0 + t) + (0.5 * g) * (1.0 - t * t) * (GELU_A * (1.0 + 3.0 * GELU_B * (g * g)))
        return a * u, u * slope, a

    def body(pl_ref, p_ref, *refs):
        hidden, ab, room, sems = refs[count:]
        w.load(pl_ref, refs[:count], room, sems)
        p = p_ref[...]

        def multiply(at, wide):
            return mm(p, room[:, at : at + wide]), mm(p, room[:, part + at : part + at + wide])

        def finish(at, wide, made):
            h, b, a = pieces(*made)
            hidden[:, at : at + wide] = h.astype(LOW)
            ab[:, at : at + wide] = b.astype(LOW)
            ab[:, part + at : part + at + wide] = a.astype(LOW)

        last = None
        for cut in column_cuts(part, 256):
            made = multiply(*cut)
            if last is not None:
                finish(*last)
            last = (*cut, made)
        finish(*last)

    def block(cols):
        return pl.BlockSpec((rows, cols), lambda r, m: (first + r, 0))

    return call(
        body,
        [like((seq, part), LOW), like((seq, 2 * part), LOW)],
        [block(D)] + w.specs(),
        [block(part), block(2 * part)],
        (pre, *w.parts),
        grid=(seq // 2 // rows,),
        flops=2 * seq * D * part,
        scratch=w.scratch(),
        into=into,
        prefetch=(places,),
    )


def down_stage(hidden, w, places, half):
    seq, part = hidden.shape
    rows = seq // 4
    count = len(w.parts)

    def body(pl_ref, h, *refs):
        even, odd, room, sems = refs[count:]
        w.load(pl_ref, refs[:count], room, sems)
        odd[...] = mm(h[rows:, :], room[...]).astype(LOW)
        even[...] = mm(h[:rows, :], room[...]).astype(LOW)

    return call(
        body,
        [like((rows, D), LOW)] * 2,
        [
            pl.BlockSpec(
                (2 * rows, part), lambda r, m: (half, 0), pipeline_mode=pl.Buffered(1)
            )
        ]
        + w.specs(),
        [held((rows, D))] * 2,
        (hidden, *w.parts),
        flops=4 * rows * D * part,
        scratch=w.scratch(),
        prefetch=(places,),
    )


def ffn_stage(parts, near, far, proj, x, cot, gains):
    rows = cot.shape[0]

    def body(p, n, f, proj_ref, x_ref, c_ref, g, out, grad, gain):
        y = p[...].astype(F32) + n[...].astype(F32) + f[...].astype(F32)
        pr = proj_ref[...]
        s = scale_of(y)
        r = x_ref[...].astype(F32) + pr * scale_of(pr) * g[1:2]
        out[...] = (r + y * s * g[3:4]).astype(LOW)
        dy = c_ref[...].astype(F32)
        grad[...] = norm_pull(y, s, g[3:4], dy).astype(LOW)
        part = jnp.sum(dy * y * s, axis=0, keepdims=True)

        @pl.when(pl.program_id(0) == 0)
        def _():
            gain[...] = part

        @pl.when(pl.program_id(0) > 0)
        def _():
            gain[...] += part

    block = pl.BlockSpec((TILE, D), lambda r: (r, 0))
    return call(
        body,
        [like((rows, D), LOW), like((rows, D), LOW), like((1, D), F32)],
        [block] * 6 + [held((4, D))],
        [block, block, held((1, D))],
        (parts, near, far, proj, x, cot, gains),
        grid=(rows // TILE,),
    )


def hidden_back(grad, w, ab, places, half, into=()):
    seq, part = ab.shape[0], ab.shape[1] // 2
    rows = 512
    first = half * (seq // 2 // rows)
    count = len(w.parts)

    def body(pl_ref, g_ref, ab_ref, *refs):
        out, room, sems = refs[count:]
        w.load(pl_ref, refs[:count], room, sems)
        g = g_ref[...]
        for at, wide in column_cuts(part, 256):
            hg = mm_nt(g, room[at : at + wide, :])
            for side in (at, part + at):
                out[:, side : side + wide] = (hg * ab_ref[:, side : side + wide].astype(F32)).astype(LOW)

    def block(cols):
        return pl.BlockSpec((rows, cols), lambda r, m: (first + r, 0))

    return call(
        body,
        [like((seq, 2 * part), LOW)],
        [pl.BlockSpec((rows, D), lambda r, m: (r, 0)), block(2 * part)] + w.specs(),
        [block(2 * part)],
        (grad, ab, *w.parts),
        grid=(seq // 2 // rows,),
        flops=seq * D * part,
        scratch=w.scratch(),
        into=into,
        prefetch=(places,),
    )[0]


def residual_back(gu, w, outs, proj, x, cot, gains, stored_map, places, half, into=()):
    seq, wide = gu.shape
    own = cot.shape[0] // TILE
    steps = seq // 2 // TILE
    first = half * steps
    count = len(w.parts)

    def body(_, pl_ref, gu_ref, w0, w1, w2, w3, proj_ref, x_ref, c_ref, g, *refs):
        rg, pg, even, odd, gain, room, sems, *made = refs[count:]
        w.load(pl_ref, refs[:count], room, sems)
        step = pl.program_id(0)

        def multiply(turn):
            made[turn][...] = mm_nt(gu_ref[...], room[...])

        def finish(turn):
            dy = made[turn][...]
            pr = proj_ref[...]
            sp = scale_of(pr)
            r = x_ref[...].astype(F32) + pr * sp * g[1:2]
            s = scale_of(r)
            dr = norm_pull(r, s, g[2:3], dy)
            if half == 0:
                dr = dr + jnp.where(step <= own, 1.0, 0.0) * c_ref[...].astype(F32)
            rg[...] = dr.astype(LOW)
            low = norm_pull(pr, sp, g[1:2], dr).astype(LOW)
            pg[...] = low
            even[0] = mm_nt(low, w0[...]).astype(LOW)
            odd[0] = mm_nt(low, w1[...]).astype(LOW)
            even[1] = mm_nt(low, w2[...]).astype(LOW)
            odd[1] = mm_nt(low, w3[...]).astype(LOW)
            before = jnp.where(step == 1, 0.0, gain[...])
            gain[0:1, :] = before[0:1] + jnp.sum(dr * pr * sp, axis=0, keepdims=True)
            gain[1:2, :] = before[1:2] + jnp.sum(dy * r * s, axis=0, keepdims=True)

        @pl.when(step == 0)
        def _():
            multiply(0)

        for turn in range(2):

            @pl.when((step > 0) & (step < steps) & (step % 2 == turn))
            def _():
                multiply(turn)
                finish(1 - turn)

        @pl.when(step == steps)
        def _():
            finish((steps - 1) % 2)

    def last(i):
        return jnp.maximum(i - 1, 0)

    def block(cols):
        return pl.BlockSpec((TILE, cols), lambda i, m, p: (first + last(i), 0))

    heads = pl.BlockSpec((2, TILE, HD), lambda i, m, p: (0, m[first + last(i)] % steps, 0))
    return call(
        body,
        [like((seq, D), LOW), like((seq, D), LOW)]
        + [like((2, seq // 2, HD), LOW)] * 2
        + [like((2, D), F32)],
        [pl.BlockSpec((TILE, wide), lambda i, m, p: (first + jnp.minimum(i, steps - 1), 0))]
        + [held((HD, D))] * 4
        + [block(D), block(D)]
        + [pl.BlockSpec((TILE, D), lambda i, m, p: (jnp.minimum(last(i), own - 1), 0)), held((4, D))]
        + w.specs(),
        [
            block(D),
            pl.BlockSpec((TILE, D), lambda i, m, p: (m[first + last(i)], 0)),
            heads,
            heads,
            held((2, D)),
        ],
        (gu, *outs, proj, x, cot, gains, *w.parts),
        grid=(steps + 1,),
        flops=seq * D * (wide + H * HD),
        scratch=w.scratch() + [pltpu.VMEM((TILE, D), F32)] * 2,
        into=into,
        prefetch=(stored_map, places),
    )


def input_back(qkv, w_in, x, rg, gain, pos_map, places):
    seq = x.shape[0]
    rows = 2 * TILE
    count = len(w_in.parts)

    def body(_, pl_ref, q0, q1, x_ref, rg_ref, g, *refs):
        even, odd, gain_out, w, sems = refs[count:]
        w_in.load(pl_ref, refs[:count], w, sems)
        step = pl.program_id(0)
        total = jnp.zeros((1, D), F32)
        made = []
        for i, q_ref in enumerate((q0, q1)):
            at = slice(i * TILE, (i + 1) * TILE)
            dy = mm_nt(q_ref[...], w[...])
            xf = x_ref[at, :].astype(F32)
            s = scale_of(xf)
            made.append((rg_ref[at, :].astype(F32) + norm_pull(xf, s, g[...], dy)).astype(LOW))
            total += jnp.sum(dy * xf * s, axis=0, keepdims=True)
        gain_out[...] = jnp.where(step == 0, 0.0, gain_out[...]) + total

        @pl.when(step % 2 == 0)
        def _():
            even[:TILE, :], even[TILE:, :] = made

        @pl.when(step % 2 == 1)
        def _():
            odd[:TILE, :], odd[TILE:, :] = made

    block = pl.BlockSpec((rows, D), lambda i, m, s: (i, 0))
    out = pl.BlockSpec((rows, D), lambda i, m, s: (i // 2, 0))
    return call(
        body,
        [like((seq // 2, D), LOW)] * 2 + [like((1, D), F32)],
        [
            pl.BlockSpec((TILE, 3 * HD), lambda i, m, s: (m[2 * i], 0)),
            pl.BlockSpec((TILE, 3 * HD), lambda i, m, s: (m[2 * i + 1], 0)),
            block,
            block,
            held((1, D)),
        ]
        + w_in.specs(),
        [out, out, held((1, D))],
        (qkv, qkv, x, rg, gain, *w_in.parts),
        grid=(seq // rows,),
        flops=2 * seq * D * 3 * HD,
        scratch=w_in.scratch(),
        prefetch=(pos_map, places),
    )


def local(
    tokens,
    cotangent,
    lengths,
    w_qkv,
    w_out,
    w_gate_up,
    w_down,
    gains,
    head_gains,
    first_qkv,
    first_out,
    first_gate_up,
    first_down,
    first_gains,
    first_head,
    second_qkv,
    second_out,
    second_gate_up,
    second_down,
    second_gains,
    second_head,
):
    low = jnp.bfloat16
    f32 = jnp.float32
    rows = tokens.shape[1]
    dp = lax.axis_size("dp")
    ctx = lax.axis_size("ctx")
    place = lax.axis_index("ctx")
    seq = rows * ctx
    in_rows = w_qkv.shape[0]
    out_rows = w_out.shape[0]
    ff_rows = w_down.shape[0]
    gain_cols = gains.shape[1]
    head_cols = head_gains.shape[1]
    qkv_cols = 3 * HD
    ring = Ring()

    q_cols = w_qkv[:, : H * HD].astype(low).reshape(in_rows, ctx, HD).transpose(1, 0, 2)
    kv_cols = jnp.broadcast_to(w_qkv[:, H * HD :].astype(low)[None], (ctx, in_rows, 2 * HD))
    extra = jnp.concatenate(
        [gains.astype(low).reshape(-1), head_gains.astype(low).reshape(-1)]
    )
    extra = jnp.pad(extra, (0, 4 * qkv_cols - extra.shape[0])).reshape(4, qkv_cols)
    small_sent = jnp.concatenate(
        [
            jnp.concatenate([q_cols, kv_cols], axis=2),
            jnp.broadcast_to(extra[None], (ctx, 4, qkv_cols)),
        ],
        axis=1,
    )
    to_user = [((dp * c + d), d * ctx + c) for d in range(dp) for c in range(ctx)]
    to_owner = [(b, a) for a, b in to_user]
    out_mine = lax.ppermute(w_out.astype(low), ("dp", "ctx"), to_user)
    half = out_rows // 2
    small = exchange(small_sent, "ctx")
    packed = pack_columns(tie(w_gate_up, small_sent), dp, ctx)
    own_rows = ctx * in_rows
    small_ring = Gather(
        ring,
        jnp.concatenate(
            [
                small[:, :in_rows].reshape(own_rows, qkv_cols),
                small[:, in_rows:].reshape(4 * ctx, qkv_cols),
                out_mine[:, :qkv_cols],
                jnp.concatenate([out_mine[:half, qkv_cols:], out_mine[half:, qkv_cols:]], axis=1),
            ]
        ),
    )
    down_block = jnp.pad(w_down.astype(low), ((0, padded(ff_rows) - ff_rows), (0, 0)))
    down_ring = Gather(ring, down_block)
    down_first = down_ring.advance()
    tokens_far = swap(tie(tokens[0], small), 2)
    tokens_near = swap(tie(tokens[0], small), 1)
    gate_up_cols = exchange(tie(packed, tokens_far), "ctx").reshape(own_rows, -1)
    first_len = lengths[0, 0]
    pos = tie(jnp.arange(seq, dtype=jnp.int32), packed)
    cos_t, sin_t = rope_tables(pos - jnp.where(pos < first_len, 0, first_len), HD)
    small_ring.advance(*down_first)
    small_ring.advance(cos_t, sin_t)
    tokens_last = swap(tie(tokens_far, *small_ring.held.values()), 1)
    tokens_all = jnp.concatenate([tokens[0], tokens_near, tokens_far, tokens_last])
    while small_ring.hop < ring.hops[0]:
        small_ring.advance()
    small_seen = list(small_ring.held.values())
    gate_ring = Gather(ring, gate_up_cols)
    gate_seen = gate_ring.advance(*small_seen, tokens_last)
    w_in = Blocks(small_ring, own_rows)
    places = ring.places
    gain_rows, head_rows, out_mine = unpack_small(
        small_ring, own_rows, dp, ctx, out_rows, gain_cols, head_cols
    )
    out_far, out_near = swap(out_mine, 2), swap(out_mine, 1)

    blocks = seq // TILE
    split = first_len // TILE
    base = jnp.where(split == LONG, jnp.array([0, LONG, 0]), jnp.array([SHORT, 0, 0]))
    base = (base + jnp.array([0, 0, 1]) * (place // 2)).astype(jnp.int32)
    tiles = jnp.arange(blocks, dtype=jnp.int32)
    stored_map = 2 * (place ^ (tiles // 2)) + tiles % 2
    owner = jnp.where(tiles < ctx, tiles, 2 * ctx - 1 - tiles)
    row_map = 2 * (place ^ owner) + (tiles >= ctx)
    pos_map = jnp.where(tiles % 2 == 0, stored_map // 2, 2 * ctx - 1 - stored_map // 2)

    q, k, v, raw, normed = input_stage(
        tokens_all, w_in, gain_rows[0:1], head_rows, cos_t, sin_t, row_map, places
    )
    down_second = down_ring.advance(q, *gate_seen)
    gate_ring.advance(q)
    mixed, lse = attention(tie(q, *gate_seen, out_far, out_near), k, v, base)
    mixed = tie(mixed, *down_second)
    mixed_far, mixed_near = swap(mixed, 2), swap(mixed, 1)
    out_parts = [out_mine, out_near, out_far, swap(tie(out_far, mixed), 1)]
    down_ring.advance(mixed)
    gate_ring.advance(mixed)
    mixed_parts = [mixed, mixed_near, mixed_far, swap(mixed_far, 1)]
    proj, pre_low = project(mixed_parts, out_parts, tokens_all, gain_rows, stored_map)
    while gate_ring.hop < ring.hops[0]:
        gate_ring.advance(pre_low)
        if down_ring.hop < ring.hops[0]:
            down_ring.advance(pre_low)
    down_ring.finish()
    full_gate_up = Blocks(gate_ring)
    full_down = Blocks(down_ring)
    buffers = gate_stage(pre_low, full_gate_up, places, 1)
    even, odd = down_stage(buffers[0], full_down, places, 1)
    summed = add_low(even, swap(odd, 1))
    far = swap(summed, 2)
    hidden_low, slopes = gate_stage(tie(pre_low, summed), full_gate_up, places, 0, buffers)
    even, odd = down_stage(tie(hidden_low, far), full_down, places, 0)
    near = swap(odd, 1)
    result, ffn_grad, gain_grad_d = ffn_stage(
        even, near, far, proj, tokens[0], cotangent[0], gain_rows
    )

    far = swap(ffn_grad, 2)
    ffn_here = jnp.concatenate([ffn_grad, swap(ffn_grad, 1)])
    residual = partial(
        residual_back,
        w=full_gate_up,
        outs=out_parts,
        proj=proj,
        x=tokens_all,
        cot=cotangent[0],
        gains=gain_rows,
        stored_map=stored_map,
        places=places,
    )
    gate_up_low = hidden_back(ffn_here, full_down, slopes, places, 0)
    far = tie(far, gate_up_low)
    ffn_there = jnp.concatenate([far, swap(far, 1)])
    gate_up_low = hidden_back(ffn_there, full_down, slopes, places, 1, (gate_up_low,))
    grad_gate_up = mm_tn(pre_low, gate_up_low).astype(low)
    gate_sum = Reduce(ring, grad_gate_up).send()
    resid_grad, proj_low, even, odd, gain_grad_here = residual(
        tie(gate_up_low, *gate_sum.tokens()), half=0
    )
    held_gate = gate_sum.absorb(resid_grad)
    near = swap(tie(odd, *held_gate), 1)
    parts_here = (even, near)
    summed = add_low(even[1], near[1])
    far_there = swap(summed, 2)
    gate_sum.send()
    ffn_low = jnp.concatenate([ffn_here, ffn_there])
    grad_down = mm_tn(hidden_low, tie(ffn_low, summed, *held_gate)).astype(low)
    down_sum = Reduce(ring, grad_down).send()
    resid_grad, proj_low, even, odd, gain_grad_there = residual(
        tie(gate_up_low, far_there, *down_sum.tokens()), half=1, into=(resid_grad, proj_low)
    )
    held_gate = gate_sum.absorb(odd)
    held_down = down_sum.absorb(odd)
    near = swap(tie(odd, *held_gate, *held_down), 1)
    summed = add_low(even[1], near[1])
    far_here = swap(summed, 2)
    gate_sum.send(summed)
    down_sum.send(summed)
    proj_low = tie(proj_low, summed)
    grad_out = [mm_tn(m, proj_low).astype(low) for m in mixed_parts]
    far_here = tie(far_here, *grad_out)
    grad_out = reduce_ctx(grad_out).astype(low)
    qkv_low, head_grads = attention_back(
        q,
        k,
        v,
        raw,
        lse,
        parts_here + (far_here,) + (even, near, far_there),
        head_rows,
        cos_t,
        sin_t,
        base,
    )
    held_gate = gate_sum.absorb(qkv_low)
    held_down = down_sum.absorb(qkv_low)
    gate_sum.send()
    down_sum.send()
    grad_in = mm_tn(tie(normed, *held_gate, *held_down), qkv_low).astype(low)
    grad_out = grad_out.reshape(dp, out_rows, D)
    in_blocks = jnp.concatenate(
        [
            grad_in.reshape(dp, own_rows, qkv_cols),
            grad_out[:, :, :qkv_cols],
            jnp.concatenate(
                [grad_out[:, :half, qkv_cols:], grad_out[:, half:, qkv_cols:]], axis=2
            ),
        ],
        axis=1,
    )
    in_sum = Reduce(ring, in_blocks.reshape(-1, qkv_cols)).send()
    input_even, input_odd, gain_grad_a = input_back(
        tie(qkv_low, *in_sum.tokens()),
        w_in,
        tokens_all,
        resid_grad,
        gain_rows[0:1],
        pos_map,
        places,
    )
    gate_sum.absorb(input_odd)
    down_sum.absorb(input_odd)
    in_sum.absorb(input_odd)
    gate_up_own = gate_sum.finish().astype(low)
    in_sum.send(gate_up_own)
    down_own = down_sum.finish()[:ff_rows]
    gate_up_own = exchange(gate_up_own.reshape(ctx, in_rows, -1), "ctx")
    near = swap(input_odd, 1)
    summed = add_low(input_even[rows:], near[rows:])
    gain_grad_bc = gain_grad_here + gain_grad_there
    in_sum.absorb()

    in_own = in_sum.finish().astype(low)
    gate_up_own = unpack_columns(gate_up_own, dp, ctx, ff_rows)
    out_own = in_own[own_rows:]
    out_own = jnp.concatenate(
        [
            out_own[:out_rows],
            jnp.concatenate(
                [out_own[out_rows:, : D - qkv_cols], out_own[out_rows:, D - qkv_cols :]], axis=0
            ),
        ],
        axis=1,
    )
    out_own = lax.ppermute(out_own, ("dp", "ctx"), to_owner).astype(f32)
    in_own = exchange(in_own[:own_rows].reshape(ctx, in_rows, qkv_cols), "ctx").astype(f32)
    qkv_own = jnp.concatenate(
        [
            in_own[:, :, :HD].transpose(1, 0, 2).reshape(in_rows, H * HD),
            jnp.sum(in_own[:, :, HD:], axis=0),
        ],
        axis=1,
    )
    gain_grads = jnp.concatenate([gain_grad_a, gain_grad_bc, gain_grad_d], axis=0)
    local_squares = jnp.float32(0.0)
    for piece in (qkv_own, out_own, gate_up_own, down_own):
        local_squares = local_squares + jnp.sum(piece * piece)
    lines = jnp.concatenate([gain_grads.reshape(-1, 128), head_grads.reshape(-1, 128)])
    squares = jnp.pad(local_squares.reshape(1, 1), ((0, 7), (0, 127)))
    sums = tie(jnp.concatenate([lines, squares]), summed)
    sums = sums + swap(sums, 2)
    far = swap(tie(summed, sums), 2)
    input_grad = (
        input_even[:rows].astype(f32) + near[:rows].astype(f32) + far.astype(f32)
    )
    sums = sum_rest(sums)
    small_grads = sums[: lines.shape[0]]
    index = lax.axis_index("dp") * ctx + place
    gains_own = lax.dynamic_slice_in_dim(
        small_grads[: 4 * D // 128].reshape(4, D), index * gain_cols, gain_cols, axis=1
    )
    head_own = lax.dynamic_slice_in_dim(
        small_grads[4 * D // 128 :].reshape(2, HD), index * head_cols, head_cols, axis=1
    )
    reduced = (qkv_own, out_own, gate_up_own, down_own, gains_own, head_own)
    total_squares = sums[lines.shape[0], 0] + jnp.sum(small_grads * small_grads)
    grad_norm = jnp.sqrt(total_squares)
    factor = 1.0 / jnp.maximum(grad_norm, 1.0)
    weights = (w_qkv, w_out, w_gate_up, w_down, gains, head_gains)
    firsts = (first_qkv, first_out, first_gate_up, first_down, first_gains, first_head)
    seconds = (second_qkv, second_out, second_gate_up, second_down, second_gains, second_head)
    rates = (D ** (-0.5), (H * HD) ** (-0.5), D ** (-0.5), FF ** (-0.5), GAIN_RATE, GAIN_RATE)
    decays = (WEIGHT_DECAY, WEIGHT_DECAY, WEIGHT_DECAY, WEIGHT_DECAY, 0.0, 0.0)
    reduced = reduced[:2] + (tie(gate_up_own, far, grad_norm),) + reduced[3:]
    updates = [
        adam_update(
            weights[index],
            firsts[index],
            seconds[index],
            reduced[index] * factor,
            rates[index],
            decays[index],
        )
        for index in range(6)
    ]
    return (
        result[None],
        input_grad[None],
        updates[0][0],
        updates[1][0],
        updates[2][0],
        updates[3][0],
        updates[4][0],
        updates[5][0],
        updates[0][1],
        updates[1][1],
        updates[2][1],
        updates[3][1],
        updates[4][1],
        updates[5][1],
        updates[0][2],
        updates[1][2],
        updates[2][2],
        updates[3][2],
        updates[4][2],
        updates[5][2],
        grad_norm,
    )


def solution(mesh):
    in_specs = (
        P("dp", "ctx", None),
        P("dp", "ctx", None),
        P("dp", None),
        P(("dp", "ctx"), None),
        P(("dp", "ctx"), None),
        P(("dp", "ctx"), None),
        P(("dp", "ctx"), None),
        P(None, ("dp", "ctx")),
        P(None, ("dp", "ctx")),
        P(("dp", "ctx"), None),
        P(("dp", "ctx"), None),
        P(("dp", "ctx"), None),
        P(("dp", "ctx"), None),
        P(None, ("dp", "ctx")),
        P(None, ("dp", "ctx")),
        P(("dp", "ctx"), None),
        P(("dp", "ctx"), None),
        P(("dp", "ctx"), None),
        P(("dp", "ctx"), None),
        P(None, ("dp", "ctx")),
        P(None, ("dp", "ctx")),
    )
    out_specs = (
        P("dp", "ctx", None),
        P("dp", "ctx", None),
        P(("dp", "ctx"), None),
        P(("dp", "ctx"), None),
        P(("dp", "ctx"), None),
        P(("dp", "ctx"), None),
        P(None, ("dp", "ctx")),
        P(None, ("dp", "ctx")),
        P(("dp", "ctx"), None),
        P(("dp", "ctx"), None),
        P(("dp", "ctx"), None),
        P(("dp", "ctx"), None),
        P(None, ("dp", "ctx")),
        P(None, ("dp", "ctx")),
        P(("dp", "ctx"), None),
        P(("dp", "ctx"), None),
        P(("dp", "ctx"), None),
        P(("dp", "ctx"), None),
        P(None, ("dp", "ctx")),
        P(None, ("dp", "ctx")),
        P(),
    )
    return jax.shard_map(local, mesh=mesh, in_specs=in_specs, out_specs=out_specs, check_vma=False)
```

```python
from functools import partial

import jax
import jax.numpy as jnp
from jax import lax
from jax.experimental import pallas as pl
from jax.experimental.pallas import tpu as pltpu
from jax.sharding import PartitionSpec as P

D = 1152
H = 4
HD = 256
FF = 6912
STEP = 10

EPSILON = 1e-06
ROPE_BASE = 1000000.0
BETA_ONE = 0.9
BETA_TWO = 0.95
ADAM_EPSILON = 1e-08
WEIGHT_DECAY = 0.1
GAIN_RATE = 1.0


def rope_tables(offsets, width):
    half = width // 2
    freq = jnp.exp(-jnp.log(ROPE_BASE) * jnp.arange(half, dtype=jnp.float32) * (2.0 / width))
    angle = offsets.astype(jnp.float32)[:, None] * freq[None, :]
    return (jnp.cos(angle), jnp.sin(angle))


def adam_update(weight, first, second, grad, rate, decay):
    first_new = BETA_ONE * first + (1.0 - BETA_ONE) * grad
    second_new = BETA_TWO * second + (1.0 - BETA_TWO) * grad * grad
    first_hat = first_new / (1.0 - BETA_ONE**STEP)
    second_hat = second_new / (1.0 - BETA_TWO**STEP)
    updated = weight - rate * (first_hat / (jnp.sqrt(second_hat) + ADAM_EPSILON) + decay * weight)
    return (updated, first_new, second_new)


def exchange(parts, axis):
    return lax.all_to_all(parts, axis, split_axis=0, concat_axis=0, tiled=True)


def swap(value, bit):
    count = lax.axis_size("ctx")
    return lax.ppermute(value, "ctx", [(i, i ^ bit) for i in range(count)])


def swap_dp(value, bit):
    count = lax.axis_size("dp")
    return lax.ppermute(value, "dp", [(i, i ^ bit) for i in range(count)])


def gather_ctx(block):
    far = swap(block, 2)
    return [block, swap(block, 1), far, swap(far, 1)]


def add_low(a, b):
    return a + b


def reduce_ctx(blocks):
    near, far = jnp.concatenate([blocks[1], blocks[3]]), None
    near = swap(near, 1)
    size = blocks[0].shape[0]
    far = swap(add_low(blocks[2], near[size:]), 2)
    mine = blocks[0].astype(jnp.float32) + near[:size].astype(jnp.float32)
    return mine + far.astype(jnp.float32)


def reorder(value, bit, rows):
    parts = [value[j * rows : (j + 1) * rows] for j in range(value.shape[0] // rows)]
    return jnp.concatenate([parts[j ^ bit] for j in range(len(parts))])


def sum_rest(value):
    value = value + swap(value, 1)
    bit = 1
    while bit < lax.axis_size("dp"):
        value = value + swap_dp(value, bit)
        bit *= 2
    return value


def tie(value, *tokens):
    return lax.optimization_barrier((value, *tokens))[0]


class Ring:
    def __init__(self):
        count = self.count = lax.axis_size("dp")
        self.ctx = lax.axis_size("ctx")
        self.order = list(range(0, count, 2)) + list(range(count - 1, 0, -2))
        self.hops = (count // 2, count - 1 - count // 2)
        table = [
            [self.order[(self.order.index(i) + sense * step) % count] for step in range(count)]
            for sense in (1, -1)
            for i in range(count)
        ]
        row = (lax.axis_index("ctx") % 2) * count + lax.axis_index("dp")
        self.places = lax.dynamic_slice(
            jnp.array(table, jnp.int32), (row, 0), (1, count), allow_negative_indices=False
        )[0]

    def send(self, value, way):
        pairs = []
        for place, source in enumerate(self.order):
            for c in range(self.ctx):
                target = self.order[(place + (way if c % 2 == 0 else -way)) % self.count]
                pairs.append((source * self.ctx + c, target * self.ctx + c))
        return lax.ppermute(value, ("dp", "ctx"), pairs)

    def ways(self, hop):
        return [way for way, last in zip((1, -1), self.hops) if hop <= last]


class Gather:
    def __init__(self, ring, block):
        self.ring, self.hop = ring, 0
        self.held = {1: block, -1: block}
        self.parts, self.steps = [block], [0]

    def advance(self, *tokens):
        self.hop += 1
        for way in self.ring.ways(self.hop):
            self.held[way] = self.ring.send(tie(self.held[way], *tokens), way)
            self.parts.append(self.held[way])
            self.steps.append(-way * self.hop % self.ring.count)
        return list(self.held.values())

    def finish(self):
        while self.hop < self.ring.hops[0]:
            self.advance()
        return self

    def whole(self):
        block = self.parts[0]
        rows = block.shape[0]
        found = jnp.zeros((rows * self.ring.count, block.shape[1]), block.dtype)
        starts = self.ring.places * rows
        for step, part in zip(self.steps, self.parts):
            found = lax.dynamic_update_slice(
                found, part, (starts[step], 0), allow_negative_indices=False
            )
        return found


class Reduce:
    def __init__(self, ring, whole):
        self.ring, self.source, self.hop = ring, whole, ring.hops[0]
        self.rows = whole.shape[0] // ring.count
        self.starts = ring.places * self.rows
        self.held = {way: self.piece(way * last) for way, last in zip((1, -1), ring.hops)}
        self.total = None

    def piece(self, step):
        return lax.dynamic_slice(
            self.source,
            (self.starts[step % self.ring.count], 0),
            (self.rows, self.source.shape[1]),
            allow_negative_indices=False,
        )

    def tokens(self):
        return list(self.held.values())

    def send(self, *tokens):
        self.came = {
            way: self.ring.send(tie(self.held[way], *tokens), way) for way in self.ring.ways(self.hop)
        }
        return self

    def absorb(self, *tokens):
        for way, came in self.came.items():
            came = tie(came, *tokens) if tokens else came
            if self.hop > 1:
                self.held[way] = add_low(came, self.piece(way * (self.hop - 1)))
            else:
                mine = self.piece(0) if self.total is None else self.total
                self.total = mine.astype(jnp.float32) + came.astype(jnp.float32)
        self.hop -= 1
        return self.tokens() if self.total is None else [self.total]

    def finish(self):
        while self.hop > 0:
            self.send().absorb()
        return self.total


LOW = jnp.bfloat16
F32 = jnp.float32
TILE = 256
LONG = 6
SHORT = 2
GELU_A = 0.7978845608028654
GELU_B = 0.044715
VMEM = 36 * 2**20


def mm(a, b):
    return jnp.dot(a, b, preferred_element_type=F32)


def mm_nt(a, b):
    return lax.dot_general(a, b, (((1,), (1,)), ((), ())), preferred_element_type=F32)


def mm_tn(a, b):
    return lax.dot_general(a, b, (((0,), (0,)), ((), ())), preferred_element_type=F32)


def call(body, out_shape, in_specs, out_specs, args, grid=(1,), flops=0, scratch=(), into=(), prefetch=()):
    given = len(prefetch)
    used = len(in_specs)

    def kernel(*refs):
        body(*refs[: given + used], *refs[given + used + len(into) :])

    nbytes = sum(a.size * a.dtype.itemsize for a in args)
    nbytes += sum(o.size * o.dtype.itemsize for o in jax.tree.leaves(out_shape))
    return pl.pallas_call(
        kernel,
        out_shape=out_shape,
        grid_spec=pltpu.PrefetchScalarGridSpec(
            num_scalar_prefetch=given,
            grid=grid,
            in_specs=list(in_specs) + [pl.BlockSpec(memory_space=pl.ANY)] * len(into),
            out_specs=out_specs,
            scratch_shapes=list(scratch),
        ),
        compiler_params=pltpu.CompilerParams(vmem_limit_bytes=VMEM),
        cost_estimate=pl.CostEstimate(flops=flops // 16, bytes_accessed=nbytes // 16, transcendentals=0),
        input_output_aliases={given + used + i: i for i in range(len(into))},
    )(*prefetch, *args, *into)


def held(shape):
    return pl.BlockSpec(shape, lambda *_: (0,) * len(shape), pipeline_mode=pl.Buffered(1))


def like(shape, dtype):
    return jax.ShapeDtypeStruct(shape, dtype)


def scale_of(v):
    return lax.rsqrt(jnp.mean(v * v, axis=-1, keepdims=True) + EPSILON)


def norm_pull(v, s, g, dy):
    w = dy * g
    return s * w - v * (s * s * s) * jnp.mean(w * v, axis=-1, keepdims=True)


def turn(v, cos_t, sin_t, sign):
    half = v.shape[-1] // 2
    a, b = v[:, :half], v[:, half:]
    return jnp.concatenate([a * cos_t - sign * (b * sin_t), b * cos_t + sign * (a * sin_t)], axis=-1)


def stored_block(p):
    return jnp.where(p < 4, 2 * p, 2 * (7 - p) + 1)


def padded(rows):
    return -(-rows // 16) * 16


def pack_columns(w_gate_up, dp, ctx):
    rows, wide = w_gate_up.shape
    ff = wide // 2
    step = ff // (dp * ctx)
    room = padded(step)
    part = dp * room

    def body(w, out):
        zeros = [jnp.zeros((rows, room - step), F32)] if room > step else []
        for c in range(ctx):
            for side in range(2):
                cut = []
                for d in range(dp):
                    at = side * ff + (d * ctx + c) * step
                    cut += [w[:, at : at + step]] + zeros
                out[c, :, side * part : (side + 1) * part] = jnp.concatenate(cut, axis=1).astype(LOW)

    return call(
        body,
        like((ctx, rows, 2 * part), LOW),
        [held((rows, wide))],
        held((ctx, rows, 2 * part)),
        (w_gate_up,),
    )


def unpack_columns(parts, dp, ctx, step):
    rows, wide = parts.shape[1], parts.shape[2]
    part = wide // 2
    room = part // dp
    ff = dp * ctx * step

    def body(p, out):
        for c in range(ctx):
            own = p[c].astype(F32)
            for side in range(2):
                for d in range(dp):
                    at = side * ff + (d * ctx + c) * step
                    start = side * part + d * room
                    out[:, at : at + step] = own[:, start : start + step]

    return call(
        body,
        like((rows, 2 * ff), F32),
        [held(parts.shape)],
        held((rows, 2 * ff)),
        (parts,),
    )


class Blocks:
    def __init__(self, gathered, rows=None):
        block, self.cols = gathered.parts[0].shape
        self.rows = rows = rows or block
        count = gathered.ring.count
        self.height = rows * count
        if rows % 16:
            whole = gathered.whole().reshape(count, block, self.cols)[:, :rows]
            self.parts, self.steps = [whole.reshape(self.height, self.cols)], [0]
            self.rows = self.height
        else:
            self.parts, self.steps = gathered.parts, gathered.steps

    def specs(self):
        return [pl.BlockSpec(memory_space=pl.ANY)] * len(self.parts)

    def scratch(self):
        return [
            pltpu.VMEM((self.height, self.cols), LOW),
            pltpu.SemaphoreType.DMA((len(self.parts),)),
        ]

    def load(self, places, refs, room, sems):
        @pl.when(pl.program_id(0) == 0)
        def _():
            copies = []
            for i, (step, ref) in enumerate(zip(self.steps, refs)):
                at = pl.multiple_of(places[step] * self.rows, 16) if len(refs) > 1 else 0
                copies.append(
                    pltpu.make_async_copy(
                        ref.at[pl.ds(0, self.rows), :], room.at[pl.ds(at, self.rows), :], sems.at[i]
                    )
                )
            for copy in copies:
                copy.start()
            for copy in copies:
                copy.wait()


def unpack_small(gathered, first, dp, ctx, out_rows, gain_cols, head_cols):
    block, wide = gathered.parts[0].shape
    rows = block - first
    direct = first % 16 == 0 and rows % 16 == 0
    if direct:
        parts, steps = gathered.parts, gathered.steps
    else:
        parts, steps = [gathered.whole().reshape(dp, block, wide)[:, first:]], [0]
    half = out_rows // 2
    count = len(parts)

    def body(places, *refs):
        gain, head, out, room, sems = refs[count:]
        copies = []
        for i, ref in enumerate(refs[:count]):
            if direct:
                source, target = ref.at[pl.ds(first, rows), :], room.at[places[steps[i]]]
            else:
                source, target = ref, room
            copies.append(pltpu.make_async_copy(source, target, sems.at[i]))
        for copy in copies:
            copy.start()
        for copy in copies:
            copy.wait()
        lines = []
        for d in range(dp):
            extra = room[d, : 4 * ctx, :].astype(F32)
            lines += [extra[4 * c : 4 * c + 1] for c in range(ctx)]
            at, own = d * out_rows, room[d, 4 * ctx :, :]
            out[at : at + out_rows, :wide] = own[:out_rows]
            out[at : at + half, wide:] = own[out_rows:, : D - wide]
            out[at + half : at + out_rows, wide:] = own[out_rows:, D - wide :]
        for g in range(4):
            cut = [line[:, g * gain_cols : (g + 1) * gain_cols] for line in lines]
            gain[g : g + 1, :] = jnp.concatenate(cut, axis=1)
        for g in range(2):
            at = 4 * gain_cols + g * head_cols
            cut = [line[:, at : at + head_cols] for line in lines]
            head[g : g + 1, :] = jnp.concatenate(cut, axis=1)

    return call(
        body,
        [like((4, D), F32), like((2, HD), F32), like((HD, D), LOW)],
        [pl.BlockSpec(memory_space=pl.ANY)] * count,
        [held((4, D)), held((2, HD)), held((HD, D))],
        tuple(parts),
        scratch=[pltpu.VMEM((dp, rows, wide), LOW), pltpu.SemaphoreType.DMA((count,))],
        prefetch=(gathered.ring.places,),
    )


def input_stage(x, w_in, gain, head_rows, cos_t, sin_t, row_map, places):
    seq = x.shape[0]
    count = len(w_in.parts)

    def body(_, pl_ref, x0, x1, g, hg, cos, sin, *refs):
        q, k, v, raw, n_ref, w, sems = refs[count:]
        w_in.load(pl_ref, refs[:count], w, sems)
        for i, x_ref in enumerate((x0, x1)):
            at = slice(i * TILE, (i + 1) * TILE)
            xf = x_ref[...].astype(F32)
            n = (xf * scale_of(xf) * g[...]).astype(LOW)
            n_ref[at, :] = n
            y = mm(n, w[...])
            qy, ky = y[:, :HD], y[:, HD : 2 * HD]
            raw[at, :] = y[:, : 2 * HD]
            c, s = cos[at, :], sin[at, :]
            q[at, :] = turn(qy * scale_of(qy) * hg[0:1], c, s, 1.0).astype(LOW)
            k[at, :] = turn(ky * scale_of(ky) * hg[1:2], c, s, 1.0).astype(LOW)
            v[at, :] = y[:, 2 * HD :].astype(LOW)

    def block(cols):
        return pl.BlockSpec((2 * TILE, cols), lambda p, m, s: (p, 0))

    return call(
        body,
        [like((seq, HD), LOW)] * 3 + [like((seq, 2 * HD), F32), like((seq, D), LOW)],
        [
            pl.BlockSpec((TILE, D), lambda p, m, s: (m[2 * p], 0)),
            pl.BlockSpec((TILE, D), lambda p, m, s: (m[2 * p + 1], 0)),
            held((1, D)),
            held((2, HD)),
            block(HD // 2),
            block(HD // 2),
        ]
        + w_in.specs(),
        [block(HD)] * 3 + [block(2 * HD), block(D)],
        (x, x, gain, head_rows, cos_t, sin_t, *w_in.parts),
        grid=(seq // TILE // 2,),
        flops=2 * seq * D * 3 * HD,
        scratch=w_in.scratch(),
        prefetch=(row_map, places),
    )


def scores_of(q, k, doc_step):
    s = mm_nt(q, k) * HD ** (-0.5)
    row = lax.broadcasted_iota(jnp.int32, s.shape, 0) + doc_step * TILE
    col = lax.broadcasted_iota(jnp.int32, s.shape, 1)
    return jnp.where(col <= row, s, -1e30)


def attention(q, k, v, base):
    seq = q.shape[0]

    def body(b, q_ref, k_ref, v_ref, mixed, lse):
        for doc, count in enumerate((LONG, SHORT)):
            first = b[doc]
            for i in range(count):
                p = first + i
                at = pl.ds(pl.multiple_of(p * TILE, TILE), TILE)
                keys = pl.ds(pl.multiple_of(first * TILE, TILE), (i + 1) * TILE)
                s = scores_of(q_ref[at, :], k_ref[keys, :], i)
                peak = jnp.max(s, axis=-1, keepdims=True)
                e = jnp.exp(s - peak)
                total = jnp.sum(e, axis=-1, keepdims=True)
                lse[at, :] = peak + jnp.log(total)
                probs = (e * (1.0 / total)).astype(LOW)
                to = pl.ds(pl.multiple_of(stored_block(p) * TILE, TILE), TILE)
                mixed[to, :] = mm(probs, v_ref[keys, :]).astype(LOW)

    return call(
        body,
        [like((seq, HD), LOW), like((seq, 1), F32)],
        [held((seq, HD))] * 3,
        [held((seq, HD)), held((seq, 1))],
        (q, k, v),
        flops=4 * 24 * TILE * TILE * HD,
        prefetch=(base,),
    )


def attention_back(q, k, v, raw, lse, grads, head_rows, cos_t, sin_t, base):
    seq = q.shape[0]
    chip = seq // 2

    def pull_head(v_raw, g, dy, cos, sin):
        dy = turn(dy, cos, sin, -1.0)
        s = scale_of(v_raw)
        return norm_pull(v_raw, s, g, dy), jnp.sum(dy * v_raw * s, axis=0, keepdims=True)

    def body(b, q_ref, k_ref, v_ref, raw_ref, l_ref, *refs):
        hg, cos, sin, out, head_out, dk, dv, mixed_grad = refs[6:]
        for i in range(2):
            mine, near, far = refs[3 * i : 3 * i + 3]
            rows = pl.ds(pl.multiple_of((b[2] if i == 0 else 1 - b[2]) * chip, chip), chip)
            mixed_grad[rows, :] = (
                mine[0].astype(F32) + near[0].astype(F32) + far[...].astype(F32)
            ).astype(LOW)
        dk[...] = jnp.zeros_like(dk)
        dv[...] = jnp.zeros_like(dv)
        head_q = jnp.zeros((1, HD), F32)
        for doc, count in enumerate((LONG, SHORT)):
            first = b[doc]
            for i in range(count):
                p = first + i
                at = pl.ds(pl.multiple_of(p * TILE, TILE), TILE)
                keys = pl.ds(pl.multiple_of(first * TILE, TILE), (i + 1) * TILE)
                src = pl.ds(pl.multiple_of(stored_block(p) * TILE, TILE), TILE)
                do = mixed_grad[src, :]
                qs = q_ref[at, :]
                probs = jnp.exp(scores_of(qs, k_ref[keys, :], i) - l_ref[at, :])
                dp = mm_nt(do, v_ref[keys, :])
                inner = jnp.sum(probs * dp, axis=-1, keepdims=True)
                ds = (probs * (dp - inner)).astype(LOW)
                dq = mm(ds, k_ref[keys, :]) * HD ** (-0.5)
                dk[keys, :] += mm_tn(ds, qs)
                dv[keys, :] += mm_tn(probs.astype(LOW), do)
                dq, part = pull_head(raw_ref[at, :HD], hg[0:1], dq, cos[at, :], sin[at, :])
                head_q += part
                out[at, :HD] = dq.astype(LOW)
        head_k = jnp.zeros((1, HD), F32)
        for p in range(seq // TILE):
            at = slice(p * TILE, (p + 1) * TILE)
            dkp, part = pull_head(
                raw_ref[at, HD:], hg[1:2], dk[at, :] * HD ** (-0.5), cos[at, :], sin[at, :]
            )
            head_k += part
            out[at, HD : 2 * HD] = dkp.astype(LOW)
            out[at, 2 * HD :] = dv[at, :].astype(LOW)
        head_out[0:1, :] = head_q
        head_out[1:2, :] = head_k

    pair = pl.BlockSpec((1, chip, HD), lambda *_: (0, 0, 0), pipeline_mode=pl.Buffered(1))
    return call(
        body,
        [like((seq, 3 * HD), LOW), like((2, HD), F32)],
        [held((seq, HD))] * 3
        + [held((seq, 2 * HD)), held((seq, 1))]
        + [pair, pair, held((chip, HD))] * 2
        + [held((2, HD))]
        + [held((seq, HD // 2))] * 2,
        [held((seq, 3 * HD)), held((2, HD))],
        (q, k, v, raw, lse, *grads, head_rows, cos_t, sin_t),
        flops=10 * 24 * TILE * TILE * HD,
        scratch=[pltpu.VMEM((seq, HD), F32)] * 2 + [pltpu.VMEM((seq, HD), LOW)],
        prefetch=(base,),
    )


def project(mixed, outs, x, gains, stored_map):
    seq = x.shape[0]

    def body(_, m0, m1, m2, m3, w0, w1, w2, w3, x_ref, g, proj, pre):
        for i in range(2):
            at = slice(i * TILE, (i + 1) * TILE)
            y = mm(m0[at, :], w0[...]) + mm(m1[at, :], w1[...])
            y = y + mm(m2[at, :], w2[...]) + mm(m3[at, :], w3[...])
            proj[at, :] = y
            r = x_ref[at, :].astype(F32) + y * scale_of(y) * g[1:2]
            pre[at, :] = (r * scale_of(r) * g[2:3]).astype(LOW)

    def block(cols):
        return pl.BlockSpec((2 * TILE, cols), lambda r, m: (r, 0))

    return call(
        body,
        [like((seq, D), F32), like((seq, D), LOW)],
        [pl.BlockSpec((2 * TILE, HD), lambda r, m: (m[2 * r] // 2, 0))] * 4
        + [held((HD, D))] * 4
        + [block(D), held((4, D))],
        [block(D), block(D)],
        (*mixed, *outs, x, gains),
        grid=(seq // TILE // 2,),
        flops=2 * seq * D * H * HD,
        prefetch=(stored_map,),
    )


def column_cuts(main, width):
    return [(at, min(width, main - at)) for at in range(0, main, width)]


def gate_stage(pre, w, places, half, into=()):
    seq, part = pre.shape[0], w.cols // 2
    rows = 512
    first = half * (seq // 2 // rows)
    count = len(w.parts)

    def pieces(g, u):
        t = jnp.tanh(GELU_A * (g + GELU_B * (g * g * g)))
        a = 0.5 * g * (1.0 + t)
        slope = 0.5 * (1.0 + t) + (0.5 * g) * (1.0 - t * t) * (GELU_A * (1.0 + 3.0 * GELU_B * (g * g)))
        return a * u, u * slope, a

    def body(pl_ref, p_ref, *refs):
        hidden, ab, room, sems = refs[count:]
        w.load(pl_ref, refs[:count], room, sems)
        p = p_ref[...]

        def multiply(at, wide):
            return mm(p, room[:, at : at + wide]), mm(p, room[:, part + at : part + at + wide])

        def finish(at, wide, made):
            h, b, a = pieces(*made)
            hidden[:, at : at + wide] = h.astype(LOW)
            ab[:, at : at + wide] = b.astype(LOW)
            ab[:, part + at : part + at + wide] = a.astype(LOW)

        last = None
        for cut in column_cuts(part, 256):
            made = multiply(*cut)
            if last is not None:
                finish(*last)
            last = (*cut, made)
        finish(*last)

    def block(cols):
        return pl.BlockSpec((rows, cols), lambda r, m: (first + r, 0))

    return call(
        body,
        [like((seq, part), LOW), like((seq, 2 * part), LOW)],
        [block(D)] + w.specs(),
        [block(part), block(2 * part)],
        (pre, *w.parts),
        grid=(seq // 2 // rows,),
        flops=2 * seq * D * part,
        scratch=w.scratch(),
        into=into,
        prefetch=(places,),
    )


def down_stage(hidden, w, places, half):
    seq, part = hidden.shape
    rows = seq // 4
    count = len(w.parts)

    def body(pl_ref, h, *refs):
        even, odd, room, sems = refs[count:]
        w.load(pl_ref, refs[:count], room, sems)
        odd[...] = mm(h[rows:, :], room[...]).astype(LOW)
        even[...] = mm(h[:rows, :], room[...]).astype(LOW)

    return call(
        body,
        [like((rows, D), LOW)] * 2,
        [
            pl.BlockSpec(
                (2 * rows, part), lambda r, m: (half, 0), pipeline_mode=pl.Buffered(1)
            )
        ]
        + w.specs(),
        [held((rows, D))] * 2,
        (hidden, *w.parts),
        flops=4 * rows * D * part,
        scratch=w.scratch(),
        prefetch=(places,),
    )


def ffn_stage(parts, near, far, proj, x, cot, gains):
    rows = cot.shape[0]

    def body(p, n, f, proj_ref, x_ref, c_ref, g, out, grad, gain):
        y = p[...].astype(F32) + n[...].astype(F32) + f[...].astype(F32)
        pr = proj_ref[...]
        s = scale_of(y)
        r = x_ref[...].astype(F32) + pr * scale_of(pr) * g[1:2]
        out[...] = (r + y * s * g[3:4]).astype(LOW)
        dy = c_ref[...].astype(F32)
        grad[...] = norm_pull(y, s, g[3:4], dy).astype(LOW)
        part = jnp.sum(dy * y * s, axis=0, keepdims=True)

        @pl.when(pl.program_id(0) == 0)
        def _():
            gain[...] = part

        @pl.when(pl.program_id(0) > 0)
        def _():
            gain[...] += part

    block = pl.BlockSpec((TILE, D), lambda r: (r, 0))
    return call(
        body,
        [like((rows, D), LOW), like((rows, D), LOW), like((1, D), F32)],
        [block] * 6 + [held((4, D))],
        [block, block, held((1, D))],
        (parts, near, far, proj, x, cot, gains),
        grid=(rows // TILE,),
    )


def hidden_back(grad, w, ab, places, half, into=()):
    seq, part = ab.shape[0], ab.shape[1] // 2
    rows = 512
    first = half * (seq // 2 // rows)
    count = len(w.parts)

    def body(pl_ref, g_ref, ab_ref, *refs):
        out, room, sems = refs[count:]
        w.load(pl_ref, refs[:count], room, sems)
        g = g_ref[...]
        for at, wide in column_cuts(part, 256):
            hg = mm_nt(g, room[at : at + wide, :])
            for side in (at, part + at):
                out[:, side : side + wide] = (hg * ab_ref[:, side : side + wide].astype(F32)).astype(LOW)

    def block(cols):
        return pl.BlockSpec((rows, cols), lambda r, m: (first + r, 0))

    return call(
        body,
        [like((seq, 2 * part), LOW)],
        [pl.BlockSpec((rows, D), lambda r, m: (r, 0)), block(2 * part)] + w.specs(),
        [block(2 * part)],
        (grad, ab, *w.parts),
        grid=(seq // 2 // rows,),
        flops=seq * D * part,
        scratch=w.scratch(),
        into=into,
        prefetch=(places,),
    )[0]


def residual_back(gu, w, outs, proj, x, cot, gains, stored_map, places, half, into=()):
    seq, wide = gu.shape
    own = cot.shape[0] // TILE
    steps = seq // 2 // TILE
    first = half * steps
    count = len(w.parts)

    def body(_, pl_ref, gu_ref, w0, w1, w2, w3, proj_ref, x_ref, c_ref, g, *refs):
        rg, pg, even, odd, gain, room, sems, *made = refs[count:]
        w.load(pl_ref, refs[:count], room, sems)
        step = pl.program_id(0)

        def multiply(turn):
            made[turn][...] = mm_nt(gu_ref[...], room[...])

        def finish(turn):
            dy = made[turn][...]
            pr = proj_ref[...]
            sp = scale_of(pr)
            r = x_ref[...].astype(F32) + pr * sp * g[1:2]
            s = scale_of(r)
            dr = norm_pull(r, s, g[2:3], dy)
            if half == 0:
                dr = dr + jnp.where(step <= own, 1.0, 0.0) * c_ref[...].astype(F32)
            rg[...] = dr.astype(LOW)
            low = norm_pull(pr, sp, g[1:2], dr).astype(LOW)
            pg[...] = low
            even[0] = mm_nt(low, w0[...]).astype(LOW)
            odd[0] = mm_nt(low, w1[...]).astype(LOW)
            even[1] = mm_nt(low, w2[...]).astype(LOW)
            odd[1] = mm_nt(low, w3[...]).astype(LOW)
            before = jnp.where(step == 1, 0.0, gain[...])
            gain[0:1, :] = before[0:1] + jnp.sum(dr * pr * sp, axis=0, keepdims=True)
            gain[1:2, :] = before[1:2] + jnp.sum(dy * r * s, axis=0, keepdims=True)

        @pl.when(step == 0)
        def _():
            multiply(0)

        for turn in range(2):

            @pl.when((step > 0) & (step < steps) & (step % 2 == turn))
            def _():
                multiply(turn)
                finish(1 - turn)

        @pl.when(step == steps)
        def _():
            finish((steps - 1) % 2)

    def last(i):
        return jnp.maximum(i - 1, 0)

    def block(cols):
        return pl.BlockSpec((TILE, cols), lambda i, m, p: (first + last(i), 0))

    heads = pl.BlockSpec((2, TILE, HD), lambda i, m, p: (0, m[first + last(i)] % steps, 0))
    return call(
        body,
        [like((seq, D), LOW), like((seq, D), LOW)]
        + [like((2, seq // 2, HD), LOW)] * 2
        + [like((2, D), F32)],
        [pl.BlockSpec((TILE, wide), lambda i, m, p: (first + jnp.minimum(i, steps - 1), 0))]
        + [held((HD, D))] * 4
        + [block(D), block(D)]
        + [pl.BlockSpec((TILE, D), lambda i, m, p: (jnp.minimum(last(i), own - 1), 0)), held((4, D))]
        + w.specs(),
        [
            block(D),
            pl.BlockSpec((TILE, D), lambda i, m, p: (m[first + last(i)], 0)),
            heads,
            heads,
            held((2, D)),
        ],
        (gu, *outs, proj, x, cot, gains, *w.parts),
        grid=(steps + 1,),
        flops=seq * D * (wide + H * HD),
        scratch=w.scratch() + [pltpu.VMEM((TILE, D), F32)] * 2,
        into=into,
        prefetch=(stored_map, places),
    )


def input_back(qkv, w_in, x, rg, gain, pos_map, places):
    seq = x.shape[0]
    rows = 2 * TILE
    count = len(w_in.parts)

    def body(_, pl_ref, q0, q1, x_ref, rg_ref, g, *refs):
        even, odd, gain_out, w, sems = refs[count:]
        w_in.load(pl_ref, refs[:count], w, sems)
        step = pl.program_id(0)
        total = jnp.zeros((1, D), F32)
        made = []
        for i, q_ref in enumerate((q0, q1)):
            at = slice(i * TILE, (i + 1) * TILE)
            dy = mm_nt(q_ref[...], w[...])
            xf = x_ref[at, :].astype(F32)
            s = scale_of(xf)
            made.append((rg_ref[at, :].astype(F32) + norm_pull(xf, s, g[...], dy)).astype(LOW))
            total += jnp.sum(dy * xf * s, axis=0, keepdims=True)
        gain_out[...] = jnp.where(step == 0, 0.0, gain_out[...]) + total

        @pl.when(step % 2 == 0)
        def _():
            even[:TILE, :], even[TILE:, :] = made

        @pl.when(step % 2 == 1)
        def _():
            odd[:TILE, :], odd[TILE:, :] = made

    block = pl.BlockSpec((rows, D), lambda i, m, s: (i, 0))
    out = pl.BlockSpec((rows, D), lambda i, m, s: (i // 2, 0))
    return call(
        body,
        [like((seq // 2, D), LOW)] * 2 + [like((1, D), F32)],
        [
            pl.BlockSpec((TILE, 3 * HD), lambda i, m, s: (m[2 * i], 0)),
            pl.BlockSpec((TILE, 3 * HD), lambda i, m, s: (m[2 * i + 1], 0)),
            block,
            block,
            held((1, D)),
        ]
        + w_in.specs(),
        [out, out, held((1, D))],
        (qkv, qkv, x, rg, gain, *w_in.parts),
        grid=(seq // rows,),
        flops=2 * seq * D * 3 * HD,
        scratch=w_in.scratch(),
        prefetch=(pos_map, places),
    )


def local(
    tokens,
    cotangent,
    lengths,
    w_qkv,
    w_out,
    w_gate_up,
    w_down,
    gains,
    head_gains,
    first_qkv,
    first_out,
    first_gate_up,
    first_down,
    first_gains,
    first_head,
    second_qkv,
    second_out,
    second_gate_up,
    second_down,
    second_gains,
    second_head,
):
    low = jnp.bfloat16
    f32 = jnp.float32
    rows = tokens.shape[1]
    dp = lax.axis_size("dp")
    ctx = lax.axis_size("ctx")
    place = lax.axis_index("ctx")
    seq = rows * ctx
    in_rows = w_qkv.shape[0]
    out_rows = w_out.shape[0]
    ff_rows = w_down.shape[0]
    gain_cols = gains.shape[1]
    head_cols = head_gains.shape[1]
    qkv_cols = 3 * HD
    ring = Ring()

    q_cols = w_qkv[:, : H * HD].astype(low).reshape(in_rows, ctx, HD).transpose(1, 0, 2)
    kv_cols = jnp.broadcast_to(w_qkv[:, H * HD :].astype(low)[None], (ctx, in_rows, 2 * HD))
    extra = jnp.concatenate(
        [gains.astype(low).reshape(-1), head_gains.astype(low).reshape(-1)]
    )
    extra = jnp.pad(extra, (0, 4 * qkv_cols - extra.shape[0])).reshape(4, qkv_cols)
    small_sent = jnp.concatenate(
        [
            jnp.concatenate([q_cols, kv_cols], axis=2),
            jnp.broadcast_to(extra[None], (ctx, 4, qkv_cols)),
        ],
        axis=1,
    )
    to_user = [((dp * c + d), d * ctx + c) for d in range(dp) for c in range(ctx)]
    to_owner = [(b, a) for a, b in to_user]
    out_mine = lax.ppermute(w_out.astype(low), ("dp", "ctx"), to_user)
    half = out_rows // 2
    small = exchange(small_sent, "ctx")
    packed = pack_columns(tie(w_gate_up, small_sent), dp, ctx)
    own_rows = ctx * in_rows
    small_ring = Gather(
        ring,
        jnp.concatenate(
            [
                small[:, :in_rows].reshape(own_rows, qkv_cols),
                small[:, in_rows:].reshape(4 * ctx, qkv_cols),
                out_mine[:, :qkv_cols],
                jnp.concatenate([out_mine[:half, qkv_cols:], out_mine[half:, qkv_cols:]], axis=1),
            ]
        ),
    )
    down_block = jnp.pad(w_down.astype(low), ((0, padded(ff_rows) - ff_rows), (0, 0)))
    down_ring = Gather(ring, down_block)
    down_first = down_ring.advance()
    tokens_far = swap(tie(tokens[0], small), 2)
    tokens_near = swap(tie(tokens[0], small), 1)
    gate_up_cols = exchange(tie(packed, tokens_far), "ctx").reshape(own_rows, -1)
    first_len = lengths[0, 0]
    pos = tie(jnp.arange(seq, dtype=jnp.int32), packed)
    cos_t, sin_t = rope_tables(pos - jnp.where(pos < first_len, 0, first_len), HD)
    small_ring.advance(*down_first)
    small_ring.advance(cos_t, sin_t)
    tokens_last = swap(tie(tokens_far, *small_ring.held.values()), 1)
    tokens_all = jnp.concatenate([tokens[0], tokens_near, tokens_far, tokens_last])
    while small_ring.hop < ring.hops[0]:
        small_ring.advance()
    small_seen = list(small_ring.held.values())
    gate_ring = Gather(ring, gate_up_cols)
    gate_seen = gate_ring.advance(*small_seen, tokens_last)
    w_in = Blocks(small_ring, own_rows)
    places = ring.places
    gain_rows, head_rows, out_mine = unpack_small(
        small_ring, own_rows, dp, ctx, out_rows, gain_cols, head_cols
    )
    out_far, out_near = swap(out_mine, 2), swap(out_mine, 1)

    blocks = seq // TILE
    split = first_len // TILE
    base = jnp.where(split == LONG, jnp.array([0, LONG, 0]), jnp.array([SHORT, 0, 0]))
    base = (base + jnp.array([0, 0, 1]) * (place // 2)).astype(jnp.int32)
    tiles = jnp.arange(blocks, dtype=jnp.int32)
    stored_map = 2 * (place ^ (tiles // 2)) + tiles % 2
    owner = jnp.where(tiles < ctx, tiles, 2 * ctx - 1 - tiles)
    row_map = 2 * (place ^ owner) + (tiles >= ctx)
    pos_map = jnp.where(tiles % 2 == 0, stored_map // 2, 2 * ctx - 1 - stored_map // 2)

    q, k, v, raw, normed = input_stage(
        tokens_all, w_in, gain_rows[0:1], head_rows, cos_t, sin_t, row_map, places
    )
    down_second = down_ring.advance(q, *gate_seen)
    gate_second = gate_ring.advance(q)
    mixed, lse = attention(tie(q, *gate_seen, out_far, out_near), k, v, base)
    mixed = tie(mixed, *down_second)
    mixed_far, mixed_near = swap(mixed, 2), swap(mixed, 1)
    out_parts = [out_mine, out_near, out_far, swap(tie(out_far, mixed), 1)]
    down_ring.advance(mixed)
    gate_ring.advance(mixed)
    mixed_parts = [mixed, mixed_near, mixed_far, swap(tie(mixed_far, *gate_second), 1)]
    proj, pre_low = project(mixed_parts, out_parts, tokens_all, gain_rows, stored_map)
    while gate_ring.hop < ring.hops[0]:
        gate_ring.advance(pre_low)
        if down_ring.hop < ring.hops[0]:
            down_ring.advance(pre_low)
    down_ring.finish()
    full_gate_up = Blocks(gate_ring)
    full_down = Blocks(down_ring)
    buffers = gate_stage(pre_low, full_gate_up, places, 1)
    even, odd = down_stage(buffers[0], full_down, places, 1)
    summed = add_low(even, swap(odd, 1))
    far = swap(summed, 2)
    hidden_low, slopes = gate_stage(tie(pre_low, summed), full_gate_up, places, 0, buffers)
    even, odd = down_stage(tie(hidden_low, far), full_down, places, 0)
    near = swap(odd, 1)
    result, ffn_grad, gain_grad_d = ffn_stage(
        even, near, far, proj, tokens[0], cotangent[0], gain_rows
    )

    far = swap(ffn_grad, 2)
    ffn_here = jnp.concatenate([ffn_grad, swap(ffn_grad, 1)])
    residual = partial(
        residual_back,
        w=full_gate_up,
        outs=out_parts,
        proj=proj,
        x=tokens_all,
        cot=cotangent[0],
        gains=gain_rows,
        stored_map=stored_map,
        places=places,
    )
    gate_up_low = hidden_back(ffn_here, full_down, slopes, places, 0)
    far = tie(far, gate_up_low)
    ffn_there = jnp.concatenate([far, swap(far, 1)])
    gate_up_low = hidden_back(ffn_there, full_down, slopes, places, 1, (gate_up_low,))
    grad_gate_up = mm_tn(pre_low, gate_up_low).astype(low)
    gate_sum = Reduce(ring, grad_gate_up).send()
    resid_grad, proj_low, even, odd, gain_grad_here = residual(
        tie(gate_up_low, *gate_sum.tokens()), half=0
    )
    held_gate = gate_sum.absorb(resid_grad)
    near = swap(tie(odd, *held_gate), 1)
    parts_here = (even, near)
    summed = add_low(even[1], near[1])
    far_there = swap(summed, 2)
    gate_sum.send()
    ffn_low = jnp.concatenate([ffn_here, ffn_there])
    grad_down = mm_tn(hidden_low, tie(ffn_low, summed, *held_gate)).astype(low)
    down_sum = Reduce(ring, grad_down).send()
    resid_grad, proj_low, even, odd, gain_grad_there = residual(
        tie(gate_up_low, far_there, *down_sum.tokens()), half=1, into=(resid_grad, proj_low)
    )
    near = swap(tie(odd, *gate_sum.came.values(), *down_sum.came.values()), 1)
    summed = add_low(even[1], near[1])
    far_here = swap(summed, 2)
    held_gate = gate_sum.absorb(odd)
    held_down = down_sum.absorb(odd)
    gate_sum.send()
    down_sum.send()
    proj_low = tie(proj_low, *held_gate, *held_down)
    grad_out = [mm_tn(m, proj_low).astype(low) for m in mixed_parts]
    far_here = tie(far_here, *grad_out)
    grad_out = reduce_ctx(grad_out).astype(low)
    qkv_low, head_grads = attention_back(
        q,
        k,
        v,
        raw,
        lse,
        parts_here + (far_here,) + (even, near, far_there),
        head_rows,
        cos_t,
        sin_t,
        base,
    )
    grad_in = mm_tn(normed, qkv_low).astype(low)
    grad_out = grad_out.reshape(dp, out_rows, D)
    in_blocks = jnp.concatenate(
        [
            grad_in.reshape(dp, own_rows, qkv_cols),
            grad_out[:, :, :qkv_cols],
            jnp.concatenate(
                [grad_out[:, :half, qkv_cols:], grad_out[:, half:, qkv_cols:]], axis=2
            ),
        ],
        axis=1,
    )
    in_sum = Reduce(ring, in_blocks.reshape(-1, qkv_cols))
    held_gate = gate_sum.absorb(*in_sum.tokens())
    held_down = down_sum.absorb(*in_sum.tokens())
    in_sum.send()
    gate_sum.send()
    down_sum.send()
    held_in = in_sum.absorb(*held_gate, *held_down)
    in_sum.send()
    input_even, input_odd, gain_grad_a = input_back(
        tie(qkv_low, *held_in),
        w_in,
        tokens_all,
        resid_grad,
        gain_rows[0:1],
        pos_map,
        places,
    )
    held_in = in_sum.absorb(input_odd)
    in_sum.send()
    gate_came = list(gate_sum.came.values())
    gate_sum.absorb(input_odd)
    down_sum.absorb(*held_in)
    gate_up_own = gate_sum.finish().astype(low)
    gate_up_own = exchange(gate_up_own.reshape(ctx, in_rows, -1), "ctx")
    near = swap(tie(input_odd, *gate_came), 1)
    summed = add_low(input_even[rows:], near[rows:])
    gain_grad_bc = gain_grad_here + gain_grad_there
    while in_sum.hop > 1:
        in_sum.absorb()
        in_sum.send()
    held_in = in_sum.tokens()

    in_own = in_sum.absorb()[0].astype(low)
    down_sum.send(*held_in)
    down_sum.absorb(in_own)
    down_own = down_sum.finish()[:ff_rows]
    gate_up_own = unpack_columns(gate_up_own, dp, ctx, ff_rows)
    out_own = in_own[own_rows:]
    out_own = jnp.concatenate(
        [
            out_own[:out_rows],
            jnp.concatenate(
                [out_own[out_rows:, : D - qkv_cols], out_own[out_rows:, D - qkv_cols :]], axis=0
            ),
        ],
        axis=1,
    )
    out_own = lax.ppermute(out_own, ("dp", "ctx"), to_owner).astype(f32)
    in_own = exchange(in_own[:own_rows].reshape(ctx, in_rows, qkv_cols), "ctx").astype(f32)
    qkv_own = jnp.concatenate(
        [
            in_own[:, :, :HD].transpose(1, 0, 2).reshape(in_rows, H * HD),
            jnp.sum(in_own[:, :, HD:], axis=0),
        ],
        axis=1,
    )
    gain_grads = jnp.concatenate([gain_grad_a, gain_grad_bc, gain_grad_d], axis=0)
    local_squares = jnp.float32(0.0)
    for piece in (qkv_own, out_own, gate_up_own, down_own):
        local_squares = local_squares + jnp.sum(piece * piece)
    lines = jnp.concatenate([gain_grads.reshape(-1, 128), head_grads.reshape(-1, 128)])
    squares = jnp.pad(local_squares.reshape(1, 1), ((0, 7), (0, 127)))
    sums = tie(jnp.concatenate([lines, squares]), summed)
    sums = sums + swap(sums, 2)
    far = swap(tie(summed, sums), 2)
    input_grad = (
        input_even[:rows].astype(f32) + near[:rows].astype(f32) + far.astype(f32)
    )
    sums = sum_rest(sums)
    small_grads = sums[: lines.shape[0]]
    index = lax.axis_index("dp") * ctx + place
    gains_own = lax.dynamic_slice_in_dim(
        small_grads[: 4 * D // 128].reshape(4, D), index * gain_cols, gain_cols, axis=1
    )
    head_own = lax.dynamic_slice_in_dim(
        small_grads[4 * D // 128 :].reshape(2, HD), index * head_cols, head_cols, axis=1
    )
    reduced = (qkv_own, out_own, gate_up_own, down_own, gains_own, head_own)
    total_squares = sums[lines.shape[0], 0] + jnp.sum(small_grads * small_grads)
    grad_norm = jnp.sqrt(total_squares)
    factor = 1.0 / jnp.maximum(grad_norm, 1.0)
    weights = (w_qkv, w_out, w_gate_up, w_down, gains, head_gains)
    firsts = (first_qkv, first_out, first_gate_up, first_down, first_gains, first_head)
    seconds = (second_qkv, second_out, second_gate_up, second_down, second_gains, second_head)
    rates = (D ** (-0.5), (H * HD) ** (-0.5), D ** (-0.5), FF ** (-0.5), GAIN_RATE, GAIN_RATE)
    decays = (WEIGHT_DECAY, WEIGHT_DECAY, WEIGHT_DECAY, WEIGHT_DECAY, 0.0, 0.0)
    reduced = reduced[:2] + (tie(gate_up_own, far, grad_norm), tie(down_own, far, grad_norm)) + reduced[4:]
    updates = [
        adam_update(
            weights[index],
            firsts[index],
            seconds[index],
            reduced[index] * factor,
            rates[index],
            decays[index],
        )
        for index in range(6)
    ]
    return (
        result[None],
        input_grad[None],
        updates[0][0],
        updates[1][0],
        updates[2][0],
        updates[3][0],
        updates[4][0],
        updates[5][0],
        updates[0][1],
        updates[1][1],
        updates[2][1],
        updates[3][1],
        updates[4][1],
        updates[5][1],
        updates[0][2],
        updates[1][2],
        updates[2][2],
        updates[3][2],
        updates[4][2],
        updates[5][2],
        grad_norm,
    )


def solution(mesh):
    in_specs = (
        P("dp", "ctx", None),
        P("dp", "ctx", None),
        P("dp", None),
        P(("dp", "ctx"), None),
        P(("dp", "ctx"), None),
        P(("dp", "ctx"), None),
        P(("dp", "ctx"), None),
        P(None, ("dp", "ctx")),
        P(None, ("dp", "ctx")),
        P(("dp", "ctx"), None),
        P(("dp", "ctx"), None),
        P(("dp", "ctx"), None),
        P(("dp", "ctx"), None),
        P(None, ("dp", "ctx")),
        P(None, ("dp", "ctx")),
        P(("dp", "ctx"), None),
        P(("dp", "ctx"), None),
        P(("dp", "ctx"), None),
        P(("dp", "ctx"), None),
        P(None, ("dp", "ctx")),
        P(None, ("dp", "ctx")),
    )
    out_specs = (
        P("dp", "ctx", None),
        P("dp", "ctx", None),
        P(("dp", "ctx"), None),
        P(("dp", "ctx"), None),
        P(("dp", "ctx"), None),
        P(("dp", "ctx"), None),
        P(None, ("dp", "ctx")),
        P(None, ("dp", "ctx")),
        P(("dp", "ctx"), None),
        P(("dp", "ctx"), None),
        P(("dp", "ctx"), None),
        P(("dp", "ctx"), None),
        P(None, ("dp", "ctx")),
        P(None, ("dp", "ctx")),
        P(("dp", "ctx"), None),
        P(("dp", "ctx"), None),
        P(("dp", "ctx"), None),
        P(("dp", "ctx"), None),
        P(None, ("dp", "ctx")),
        P(None, ("dp", "ctx")),
        P(),
    )
    return jax.shard_map(local, mesh=mesh, in_specs=in_specs, out_specs=out_specs, check_vma=False)
```

```python
from functools import partial

import jax
import jax.numpy as jnp
from jax import lax
from jax.experimental import pallas as pl
from jax.experimental.pallas import tpu as pltpu
from jax.sharding import PartitionSpec as P

D = 1152
H = 4
HD = 256
FF = 6912
STEP = 10

EPSILON = 1e-06
ROPE_BASE = 1000000.0
BETA_ONE = 0.9
BETA_TWO = 0.95
ADAM_EPSILON = 1e-08
WEIGHT_DECAY = 0.1
GAIN_RATE = 1.0


def rope_tables(offsets, width):
    half = width // 2
    freq = jnp.exp(-jnp.log(ROPE_BASE) * jnp.arange(half, dtype=jnp.float32) * (2.0 / width))
    angle = offsets.astype(jnp.float32)[:, None] * freq[None, :]
    return (jnp.cos(angle), jnp.sin(angle))


def adam_update(weight, first, second, grad, rate, decay):
    first_new = BETA_ONE * first + (1.0 - BETA_ONE) * grad
    second_new = BETA_TWO * second + (1.0 - BETA_TWO) * grad * grad
    first_hat = first_new / (1.0 - BETA_ONE**STEP)
    second_hat = second_new / (1.0 - BETA_TWO**STEP)
    updated = weight - rate * (first_hat / (jnp.sqrt(second_hat) + ADAM_EPSILON) + decay * weight)
    return (updated, first_new, second_new)


def exchange(parts, axis):
    return lax.all_to_all(parts, axis, split_axis=0, concat_axis=0, tiled=True)


def swap(value, bit):
    count = lax.axis_size("ctx")
    return lax.ppermute(value, "ctx", [(i, i ^ bit) for i in range(count)])


def swap_dp(value, bit):
    count = lax.axis_size("dp")
    return lax.ppermute(value, "dp", [(i, i ^ bit) for i in range(count)])


def gather_ctx(block):
    far = swap(block, 2)
    return [block, swap(block, 1), far, swap(far, 1)]


def add_low(a, b):
    return a + b


def reduce_ctx(blocks):
    near, far = jnp.concatenate([blocks[1], blocks[3]]), None
    near = swap(near, 1)
    size = blocks[0].shape[0]
    far = swap(add_low(blocks[2], near[size:]), 2)
    mine = blocks[0].astype(jnp.float32) + near[:size].astype(jnp.float32)
    return mine + far.astype(jnp.float32)


def reorder(value, bit, rows):
    parts = [value[j * rows : (j + 1) * rows] for j in range(value.shape[0] // rows)]
    return jnp.concatenate([parts[j ^ bit] for j in range(len(parts))])


def sum_rest(value):
    value = value + swap(value, 1)
    bit = 1
    while bit < lax.axis_size("dp"):
        value = value + swap_dp(value, bit)
        bit *= 2
    return value


def tie(value, *tokens):
    return lax.optimization_barrier((value, *tokens))[0]


class Ring:
    def __init__(self):
        count = self.count = lax.axis_size("dp")
        self.ctx = lax.axis_size("ctx")
        self.order = list(range(0, count, 2)) + list(range(count - 1, 0, -2))
        self.hops = (count // 2, count - 1 - count // 2)
        table = [
            [self.order[(self.order.index(i) + sense * step) % count] for step in range(count)]
            for sense in (1, -1)
            for i in range(count)
        ]
        row = (lax.axis_index("ctx") % 2) * count + lax.axis_index("dp")
        self.places = lax.dynamic_slice(
            jnp.array(table, jnp.int32), (row, 0), (1, count), allow_negative_indices=False
        )[0]

    def send(self, value, way):
        pairs = []
        for place, source in enumerate(self.order):
            for c in range(self.ctx):
                target = self.order[(place + (way if c % 2 == 0 else -way)) % self.count]
                pairs.append((source * self.ctx + c, target * self.ctx + c))
        return lax.ppermute(value, ("dp", "ctx"), pairs)

    def ways(self, hop):
        return [way for way, last in zip((1, -1), self.hops) if hop <= last]


class Gather:
    def __init__(self, ring, block):
        self.ring, self.hop = ring, 0
        self.held = {1: block, -1: block}
        self.parts, self.steps = [block], [0]

    def advance(self, *tokens):
        self.hop += 1
        for way in self.ring.ways(self.hop):
            self.held[way] = self.ring.send(tie(self.held[way], *tokens), way)
            self.parts.append(self.held[way])
            self.steps.append(-way * self.hop % self.ring.count)
        return list(self.held.values())

    def finish(self):
        while self.hop < self.ring.hops[0]:
            self.advance()
        return self

    def whole(self):
        block = self.parts[0]
        rows = block.shape[0]
        found = jnp.zeros((rows * self.ring.count, block.shape[1]), block.dtype)
        starts = self.ring.places * rows
        for step, part in zip(self.steps, self.parts):
            found = lax.dynamic_update_slice(
                found, part, (starts[step], 0), allow_negative_indices=False
            )
        return found


class Reduce:
    def __init__(self, ring, whole):
        self.ring, self.source, self.hop = ring, whole, ring.hops[0]
        self.rows = whole.shape[0] // ring.count
        self.starts = ring.places * self.rows
        self.held = {way: self.piece(way * last) for way, last in zip((1, -1), ring.hops)}
        self.total = None

    def piece(self, step):
        return lax.dynamic_slice(
            self.source,
            (self.starts[step % self.ring.count], 0),
            (self.rows, self.source.shape[1]),
            allow_negative_indices=False,
        )

    def tokens(self):
        return list(self.held.values())

    def send(self, *tokens):
        self.came = {
            way: self.ring.send(tie(self.held[way], *tokens), way) for way in self.ring.ways(self.hop)
        }
        return self

    def absorb(self, *tokens):
        for way, came in self.came.items():
            came = tie(came, *tokens) if tokens else came
            if self.hop > 1:
                self.held[way] = add_low(came, self.piece(way * (self.hop - 1)))
            else:
                mine = self.piece(0) if self.total is None else self.total
                self.total = mine.astype(jnp.float32) + came.astype(jnp.float32)
        self.hop -= 1
        return self.tokens() if self.total is None else [self.total]

    def finish(self):
        while self.hop > 0:
            self.send().absorb()
        return self.total


LOW = jnp.bfloat16
F32 = jnp.float32
TILE = 256
LONG = 6
SHORT = 2
GELU_A = 0.7978845608028654
GELU_B = 0.044715
VMEM = 36 * 2**20


def mm(a, b):
    return jnp.dot(a, b, preferred_element_type=F32)


def mm_nt(a, b):
    return lax.dot_general(a, b, (((1,), (1,)), ((), ())), preferred_element_type=F32)


def mm_tn(a, b):
    return lax.dot_general(a, b, (((0,), (0,)), ((), ())), preferred_element_type=F32)


def call(body, out_shape, in_specs, out_specs, args, grid=(1,), flops=0, scratch=(), into=(), prefetch=()):
    given = len(prefetch)
    used = len(in_specs)

    def kernel(*refs):
        body(*refs[: given + used], *refs[given + used + len(into) :])

    nbytes = sum(a.size * a.dtype.itemsize for a in args)
    nbytes += sum(o.size * o.dtype.itemsize for o in jax.tree.leaves(out_shape))
    return pl.pallas_call(
        kernel,
        out_shape=out_shape,
        grid_spec=pltpu.PrefetchScalarGridSpec(
            num_scalar_prefetch=given,
            grid=grid,
            in_specs=list(in_specs) + [pl.BlockSpec(memory_space=pl.ANY)] * len(into),
            out_specs=out_specs,
            scratch_shapes=list(scratch),
        ),
        compiler_params=pltpu.CompilerParams(vmem_limit_bytes=VMEM),
        cost_estimate=pl.CostEstimate(flops=flops // 16, bytes_accessed=nbytes // 16, transcendentals=0),
        input_output_aliases={given + used + i: i for i in range(len(into))},
    )(*prefetch, *args, *into)


def held(shape):
    return pl.BlockSpec(shape, lambda *_: (0,) * len(shape), pipeline_mode=pl.Buffered(1))


def like(shape, dtype):
    return jax.ShapeDtypeStruct(shape, dtype)


def scale_of(v):
    return lax.rsqrt(jnp.mean(v * v, axis=-1, keepdims=True) + EPSILON)


def norm_pull(v, s, g, dy):
    w = dy * g
    return s * w - v * (s * s * s) * jnp.mean(w * v, axis=-1, keepdims=True)


def turn(v, cos_t, sin_t, sign):
    half = v.shape[-1] // 2
    a, b = v[:, :half], v[:, half:]
    return jnp.concatenate([a * cos_t - sign * (b * sin_t), b * cos_t + sign * (a * sin_t)], axis=-1)


def stored_block(p):
    return jnp.where(p < 4, 2 * p, 2 * (7 - p) + 1)


def padded(rows):
    return -(-rows // 16) * 16


def pack_columns(w_gate_up, dp, ctx):
    rows, wide = w_gate_up.shape
    ff = wide // 2
    step = ff // (dp * ctx)
    room = padded(step)
    part = dp * room

    def body(w, out):
        zeros = [jnp.zeros((rows, room - step), F32)] if room > step else []
        for c in range(ctx):
            for side in range(2):
                cut = []
                for d in range(dp):
                    at = side * ff + (d * ctx + c) * step
                    cut += [w[:, at : at + step]] + zeros
                out[c, :, side * part : (side + 1) * part] = jnp.concatenate(cut, axis=1).astype(LOW)

    return call(
        body,
        like((ctx, rows, 2 * part), LOW),
        [held((rows, wide))],
        held((ctx, rows, 2 * part)),
        (w_gate_up,),
    )


def unpack_columns(parts, dp, ctx, step):
    rows, wide = parts.shape[1], parts.shape[2]
    part = wide // 2
    room = part // dp
    ff = dp * ctx * step

    def body(p, out):
        for c in range(ctx):
            own = p[c].astype(F32)
            for side in range(2):
                for d in range(dp):
                    at = side * ff + (d * ctx + c) * step
                    start = side * part + d * room
                    out[:, at : at + step] = own[:, start : start + step]

    return call(
        body,
        like((rows, 2 * ff), F32),
        [held(parts.shape)],
        held((rows, 2 * ff)),
        (parts,),
    )


class Blocks:
    def __init__(self, gathered, rows=None):
        block, self.cols = gathered.parts[0].shape
        self.rows = rows = rows or block
        count = gathered.ring.count
        self.height = rows * count
        if rows % 16:
            whole = gathered.whole().reshape(count, block, self.cols)[:, :rows]
            self.parts, self.steps = [whole.reshape(self.height, self.cols)], [0]
            self.rows = self.height
        else:
            self.parts, self.steps = gathered.parts, gathered.steps

    def specs(self):
        return [pl.BlockSpec(memory_space=pl.ANY)] * len(self.parts)

    def scratch(self):
        return [
            pltpu.VMEM((self.height, self.cols), LOW),
            pltpu.SemaphoreType.DMA((len(self.parts),)),
        ]

    def load(self, places, refs, room, sems):
        @pl.when(pl.program_id(0) == 0)
        def _():
            copies = []
            for i, (step, ref) in enumerate(zip(self.steps, refs)):
                at = pl.multiple_of(places[step] * self.rows, 16) if len(refs) > 1 else 0
                copies.append(
                    pltpu.make_async_copy(
                        ref.at[pl.ds(0, self.rows), :], room.at[pl.ds(at, self.rows), :], sems.at[i]
                    )
                )
            for copy in copies:
                copy.start()
            for copy in copies:
                copy.wait()


def unpack_small(gathered, first, dp, ctx, out_rows, gain_cols, head_cols):
    block, wide = gathered.parts[0].shape
    rows = block - first
    direct = first % 16 == 0 and rows % 16 == 0
    if direct:
        parts, steps = gathered.parts, gathered.steps
    else:
        parts, steps = [gathered.whole().reshape(dp, block, wide)[:, first:]], [0]
    half = out_rows // 2
    count = len(parts)

    def body(places, *refs):
        gain, head, out, room, sems = refs[count:]
        copies = []
        for i, ref in enumerate(refs[:count]):
            if direct:
                source, target = ref.at[pl.ds(first, rows), :], room.at[places[steps[i]]]
            else:
                source, target = ref, room
            copies.append(pltpu.make_async_copy(source, target, sems.at[i]))
        for copy in copies:
            copy.start()
        for copy in copies:
            copy.wait()
        lines = []
        for d in range(dp):
            extra = room[d, : 4 * ctx, :].astype(F32)
            lines += [extra[4 * c : 4 * c + 1] for c in range(ctx)]
            at, own = d * out_rows, room[d, 4 * ctx :, :]
            out[at : at + out_rows, :wide] = own[:out_rows]
            out[at : at + half, wide:] = own[out_rows:, : D - wide]
            out[at + half : at + out_rows, wide:] = own[out_rows:, D - wide :]
        for g in range(4):
            cut = [line[:, g * gain_cols : (g + 1) * gain_cols] for line in lines]
            gain[g : g + 1, :] = jnp.concatenate(cut, axis=1)
        for g in range(2):
            at = 4 * gain_cols + g * head_cols
            cut = [line[:, at : at + head_cols] for line in lines]
            head[g : g + 1, :] = jnp.concatenate(cut, axis=1)

    return call(
        body,
        [like((4, D), F32), like((2, HD), F32), like((HD, D), LOW)],
        [pl.BlockSpec(memory_space=pl.ANY)] * count,
        [held((4, D)), held((2, HD)), held((HD, D))],
        tuple(parts),
        scratch=[pltpu.VMEM((dp, rows, wide), LOW), pltpu.SemaphoreType.DMA((count,))],
        prefetch=(gathered.ring.places,),
    )


def input_stage(x, w_in, gain, head_rows, cos_t, sin_t, row_map, places):
    seq = x.shape[0]
    count = len(w_in.parts)

    def body(_, pl_ref, x0, x1, g, hg, cos, sin, *refs):
        q, k, v, raw, n_ref, w, sems = refs[count:]
        w_in.load(pl_ref, refs[:count], w, sems)
        for i, x_ref in enumerate((x0, x1)):
            at = slice(i * TILE, (i + 1) * TILE)
            xf = x_ref[...].astype(F32)
            n = (xf * scale_of(xf) * g[...]).astype(LOW)
            n_ref[at, :] = n
            y = mm(n, w[...])
            qy, ky = y[:, :HD], y[:, HD : 2 * HD]
            raw[at, :] = y[:, : 2 * HD]
            c, s = cos[at, :], sin[at, :]
            q[at, :] = turn(qy * scale_of(qy) * hg[0:1], c, s, 1.0).astype(LOW)
            k[at, :] = turn(ky * scale_of(ky) * hg[1:2], c, s, 1.0).astype(LOW)
            v[at, :] = y[:, 2 * HD :].astype(LOW)

    def block(cols):
        return pl.BlockSpec((2 * TILE, cols), lambda p, m, s: (p, 0))

    return call(
        body,
        [like((seq, HD), LOW)] * 3 + [like((seq, 2 * HD), F32), like((seq, D), LOW)],
        [
            pl.BlockSpec((TILE, D), lambda p, m, s: (m[2 * p], 0)),
            pl.BlockSpec((TILE, D), lambda p, m, s: (m[2 * p + 1], 0)),
            held((1, D)),
            held((2, HD)),
            block(HD // 2),
            block(HD // 2),
        ]
        + w_in.specs(),
        [block(HD)] * 3 + [block(2 * HD), block(D)],
        (x, x, gain, head_rows, cos_t, sin_t, *w_in.parts),
        grid=(seq // TILE // 2,),
        flops=2 * seq * D * 3 * HD,
        scratch=w_in.scratch(),
        prefetch=(row_map, places),
    )


def scores_of(q, k, doc_step):
    s = mm_nt(q, k) * HD ** (-0.5)
    row = lax.broadcasted_iota(jnp.int32, s.shape, 0) + doc_step * TILE
    col = lax.broadcasted_iota(jnp.int32, s.shape, 1)
    return jnp.where(col <= row, s, -1e30)


def attention(q, k, v, base):
    seq = q.shape[0]

    def body(b, q_ref, k_ref, v_ref, mixed, lse):
        for doc, count in enumerate((LONG, SHORT)):
            first = b[doc]
            for i in range(count):
                p = first + i
                at = pl.ds(pl.multiple_of(p * TILE, TILE), TILE)
                keys = pl.ds(pl.multiple_of(first * TILE, TILE), (i + 1) * TILE)
                s = scores_of(q_ref[at, :], k_ref[keys, :], i)
                peak = jnp.max(s, axis=-1, keepdims=True)
                e = jnp.exp(s - peak)
                total = jnp.sum(e, axis=-1, keepdims=True)
                lse[at, :] = peak + jnp.log(total)
                probs = (e * (1.0 / total)).astype(LOW)
                to = pl.ds(pl.multiple_of(stored_block(p) * TILE, TILE), TILE)
                mixed[to, :] = mm(probs, v_ref[keys, :]).astype(LOW)

    return call(
        body,
        [like((seq, HD), LOW), like((seq, 1), F32)],
        [held((seq, HD))] * 3,
        [held((seq, HD)), held((seq, 1))],
        (q, k, v),
        flops=4 * 24 * TILE * TILE * HD,
        prefetch=(base,),
    )


def attention_back(q, k, v, raw, lse, grads, head_rows, cos_t, sin_t, base):
    seq = q.shape[0]
    chip = seq // 2

    def pull_head(v_raw, g, dy, cos, sin):
        dy = turn(dy, cos, sin, -1.0)
        s = scale_of(v_raw)
        return norm_pull(v_raw, s, g, dy), jnp.sum(dy * v_raw * s, axis=0, keepdims=True)

    def body(b, q_ref, k_ref, v_ref, raw_ref, l_ref, *refs):
        hg, cos, sin, out, head_out, dk, dv, mixed_grad = refs[6:]
        for i in range(2):
            mine, near, far = refs[3 * i : 3 * i + 3]
            rows = pl.ds(pl.multiple_of((b[2] if i == 0 else 1 - b[2]) * chip, chip), chip)
            mixed_grad[rows, :] = (
                mine[0].astype(F32) + near[0].astype(F32) + far[...].astype(F32)
            ).astype(LOW)
        dk[...] = jnp.zeros_like(dk)
        dv[...] = jnp.zeros_like(dv)
        head_q = jnp.zeros((1, HD), F32)
        for doc, count in enumerate((LONG, SHORT)):
            first = b[doc]
            for i in range(count):
                p = first + i
                at = pl.ds(pl.multiple_of(p * TILE, TILE), TILE)
                keys = pl.ds(pl.multiple_of(first * TILE, TILE), (i + 1) * TILE)
                src = pl.ds(pl.multiple_of(stored_block(p) * TILE, TILE), TILE)
                do = mixed_grad[src, :]
                qs = q_ref[at, :]
                probs = jnp.exp(scores_of(qs, k_ref[keys, :], i) - l_ref[at, :])
                dp = mm_nt(do, v_ref[keys, :])
                inner = jnp.sum(probs * dp, axis=-1, keepdims=True)
                ds = (probs * (dp - inner)).astype(LOW)
                dq = mm(ds, k_ref[keys, :]) * HD ** (-0.5)
                dk[keys, :] += mm_tn(ds, qs)
                dv[keys, :] += mm_tn(probs.astype(LOW), do)
                dq, part = pull_head(raw_ref[at, :HD], hg[0:1], dq, cos[at, :], sin[at, :])
                head_q += part
                out[at, :HD] = dq.astype(LOW)
        head_k = jnp.zeros((1, HD), F32)
        for p in range(seq // TILE):
            at = slice(p * TILE, (p + 1) * TILE)
            dkp, part = pull_head(
                raw_ref[at, HD:], hg[1:2], dk[at, :] * HD ** (-0.5), cos[at, :], sin[at, :]
            )
            head_k += part
            out[at, HD : 2 * HD] = dkp.astype(LOW)
            out[at, 2 * HD :] = dv[at, :].astype(LOW)
        head_out[0:1, :] = head_q
        head_out[1:2, :] = head_k

    pair = pl.BlockSpec((1, chip, HD), lambda *_: (0, 0, 0), pipeline_mode=pl.Buffered(1))
    return call(
        body,
        [like((seq, 3 * HD), LOW), like((2, HD), F32)],
        [held((seq, HD))] * 3
        + [held((seq, 2 * HD)), held((seq, 1))]
        + [pair, pair, held((chip, HD))] * 2
        + [held((2, HD))]
        + [held((seq, HD // 2))] * 2,
        [held((seq, 3 * HD)), held((2, HD))],
        (q, k, v, raw, lse, *grads, head_rows, cos_t, sin_t),
        flops=10 * 24 * TILE * TILE * HD,
        scratch=[pltpu.VMEM((seq, HD), F32)] * 2 + [pltpu.VMEM((seq, HD), LOW)],
        prefetch=(base,),
    )


def project(mixed, outs, x, gains, stored_map):
    seq = x.shape[0]

    def body(_, m0, m1, m2, m3, w0, w1, w2, w3, x_ref, g, proj, pre):
        for i in range(2):
            at = slice(i * TILE, (i + 1) * TILE)
            y = mm(m0[at, :], w0[...]) + mm(m1[at, :], w1[...])
            y = y + mm(m2[at, :], w2[...]) + mm(m3[at, :], w3[...])
            proj[at, :] = y
            r = x_ref[at, :].astype(F32) + y * scale_of(y) * g[1:2]
            pre[at, :] = (r * scale_of(r) * g[2:3]).astype(LOW)

    def block(cols):
        return pl.BlockSpec((2 * TILE, cols), lambda r, m: (r, 0))

    return call(
        body,
        [like((seq, D), F32), like((seq, D), LOW)],
        [pl.BlockSpec((2 * TILE, HD), lambda r, m: (m[2 * r] // 2, 0))] * 4
        + [held((HD, D))] * 4
        + [block(D), held((4, D))],
        [block(D), block(D)],
        (*mixed, *outs, x, gains),
        grid=(seq // TILE // 2,),
        flops=2 * seq * D * H * HD,
        prefetch=(stored_map,),
    )


def column_cuts(main, width):
    return [(at, min(width, main - at)) for at in range(0, main, width)]


def gate_stage(pre, w, places, half, into=()):
    seq, part = pre.shape[0], w.cols // 2
    rows = 512
    first = half * (seq // 2 // rows)
    count = len(w.parts)

    def pieces(g, u):
        t = jnp.tanh(GELU_A * (g + GELU_B * (g * g * g)))
        a = 0.5 * g * (1.0 + t)
        slope = 0.5 * (1.0 + t) + (0.5 * g) * (1.0 - t * t) * (GELU_A * (1.0 + 3.0 * GELU_B * (g * g)))
        return a * u, u * slope, a

    def body(pl_ref, p_ref, *refs):
        hidden, ab, room, sems = refs[count:]
        w.load(pl_ref, refs[:count], room, sems)
        p = p_ref[...]

        def multiply(at, wide):
            return mm(p, room[:, at : at + wide]), mm(p, room[:, part + at : part + at + wide])

        def finish(at, wide, made):
            h, b, a = pieces(*made)
            hidden[:, at : at + wide] = h.astype(LOW)
            ab[:, at : at + wide] = b.astype(LOW)
            ab[:, part + at : part + at + wide] = a.astype(LOW)

        last = None
        for cut in column_cuts(part, 256):
            made = multiply(*cut)
            if last is not None:
                finish(*last)
            last = (*cut, made)
        finish(*last)

    def block(cols):
        return pl.BlockSpec((rows, cols), lambda r, m: (first + r, 0))

    return call(
        body,
        [like((seq, part), LOW), like((seq, 2 * part), LOW)],
        [block(D)] + w.specs(),
        [block(part), block(2 * part)],
        (pre, *w.parts),
        grid=(seq // 2 // rows,),
        flops=2 * seq * D * part,
        scratch=w.scratch(),
        into=into,
        prefetch=(places,),
    )


def down_stage(hidden, w, places, half):
    seq, part = hidden.shape
    rows = seq // 4
    count = len(w.parts)

    def body(pl_ref, h, *refs):
        even, odd, room, sems = refs[count:]
        w.load(pl_ref, refs[:count], room, sems)
        odd[...] = mm(h[rows:, :], room[...]).astype(LOW)
        even[...] = mm(h[:rows, :], room[...]).astype(LOW)

    return call(
        body,
        [like((rows, D), LOW)] * 2,
        [
            pl.BlockSpec(
                (2 * rows, part), lambda r, m: (half, 0), pipeline_mode=pl.Buffered(1)
            )
        ]
        + w.specs(),
        [held((rows, D))] * 2,
        (hidden, *w.parts),
        flops=4 * rows * D * part,
        scratch=w.scratch(),
        prefetch=(places,),
    )


def ffn_stage(parts, near, far, proj, x, cot, gains):
    rows = cot.shape[0]

    def body(p, n, f, proj_ref, x_ref, c_ref, g, out, grad, gain):
        y = p[...].astype(F32) + n[...].astype(F32) + f[...].astype(F32)
        pr = proj_ref[...]
        s = scale_of(y)
        r = x_ref[...].astype(F32) + pr * scale_of(pr) * g[1:2]
        out[...] = (r + y * s * g[3:4]).astype(LOW)
        dy = c_ref[...].astype(F32)
        grad[...] = norm_pull(y, s, g[3:4], dy).astype(LOW)
        part = jnp.sum(dy * y * s, axis=0, keepdims=True)

        @pl.when(pl.program_id(0) == 0)
        def _():
            gain[...] = part

        @pl.when(pl.program_id(0) > 0)
        def _():
            gain[...] += part

    block = pl.BlockSpec((TILE, D), lambda r: (r, 0))
    return call(
        body,
        [like((rows, D), LOW), like((rows, D), LOW), like((1, D), F32)],
        [block] * 6 + [held((4, D))],
        [block, block, held((1, D))],
        (parts, near, far, proj, x, cot, gains),
        grid=(rows // TILE,),
    )


def hidden_back(grad, w, ab, places, half, into=()):
    seq, part = ab.shape[0], ab.shape[1] // 2
    rows = 512
    first = half * (seq // 2 // rows)
    count = len(w.parts)

    def body(pl_ref, g_ref, ab_ref, *refs):
        out, room, sems = refs[count:]
        w.load(pl_ref, refs[:count], room, sems)
        g = g_ref[...]
        for at, wide in column_cuts(part, 256):
            hg = mm_nt(g, room[at : at + wide, :])
            for side in (at, part + at):
                out[:, side : side + wide] = (hg * ab_ref[:, side : side + wide].astype(F32)).astype(LOW)

    def block(cols):
        return pl.BlockSpec((rows, cols), lambda r, m: (first + r, 0))

    return call(
        body,
        [like((seq, 2 * part), LOW)],
        [pl.BlockSpec((rows, D), lambda r, m: (r, 0)), block(2 * part)] + w.specs(),
        [block(2 * part)],
        (grad, ab, *w.parts),
        grid=(seq // 2 // rows,),
        flops=seq * D * part,
        scratch=w.scratch(),
        into=into,
        prefetch=(places,),
    )[0]


def residual_back(gu, w, outs, proj, x, cot, gains, stored_map, places, half, into=()):
    seq, wide = gu.shape
    own = cot.shape[0] // TILE
    steps = seq // 2 // TILE
    first = half * steps
    count = len(w.parts)

    def body(_, pl_ref, gu_ref, w0, w1, w2, w3, proj_ref, x_ref, c_ref, g, *refs):
        rg, pg, even, odd, gain, room, sems, *made = refs[count:]
        w.load(pl_ref, refs[:count], room, sems)
        step = pl.program_id(0)

        def multiply(turn):
            made[turn][...] = mm_nt(gu_ref[...], room[...])

        def finish(turn):
            dy = made[turn][...]
            pr = proj_ref[...]
            sp = scale_of(pr)
            r = x_ref[...].astype(F32) + pr * sp * g[1:2]
            s = scale_of(r)
            dr = norm_pull(r, s, g[2:3], dy)
            if half == 0:
                dr = dr + jnp.where(step <= own, 1.0, 0.0) * c_ref[...].astype(F32)
            rg[...] = dr.astype(LOW)
            low = norm_pull(pr, sp, g[1:2], dr).astype(LOW)
            pg[...] = low
            even[0] = mm_nt(low, w0[...]).astype(LOW)
            odd[0] = mm_nt(low, w1[...]).astype(LOW)
            even[1] = mm_nt(low, w2[...]).astype(LOW)
            odd[1] = mm_nt(low, w3[...]).astype(LOW)
            before = jnp.where(step == 1, 0.0, gain[...])
            gain[0:1, :] = before[0:1] + jnp.sum(dr * pr * sp, axis=0, keepdims=True)
            gain[1:2, :] = before[1:2] + jnp.sum(dy * r * s, axis=0, keepdims=True)

        @pl.when(step == 0)
        def _():
            multiply(0)

        for turn in range(2):

            @pl.when((step > 0) & (step < steps) & (step % 2 == turn))
            def _():
                multiply(turn)
                finish(1 - turn)

        @pl.when(step == steps)
        def _():
            finish((steps - 1) % 2)

    def last(i):
        return jnp.maximum(i - 1, 0)

    def block(cols):
        return pl.BlockSpec((TILE, cols), lambda i, m, p: (first + last(i), 0))

    heads = pl.BlockSpec((2, TILE, HD), lambda i, m, p: (0, m[first + last(i)] % steps, 0))
    return call(
        body,
        [like((seq, D), LOW), like((seq, D), LOW)]
        + [like((2, seq // 2, HD), LOW)] * 2
        + [like((2, D), F32)],
        [pl.BlockSpec((TILE, wide), lambda i, m, p: (first + jnp.minimum(i, steps - 1), 0))]
        + [held((HD, D))] * 4
        + [block(D), block(D)]
        + [pl.BlockSpec((TILE, D), lambda i, m, p: (jnp.minimum(last(i), own - 1), 0)), held((4, D))]
        + w.specs(),
        [
            block(D),
            pl.BlockSpec((TILE, D), lambda i, m, p: (m[first + last(i)], 0)),
            heads,
            heads,
            held((2, D)),
        ],
        (gu, *outs, proj, x, cot, gains, *w.parts),
        grid=(steps + 1,),
        flops=seq * D * (wide + H * HD),
        scratch=w.scratch() + [pltpu.VMEM((TILE, D), F32)] * 2,
        into=into,
        prefetch=(stored_map, places),
    )


def input_back(qkv, w_in, x, rg, gain, pos_map, places):
    seq = x.shape[0]
    rows = 2 * TILE
    count = len(w_in.parts)

    def body(_, pl_ref, q0, q1, x_ref, rg_ref, g, *refs):
        even, odd, gain_out, w, sems = refs[count:]
        w_in.load(pl_ref, refs[:count], w, sems)
        step = pl.program_id(0)
        total = jnp.zeros((1, D), F32)
        made = []
        for i, q_ref in enumerate((q0, q1)):
            at = slice(i * TILE, (i + 1) * TILE)
            dy = mm_nt(q_ref[...], w[...])
            xf = x_ref[at, :].astype(F32)
            s = scale_of(xf)
            made.append((rg_ref[at, :].astype(F32) + norm_pull(xf, s, g[...], dy)).astype(LOW))
            total += jnp.sum(dy * xf * s, axis=0, keepdims=True)
        gain_out[...] = jnp.where(step == 0, 0.0, gain_out[...]) + total

        @pl.when(step % 2 == 0)
        def _():
            even[:TILE, :], even[TILE:, :] = made

        @pl.when(step % 2 == 1)
        def _():
            odd[:TILE, :], odd[TILE:, :] = made

    block = pl.BlockSpec((rows, D), lambda i, m, s: (i, 0))
    out = pl.BlockSpec((rows, D), lambda i, m, s: (i // 2, 0))
    return call(
        body,
        [like((seq // 2, D), LOW)] * 2 + [like((1, D), F32)],
        [
            pl.BlockSpec((TILE, 3 * HD), lambda i, m, s: (m[2 * i], 0)),
            pl.BlockSpec((TILE, 3 * HD), lambda i, m, s: (m[2 * i + 1], 0)),
            block,
            block,
            held((1, D)),
        ]
        + w_in.specs(),
        [out, out, held((1, D))],
        (qkv, qkv, x, rg, gain, *w_in.parts),
        grid=(seq // rows,),
        flops=2 * seq * D * 3 * HD,
        scratch=w_in.scratch(),
        prefetch=(pos_map, places),
    )


def local(
    tokens,
    cotangent,
    lengths,
    w_qkv,
    w_out,
    w_gate_up,
    w_down,
    gains,
    head_gains,
    first_qkv,
    first_out,
    first_gate_up,
    first_down,
    first_gains,
    first_head,
    second_qkv,
    second_out,
    second_gate_up,
    second_down,
    second_gains,
    second_head,
):
    low = jnp.bfloat16
    f32 = jnp.float32
    rows = tokens.shape[1]
    dp = lax.axis_size("dp")
    ctx = lax.axis_size("ctx")
    place = lax.axis_index("ctx")
    seq = rows * ctx
    in_rows = w_qkv.shape[0]
    out_rows = w_out.shape[0]
    ff_rows = w_down.shape[0]
    gain_cols = gains.shape[1]
    head_cols = head_gains.shape[1]
    qkv_cols = 3 * HD
    ring = Ring()

    q_cols = w_qkv[:, : H * HD].astype(low).reshape(in_rows, ctx, HD).transpose(1, 0, 2)
    kv_cols = jnp.broadcast_to(w_qkv[:, H * HD :].astype(low)[None], (ctx, in_rows, 2 * HD))
    extra = jnp.concatenate(
        [gains.astype(low).reshape(-1), head_gains.astype(low).reshape(-1)]
    )
    extra = jnp.pad(extra, (0, 4 * qkv_cols - extra.shape[0])).reshape(4, qkv_cols)
    small_sent = jnp.concatenate(
        [
            jnp.concatenate([q_cols, kv_cols], axis=2),
            jnp.broadcast_to(extra[None], (ctx, 4, qkv_cols)),
        ],
        axis=1,
    )
    to_user = [((dp * c + d), d * ctx + c) for d in range(dp) for c in range(ctx)]
    to_owner = [(b, a) for a, b in to_user]
    out_mine = lax.ppermute(w_out.astype(low), ("dp", "ctx"), to_user)
    half = out_rows // 2
    small = exchange(small_sent, "ctx")
    packed = pack_columns(tie(w_gate_up, small_sent), dp, ctx)
    own_rows = ctx * in_rows
    small_ring = Gather(
        ring,
        jnp.concatenate(
            [
                small[:, :in_rows].reshape(own_rows, qkv_cols),
                small[:, in_rows:].reshape(4 * ctx, qkv_cols),
                out_mine[:, :qkv_cols],
                jnp.concatenate([out_mine[:half, qkv_cols:], out_mine[half:, qkv_cols:]], axis=1),
            ]
        ),
    )
    down_block = jnp.pad(w_down.astype(low), ((0, padded(ff_rows) - ff_rows), (0, 0)))
    down_ring = Gather(ring, down_block)
    down_first = down_ring.advance()
    tokens_far = swap(tie(tokens[0], small), 2)
    tokens_near = swap(tie(tokens[0], small), 1)
    gate_up_cols = exchange(tie(packed, tokens_far), "ctx").reshape(own_rows, -1)
    first_len = lengths[0, 0]
    pos = tie(jnp.arange(seq, dtype=jnp.int32), packed)
    cos_t, sin_t = rope_tables(pos - jnp.where(pos < first_len, 0, first_len), HD)
    small_ring.advance(*down_first)
    small_ring.advance(cos_t, sin_t)
    tokens_last = swap(tie(tokens_far, *small_ring.held.values()), 1)
    tokens_all = jnp.concatenate([tokens[0], tokens_near, tokens_far, tokens_last])
    while small_ring.hop < ring.hops[0]:
        small_ring.advance()
    small_seen = list(small_ring.held.values())
    gate_ring = Gather(ring, gate_up_cols)
    gate_seen = gate_ring.advance(*small_seen, tokens_last)
    w_in = Blocks(small_ring, own_rows)
    places = ring.places
    gain_rows, head_rows, out_mine = unpack_small(
        small_ring, own_rows, dp, ctx, out_rows, gain_cols, head_cols
    )
    out_far, out_near = swap(out_mine, 2), swap(out_mine, 1)

    blocks = seq // TILE
    split = first_len // TILE
    base = jnp.where(split == LONG, jnp.array([0, LONG, 0]), jnp.array([SHORT, 0, 0]))
    base = (base + jnp.array([0, 0, 1]) * (place // 2)).astype(jnp.int32)
    tiles = jnp.arange(blocks, dtype=jnp.int32)
    stored_map = 2 * (place ^ (tiles // 2)) + tiles % 2
    owner = jnp.where(tiles < ctx, tiles, 2 * ctx - 1 - tiles)
    row_map = 2 * (place ^ owner) + (tiles >= ctx)
    pos_map = jnp.where(tiles % 2 == 0, stored_map // 2, 2 * ctx - 1 - stored_map // 2)

    q, k, v, raw, normed = input_stage(
        tokens_all, w_in, gain_rows[0:1], head_rows, cos_t, sin_t, row_map, places
    )
    down_second = down_ring.advance(q, *gate_seen)
    gate_second = gate_ring.advance(q)
    mixed, lse = attention(tie(q, *gate_seen, out_far, out_near), k, v, base)
    mixed = tie(mixed, *down_second)
    mixed_far, mixed_near = swap(mixed, 2), swap(mixed, 1)
    out_parts = [out_mine, out_near, out_far, swap(tie(out_far, mixed), 1)]
    down_ring.advance(mixed)
    gate_ring.advance(mixed)
    mixed_parts = [mixed, mixed_near, mixed_far, swap(tie(mixed_far, *gate_second), 1)]
    proj, pre_low = project(mixed_parts, out_parts, tokens_all, gain_rows, stored_map)
    while gate_ring.hop < ring.hops[0]:
        gate_ring.advance(pre_low)
        if down_ring.hop < ring.hops[0]:
            down_ring.advance(pre_low)
    down_ring.finish()
    full_gate_up = Blocks(gate_ring)
    full_down = Blocks(down_ring)
    buffers = gate_stage(pre_low, full_gate_up, places, 1)
    even, odd = down_stage(buffers[0], full_down, places, 1)
    summed = add_low(even, swap(odd, 1))
    far = swap(summed, 2)
    hidden_low, slopes = gate_stage(tie(pre_low, summed), full_gate_up, places, 0, buffers)
    even, odd = down_stage(tie(hidden_low, far), full_down, places, 0)
    near = swap(odd, 1)
    result, ffn_grad, gain_grad_d = ffn_stage(
        even, near, far, proj, tokens[0], cotangent[0], gain_rows
    )

    far = swap(ffn_grad, 2)
    ffn_here = jnp.concatenate([ffn_grad, swap(ffn_grad, 1)])
    residual = partial(
        residual_back,
        w=full_gate_up,
        outs=out_parts,
        proj=proj,
        x=tokens_all,
        cot=cotangent[0],
        gains=gain_rows,
        stored_map=stored_map,
        places=places,
    )
    gate_up_low = hidden_back(ffn_here, full_down, slopes, places, 0)
    far = tie(far, gate_up_low)
    ffn_there = jnp.concatenate([far, swap(far, 1)])
    gate_up_low = hidden_back(ffn_there, full_down, slopes, places, 1, (gate_up_low,))
    grad_gate_up = mm_tn(pre_low, gate_up_low).astype(low)
    gate_sum = Reduce(ring, grad_gate_up).send()
    resid_grad, proj_low, even, odd, gain_grad_here = residual(
        tie(gate_up_low, *gate_sum.tokens()), half=0
    )
    held_gate = gate_sum.absorb(resid_grad)
    near = swap(tie(odd, *held_gate), 1)
    parts_here = (even, near)
    summed = add_low(even[1], near[1])
    far_there = swap(summed, 2)
    gate_sum.send()
    ffn_low = jnp.concatenate([ffn_here, ffn_there])
    grad_down = mm_tn(hidden_low, tie(ffn_low, summed, *held_gate)).astype(low)
    down_sum = Reduce(ring, grad_down).send()
    resid_grad, proj_low, even, odd, gain_grad_there = residual(
        tie(gate_up_low, far_there, *down_sum.tokens()), half=1, into=(resid_grad, proj_low)
    )
    near = swap(tie(odd, *gate_sum.came.values(), *down_sum.came.values()), 1)
    summed = add_low(even[1], near[1])
    far_here = swap(summed, 2)
    held_gate = gate_sum.absorb(odd)
    held_down = down_sum.absorb(odd)
    gate_sum.send()
    down_sum.send()
    proj_low = tie(proj_low, *held_gate, *held_down)
    grad_out = [mm_tn(m, proj_low).astype(low) for m in mixed_parts]
    far_here = tie(far_here, *grad_out)
    grad_out = reduce_ctx(grad_out).astype(low)
    qkv_low, head_grads = attention_back(
        q,
        k,
        v,
        raw,
        lse,
        parts_here + (far_here,) + (even, near, far_there),
        head_rows,
        cos_t,
        sin_t,
        base,
    )
    grad_in = mm_tn(normed, qkv_low).astype(low)
    grad_out = grad_out.reshape(dp, out_rows, D)
    in_blocks = jnp.concatenate(
        [
            grad_in.reshape(dp, own_rows, qkv_cols),
            grad_out[:, :, :qkv_cols],
            jnp.concatenate(
                [grad_out[:, :half, qkv_cols:], grad_out[:, half:, qkv_cols:]], axis=2
            ),
        ],
        axis=1,
    )
    in_sum = Reduce(ring, in_blocks.reshape(-1, qkv_cols))
    held_gate = gate_sum.absorb(*in_sum.tokens())
    held_down = down_sum.absorb(*in_sum.tokens())
    in_sum.send()
    gate_sum.send()
    down_sum.send()
    held_in = in_sum.absorb(*held_gate, *held_down)
    in_sum.send()
    input_even, input_odd, gain_grad_a = input_back(
        tie(qkv_low, *held_in),
        w_in,
        tokens_all,
        resid_grad,
        gain_rows[0:1],
        pos_map,
        places,
    )
    gate_came = list(gate_sum.came.values())
    in_sum.absorb(input_odd)
    in_sum.send(*gate_came)
    gate_sum.absorb(input_odd)
    down_sum.absorb(input_odd)
    gate_up_own = gate_sum.finish().astype(low)
    gate_up_own = exchange(gate_up_own.reshape(ctx, in_rows, -1), "ctx")
    near = swap(tie(input_odd, *gate_came), 1)
    summed = add_low(input_even[rows:], near[rows:])
    gain_grad_bc = gain_grad_here + gain_grad_there
    while in_sum.hop > 1:
        in_sum.absorb()
        in_sum.send()

    in_own = in_sum.absorb()[0].astype(low)
    down_sum.send(in_own)
    down_sum.absorb()
    down_own = down_sum.finish()[:ff_rows]
    gate_up_own = unpack_columns(gate_up_own, dp, ctx, ff_rows)
    out_own = in_own[own_rows:]
    out_own = jnp.concatenate(
        [
            out_own[:out_rows],
            jnp.concatenate(
                [out_own[out_rows:, : D - qkv_cols], out_own[out_rows:, D - qkv_cols :]], axis=0
            ),
        ],
        axis=1,
    )
    out_own = lax.ppermute(out_own, ("dp", "ctx"), to_owner).astype(f32)
    in_own = exchange(in_own[:own_rows].reshape(ctx, in_rows, qkv_cols), "ctx").astype(f32)
    qkv_own = jnp.concatenate(
        [
            in_own[:, :, :HD].transpose(1, 0, 2).reshape(in_rows, H * HD),
            jnp.sum(in_own[:, :, HD:], axis=0),
        ],
        axis=1,
    )
    gain_grads = jnp.concatenate([gain_grad_a, gain_grad_bc, gain_grad_d], axis=0)
    local_squares = jnp.float32(0.0)
    for piece in (qkv_own, out_own, gate_up_own, down_own):
        local_squares = local_squares + jnp.sum(piece * piece)
    lines = jnp.concatenate([gain_grads.reshape(-1, 128), head_grads.reshape(-1, 128)])
    squares = jnp.pad(local_squares.reshape(1, 1), ((0, 7), (0, 127)))
    sums = tie(jnp.concatenate([lines, squares]), summed)
    sums = sums + swap(sums, 2)
    far = swap(tie(summed, sums), 2)
    input_grad = (
        input_even[:rows].astype(f32) + near[:rows].astype(f32) + far.astype(f32)
    )
    sums = sum_rest(sums)
    small_grads = sums[: lines.shape[0]]
    index = lax.axis_index("dp") * ctx + place
    gains_own = lax.dynamic_slice_in_dim(
        small_grads[: 4 * D // 128].reshape(4, D), index * gain_cols, gain_cols, axis=1
    )
    head_own = lax.dynamic_slice_in_dim(
        small_grads[4 * D // 128 :].reshape(2, HD), index * head_cols, head_cols, axis=1
    )
    reduced = (qkv_own, out_own, gate_up_own, down_own, gains_own, head_own)
    total_squares = sums[lines.shape[0], 0] + jnp.sum(small_grads * small_grads)
    grad_norm = jnp.sqrt(total_squares)
    factor = 1.0 / jnp.maximum(grad_norm, 1.0)
    weights = (w_qkv, w_out, w_gate_up, w_down, gains, head_gains)
    firsts = (first_qkv, first_out, first_gate_up, first_down, first_gains, first_head)
    seconds = (second_qkv, second_out, second_gate_up, second_down, second_gains, second_head)
    rates = (D ** (-0.5), (H * HD) ** (-0.5), D ** (-0.5), FF ** (-0.5), GAIN_RATE, GAIN_RATE)
    decays = (WEIGHT_DECAY, WEIGHT_DECAY, WEIGHT_DECAY, WEIGHT_DECAY, 0.0, 0.0)
    reduced = reduced[:2] + (tie(gate_up_own, far, grad_norm), tie(down_own, far, grad_norm)) + reduced[4:]
    updates = [
        adam_update(
            weights[index],
            firsts[index],
            seconds[index],
            reduced[index] * factor,
            rates[index],
            decays[index],
        )
        for index in range(6)
    ]
    return (
        result[None],
        input_grad[None],
        updates[0][0],
        updates[1][0],
        updates[2][0],
        updates[3][0],
        updates[4][0],
        updates[5][0],
        updates[0][1],
        updates[1][1],
        updates[2][1],
        updates[3][1],
        updates[4][1],
        updates[5][1],
        updates[0][2],
        updates[1][2],
        updates[2][2],
        updates[3][2],
        updates[4][2],
        updates[5][2],
        grad_norm,
    )


def solution(mesh):
    in_specs = (
        P("dp", "ctx", None),
        P("dp", "ctx", None),
        P("dp", None),
        P(("dp", "ctx"), None),
        P(("dp", "ctx"), None),
        P(("dp", "ctx"), None),
        P(("dp", "ctx"), None),
        P(None, ("dp", "ctx")),
        P(None, ("dp", "ctx")),
        P(("dp", "ctx"), None),
        P(("dp", "ctx"), None),
        P(("dp", "ctx"), None),
        P(("dp", "ctx"), None),
        P(None, ("dp", "ctx")),
        P(None, ("dp", "ctx")),
        P(("dp", "ctx"), None),
        P(("dp", "ctx"), None),
        P(("dp", "ctx"), None),
        P(("dp", "ctx"), None),
        P(None, ("dp", "ctx")),
        P(None, ("dp", "ctx")),
    )
    out_specs = (
        P("dp", "ctx", None),
        P("dp", "ctx", None),
        P(("dp", "ctx"), None),
        P(("dp", "ctx"), None),
        P(("dp", "ctx"), None),
        P(("dp", "ctx"), None),
        P(None, ("dp", "ctx")),
        P(None, ("dp", "ctx")),
        P(("dp", "ctx"), None),
        P(("dp", "ctx"), None),
        P(("dp", "ctx"), None),
        P(("dp", "ctx"), None),
        P(None, ("dp", "ctx")),
        P(None, ("dp", "ctx")),
        P(("dp", "ctx"), None),
        P(("dp", "ctx"), None),
        P(("dp", "ctx"), None),
        P(("dp", "ctx"), None),
        P(None, ("dp", "ctx")),
        P(None, ("dp", "ctx")),
        P(),
    )
    return jax.shard_map(local, mesh=mesh, in_specs=in_specs, out_specs=out_specs, check_vma=False)
```

```python
from functools import partial

import jax
import jax.numpy as jnp
from jax import lax
from jax.experimental import pallas as pl
from jax.experimental.pallas import tpu as pltpu
from jax.sharding import PartitionSpec as P

D = 1152
H = 4
HD = 256
FF = 6912
STEP = 10

EPSILON = 1e-06
ROPE_BASE = 1000000.0
BETA_ONE = 0.9
BETA_TWO = 0.95
ADAM_EPSILON = 1e-08
WEIGHT_DECAY = 0.1
GAIN_RATE = 1.0


def rope_tables(offsets, width):
    half = width // 2
    freq = jnp.exp(-jnp.log(ROPE_BASE) * jnp.arange(half, dtype=jnp.float32) * (2.0 / width))
    angle = offsets.astype(jnp.float32)[:, None] * freq[None, :]
    return (jnp.cos(angle), jnp.sin(angle))


def adam_update(weight, first, second, grad, rate, decay):
    first_new = BETA_ONE * first + (1.0 - BETA_ONE) * grad
    second_new = BETA_TWO * second + (1.0 - BETA_TWO) * grad * grad
    first_hat = first_new / (1.0 - BETA_ONE**STEP)
    second_hat = second_new / (1.0 - BETA_TWO**STEP)
    updated = weight - rate * (first_hat / (jnp.sqrt(second_hat) + ADAM_EPSILON) + decay * weight)
    return (updated, first_new, second_new)


def exchange(parts, axis):
    return lax.all_to_all(parts, axis, split_axis=0, concat_axis=0, tiled=True)


def swap(value, bit):
    count = lax.axis_size("ctx")
    return lax.ppermute(value, "ctx", [(i, i ^ bit) for i in range(count)])


def swap_dp(value, bit):
    count = lax.axis_size("dp")
    return lax.ppermute(value, "dp", [(i, i ^ bit) for i in range(count)])


def gather_ctx(block):
    far = swap(block, 2)
    return [block, swap(block, 1), far, swap(far, 1)]


def add_low(a, b):
    return a + b


def reduce_ctx(blocks):
    near, far = jnp.concatenate([blocks[1], blocks[3]]), None
    near = swap(near, 1)
    size = blocks[0].shape[0]
    far = swap(add_low(blocks[2], near[size:]), 2)
    mine = blocks[0].astype(jnp.float32) + near[:size].astype(jnp.float32)
    return mine + far.astype(jnp.float32)


def reorder(value, bit, rows):
    parts = [value[j * rows : (j + 1) * rows] for j in range(value.shape[0] // rows)]
    return jnp.concatenate([parts[j ^ bit] for j in range(len(parts))])


def sum_others(value):
    value = value + swap(value, 1)
    bit = 1
    while bit < lax.axis_size("dp"):
        value = value + swap_dp(value, bit)
        bit *= 2
    return value


def tie(value, *tokens):
    return lax.optimization_barrier((value, *tokens))[0]


class Ring:
    def __init__(self):
        count = self.count = lax.axis_size("dp")
        self.ctx = lax.axis_size("ctx")
        self.order = list(range(0, count, 2)) + list(range(count - 1, 0, -2))
        self.hops = (count // 2, count - 1 - count // 2)
        table = [
            [self.order[(self.order.index(i) + sense * step) % count] for step in range(count)]
            for sense in (1, -1)
            for i in range(count)
        ]
        row = (lax.axis_index("ctx") % 2) * count + lax.axis_index("dp")
        self.places = lax.dynamic_slice(
            jnp.array(table, jnp.int32), (row, 0), (1, count), allow_negative_indices=False
        )[0]

    def send(self, value, way):
        pairs = []
        for place, source in enumerate(self.order):
            for c in range(self.ctx):
                target = self.order[(place + (way if c % 2 == 0 else -way)) % self.count]
                pairs.append((source * self.ctx + c, target * self.ctx + c))
        return lax.ppermute(value, ("dp", "ctx"), pairs)

    def ways(self, hop):
        return [way for way, last in zip((1, -1), self.hops) if hop <= last]


class Gather:
    def __init__(self, ring, block):
        self.ring, self.hop = ring, 0
        self.held = {1: block, -1: block}
        self.parts, self.steps = [block], [0]

    def advance(self, *tokens):
        self.hop += 1
        for way in self.ring.ways(self.hop):
            self.held[way] = self.ring.send(tie(self.held[way], *tokens), way)
            self.parts.append(self.held[way])
            self.steps.append(-way * self.hop % self.ring.count)
        return list(self.held.values())

    def finish(self):
        while self.hop < self.ring.hops[0]:
            self.advance()
        return self

    def whole(self):
        block = self.parts[0]
        rows = block.shape[0]
        found = jnp.zeros((rows * self.ring.count, block.shape[1]), block.dtype)
        starts = self.ring.places * rows
        for step, part in zip(self.steps, self.parts):
            found = lax.dynamic_update_slice(
                found, part, (starts[step], 0), allow_negative_indices=False
            )
        return found


class Reduce:
    def __init__(self, ring, whole):
        self.ring, self.source, self.hop = ring, whole, ring.hops[0]
        self.rows = whole.shape[0] // ring.count
        self.starts = ring.places * self.rows
        self.held = {way: self.piece(way * last) for way, last in zip((1, -1), ring.hops)}
        self.total = None

    def piece(self, step):
        return lax.dynamic_slice(
            self.source,
            (self.starts[step % self.ring.count], 0),
            (self.rows, self.source.shape[1]),
            allow_negative_indices=False,
        )

    def tokens(self):
        return list(self.held.values())

    def send(self, *tokens):
        self.came = {
            way: self.ring.send(tie(self.held[way], *tokens), way) for way in self.ring.ways(self.hop)
        }
        return self

    def absorb(self, *tokens):
        for way, came in self.came.items():
            came = tie(came, *tokens) if tokens else came
            if self.hop > 1:
                self.held[way] = add_low(came, self.piece(way * (self.hop - 1)))
            else:
                mine = self.piece(0) if self.total is None else self.total
                self.total = mine.astype(jnp.float32) + came.astype(jnp.float32)
        self.hop -= 1
        return self.tokens() if self.total is None else [self.total]

    def finish(self):
        while self.hop > 0:
            self.send().absorb()
        return self.total


LOW = jnp.bfloat16
F32 = jnp.float32
TILE = 256
LONG = 6
SHORT = 2
GELU_A = 0.7978845608028654
GELU_B = 0.044715
VMEM = 36 * 2**20


def mm(a, b):
    return jnp.dot(a, b, preferred_element_type=F32)


def mm_nt(a, b):
    return lax.dot_general(a, b, (((1,), (1,)), ((), ())), preferred_element_type=F32)


def mm_tn(a, b):
    return lax.dot_general(a, b, (((0,), (0,)), ((), ())), preferred_element_type=F32)


def call(body, out_shape, in_specs, out_specs, args, grid=(1,), flops=0, scratch=(), into=(), prefetch=()):
    given = len(prefetch)
    used = len(in_specs)

    def kernel(*refs):
        body(*refs[: given + used], *refs[given + used + len(into) :])

    nbytes = sum(a.size * a.dtype.itemsize for a in args)
    nbytes += sum(o.size * o.dtype.itemsize for o in jax.tree.leaves(out_shape))
    return pl.pallas_call(
        kernel,
        out_shape=out_shape,
        grid_spec=pltpu.PrefetchScalarGridSpec(
            num_scalar_prefetch=given,
            grid=grid,
            in_specs=list(in_specs) + [pl.BlockSpec(memory_space=pl.ANY)] * len(into),
            out_specs=out_specs,
            scratch_shapes=list(scratch),
        ),
        compiler_params=pltpu.CompilerParams(vmem_limit_bytes=VMEM),
        cost_estimate=pl.CostEstimate(flops=flops // 16, bytes_accessed=nbytes // 16, transcendentals=0),
        input_output_aliases={given + used + i: i for i in range(len(into))},
    )(*prefetch, *args, *into)


def held(shape):
    return pl.BlockSpec(shape, lambda *_: (0,) * len(shape), pipeline_mode=pl.Buffered(1))


def like(shape, dtype):
    return jax.ShapeDtypeStruct(shape, dtype)


def scale_of(v):
    return lax.rsqrt(jnp.mean(v * v, axis=-1, keepdims=True) + EPSILON)


def norm_pull(v, s, g, dy):
    w = dy * g
    return s * w - v * (s * s * s) * jnp.mean(w * v, axis=-1, keepdims=True)


def turn(v, cos_t, sin_t, sign):
    half = v.shape[-1] // 2
    a, b = v[:, :half], v[:, half:]
    return jnp.concatenate([a * cos_t - sign * (b * sin_t), b * cos_t + sign * (a * sin_t)], axis=-1)


def stored_block(p):
    return jnp.where(p < 4, 2 * p, 2 * (7 - p) + 1)


def padded(rows):
    return -(-rows // 16) * 16


def pack_columns(w_gate_up, dp, ctx):
    rows, wide = w_gate_up.shape
    ff = wide // 2
    step = ff // (dp * ctx)
    room = padded(step)
    part = dp * room

    def body(w, out):
        zeros = [jnp.zeros((rows, room - step), F32)] if room > step else []
        for c in range(ctx):
            for side in range(2):
                cut = []
                for d in range(dp):
                    at = side * ff + (d * ctx + c) * step
                    cut += [w[:, at : at + step]] + zeros
                out[c, :, side * part : (side + 1) * part] = jnp.concatenate(cut, axis=1).astype(LOW)

    return call(
        body,
        like((ctx, rows, 2 * part), LOW),
        [held((rows, wide))],
        held((ctx, rows, 2 * part)),
        (w_gate_up,),
    )


def unpack_columns(parts, dp, ctx, step):
    rows, wide = parts.shape[1], parts.shape[2]
    part = wide // 2
    room = part // dp
    ff = dp * ctx * step

    def body(p, out):
        for c in range(ctx):
            own = p[c].astype(F32)
            for side in range(2):
                for d in range(dp):
                    at = side * ff + (d * ctx + c) * step
                    start = side * part + d * room
                    out[:, at : at + step] = own[:, start : start + step]

    return call(
        body,
        like((rows, 2 * ff), F32),
        [held(parts.shape)],
        held((rows, 2 * ff)),
        (parts,),
    )


class Blocks:
    def __init__(self, gathered, rows=None):
        block, self.cols = gathered.parts[0].shape
        self.rows = rows = rows or block
        count = gathered.ring.count
        self.height = rows * count
        if rows % 16:
            whole = gathered.whole().reshape(count, block, self.cols)[:, :rows]
            self.parts, self.steps = [whole.reshape(self.height, self.cols)], [0]
            self.rows = self.height
        else:
            self.parts, self.steps = gathered.parts, gathered.steps

    def specs(self):
        return [pl.BlockSpec(memory_space=pl.ANY)] * len(self.parts)

    def scratch(self):
        return [
            pltpu.VMEM((self.height, self.cols), LOW),
            pltpu.SemaphoreType.DMA((len(self.parts),)),
        ]

    def load(self, places, refs, room, sems):
        @pl.when(pl.program_id(0) == 0)
        def _():
            copies = []
            for i, (step, ref) in enumerate(zip(self.steps, refs)):
                at = pl.multiple_of(places[step] * self.rows, 16) if len(refs) > 1 else 0
                copies.append(
                    pltpu.make_async_copy(
                        ref.at[pl.ds(0, self.rows), :], room.at[pl.ds(at, self.rows), :], sems.at[i]
                    )
                )
            for copy in copies:
                copy.start()
            for copy in copies:
                copy.wait()


def unpack_small(gathered, first, dp, ctx, out_rows, gain_cols, head_cols):
    block, wide = gathered.parts[0].shape
    rows = block - first
    direct = first % 16 == 0 and rows % 16 == 0
    if direct:
        parts, steps = gathered.parts, gathered.steps
    else:
        parts, steps = [gathered.whole().reshape(dp, block, wide)[:, first:]], [0]
    half = out_rows // 2
    count = len(parts)

    def body(places, *refs):
        gain, head, out, room, sems = refs[count:]
        copies = []
        for i, ref in enumerate(refs[:count]):
            if direct:
                source, target = ref.at[pl.ds(first, rows), :], room.at[places[steps[i]]]
            else:
                source, target = ref, room
            copies.append(pltpu.make_async_copy(source, target, sems.at[i]))
        for copy in copies:
            copy.start()
        for copy in copies:
            copy.wait()
        lines = []
        for d in range(dp):
            extra = room[d, : 4 * ctx, :].astype(F32)
            lines += [extra[4 * c : 4 * c + 1] for c in range(ctx)]
            at, own = d * out_rows, room[d, 4 * ctx :, :]
            out[at : at + out_rows, :wide] = own[:out_rows]
            out[at : at + half, wide:] = own[out_rows:, : D - wide]
            out[at + half : at + out_rows, wide:] = own[out_rows:, D - wide :]
        for g in range(4):
            cut = [line[:, g * gain_cols : (g + 1) * gain_cols] for line in lines]
            gain[g : g + 1, :] = jnp.concatenate(cut, axis=1)
        for g in range(2):
            at = 4 * gain_cols + g * head_cols
            cut = [line[:, at : at + head_cols] for line in lines]
            head[g : g + 1, :] = jnp.concatenate(cut, axis=1)

    return call(
        body,
        [like((4, D), F32), like((2, HD), F32), like((HD, D), LOW)],
        [pl.BlockSpec(memory_space=pl.ANY)] * count,
        [held((4, D)), held((2, HD)), held((HD, D))],
        tuple(parts),
        scratch=[pltpu.VMEM((dp, rows, wide), LOW), pltpu.SemaphoreType.DMA((count,))],
        prefetch=(gathered.ring.places,),
    )


def input_stage(x, w_in, gain, head_rows, cos_t, sin_t, row_map, places):
    seq = x.shape[0]
    count = len(w_in.parts)

    def body(_, pl_ref, x0, x1, g, hg, cos, sin, *refs):
        q, k, v, raw, n_ref, w, sems = refs[count:]
        w_in.load(pl_ref, refs[:count], w, sems)
        for i, x_ref in enumerate((x0, x1)):
            at = slice(i * TILE, (i + 1) * TILE)
            xf = x_ref[...].astype(F32)
            n = (xf * scale_of(xf) * g[...]).astype(LOW)
            n_ref[at, :] = n
            y = mm(n, w[...])
            qy, ky = y[:, :HD], y[:, HD : 2 * HD]
            raw[at, :] = y[:, : 2 * HD]
            c, s = cos[at, :], sin[at, :]
            q[at, :] = turn(qy * scale_of(qy) * hg[0:1], c, s, 1.0).astype(LOW)
            k[at, :] = turn(ky * scale_of(ky) * hg[1:2], c, s, 1.0).astype(LOW)
            v[at, :] = y[:, 2 * HD :].astype(LOW)

    def block(cols):
        return pl.BlockSpec((2 * TILE, cols), lambda p, m, s: (p, 0))

    return call(
        body,
        [like((seq, HD), LOW)] * 3 + [like((seq, 2 * HD), F32), like((seq, D), LOW)],
        [
            pl.BlockSpec((TILE, D), lambda p, m, s: (m[2 * p], 0)),
            pl.BlockSpec((TILE, D), lambda p, m, s: (m[2 * p + 1], 0)),
            held((1, D)),
            held((2, HD)),
            block(HD // 2),
            block(HD // 2),
        ]
        + w_in.specs(),
        [block(HD)] * 3 + [block(2 * HD), block(D)],
        (x, x, gain, head_rows, cos_t, sin_t, *w_in.parts),
        grid=(seq // TILE // 2,),
        flops=2 * seq * D * 3 * HD,
        scratch=w_in.scratch(),
        prefetch=(row_map, places),
    )


def scores_of(q, k, doc_step):
    s = mm_nt(q, k) * HD ** (-0.5)
    row = lax.broadcasted_iota(jnp.int32, s.shape, 0) + doc_step * TILE
    col = lax.broadcasted_iota(jnp.int32, s.shape, 1)
    return jnp.where(col <= row, s, -1e30)


def attention(q, k, v, base):
    seq = q.shape[0]

    def body(b, q_ref, k_ref, v_ref, mixed, lse):
        for doc, count in enumerate((LONG, SHORT)):
            first = b[doc]
            for i in range(count):
                p = first + i
                at = pl.ds(pl.multiple_of(p * TILE, TILE), TILE)
                keys = pl.ds(pl.multiple_of(first * TILE, TILE), (i + 1) * TILE)
                s = scores_of(q_ref[at, :], k_ref[keys, :], i)
                peak = jnp.max(s, axis=-1, keepdims=True)
                e = jnp.exp(s - peak)
                total = jnp.sum(e, axis=-1, keepdims=True)
                lse[at, :] = peak + jnp.log(total)
                probs = (e * (1.0 / total)).astype(LOW)
                to = pl.ds(pl.multiple_of(stored_block(p) * TILE, TILE), TILE)
                mixed[to, :] = mm(probs, v_ref[keys, :]).astype(LOW)

    return call(
        body,
        [like((seq, HD), LOW), like((seq, 1), F32)],
        [held((seq, HD))] * 3,
        [held((seq, HD)), held((seq, 1))],
        (q, k, v),
        flops=4 * 24 * TILE * TILE * HD,
        prefetch=(base,),
    )


def attention_back(q, k, v, raw, lse, grads, head_rows, cos_t, sin_t, base):
    seq = q.shape[0]
    chip = seq // 2

    def pull_head(v_raw, g, dy, cos, sin):
        dy = turn(dy, cos, sin, -1.0)
        s = scale_of(v_raw)
        return norm_pull(v_raw, s, g, dy), jnp.sum(dy * v_raw * s, axis=0, keepdims=True)

    def body(b, q_ref, k_ref, v_ref, raw_ref, l_ref, *refs):
        hg, cos, sin, out, head_out, dk, dv, mixed_grad = refs[6:]
        for i in range(2):
            mine, near, far = refs[3 * i : 3 * i + 3]
            rows = pl.ds(pl.multiple_of((b[2] if i == 0 else 1 - b[2]) * chip, chip), chip)
            mixed_grad[rows, :] = (
                mine[0].astype(F32) + near[0].astype(F32) + far[...].astype(F32)
            ).astype(LOW)
        dk[...] = jnp.zeros_like(dk)
        dv[...] = jnp.zeros_like(dv)
        head_q = jnp.zeros((1, HD), F32)
        for doc, count in enumerate((LONG, SHORT)):
            first = b[doc]
            for i in range(count):
                p = first + i
                at = pl.ds(pl.multiple_of(p * TILE, TILE), TILE)
                keys = pl.ds(pl.multiple_of(first * TILE, TILE), (i + 1) * TILE)
                src = pl.ds(pl.multiple_of(stored_block(p) * TILE, TILE), TILE)
                do = mixed_grad[src, :]
                qs = q_ref[at, :]
                probs = jnp.exp(scores_of(qs, k_ref[keys, :], i) - l_ref[at, :])
                dp = mm_nt(do, v_ref[keys, :])
                inner = jnp.sum(probs * dp, axis=-1, keepdims=True)
                ds = (probs * (dp - inner)).astype(LOW)
                dq = mm(ds, k_ref[keys, :]) * HD ** (-0.5)
                dk[keys, :] += mm_tn(ds, qs)
                dv[keys, :] += mm_tn(probs.astype(LOW), do)
                dq, part = pull_head(raw_ref[at, :HD], hg[0:1], dq, cos[at, :], sin[at, :])
                head_q += part
                out[at, :HD] = dq.astype(LOW)
        head_k = jnp.zeros((1, HD), F32)
        for p in range(seq // TILE):
            at = slice(p * TILE, (p + 1) * TILE)
            dkp, part = pull_head(
                raw_ref[at, HD:], hg[1:2], dk[at, :] * HD ** (-0.5), cos[at, :], sin[at, :]
            )
            head_k += part
            out[at, HD : 2 * HD] = dkp.astype(LOW)
            out[at, 2 * HD :] = dv[at, :].astype(LOW)
        head_out[0:1, :] = head_q
        head_out[1:2, :] = head_k

    pair = pl.BlockSpec((1, chip, HD), lambda *_: (0, 0, 0), pipeline_mode=pl.Buffered(1))
    return call(
        body,
        [like((seq, 3 * HD), LOW), like((2, HD), F32)],
        [held((seq, HD))] * 3
        + [held((seq, 2 * HD)), held((seq, 1))]
        + [pair, pair, held((chip, HD))] * 2
        + [held((2, HD))]
        + [held((seq, HD // 2))] * 2,
        [held((seq, 3 * HD)), held((2, HD))],
        (q, k, v, raw, lse, *grads, head_rows, cos_t, sin_t),
        flops=10 * 24 * TILE * TILE * HD,
        scratch=[pltpu.VMEM((seq, HD), F32)] * 2 + [pltpu.VMEM((seq, HD), LOW)],
        prefetch=(base,),
    )


def project(mixed, outs, x, gains, stored_map):
    seq = x.shape[0]

    def body(_, m0, m1, m2, m3, w0, w1, w2, w3, x_ref, g, proj, pre):
        for i in range(2):
            at = slice(i * TILE, (i + 1) * TILE)
            y = mm(m0[at, :], w0[...]) + mm(m1[at, :], w1[...])
            y = y + mm(m2[at, :], w2[...]) + mm(m3[at, :], w3[...])
            proj[at, :] = y
            r = x_ref[at, :].astype(F32) + y * scale_of(y) * g[1:2]
            pre[at, :] = (r * scale_of(r) * g[2:3]).astype(LOW)

    def block(cols):
        return pl.BlockSpec((2 * TILE, cols), lambda r, m: (r, 0))

    return call(
        body,
        [like((seq, D), F32), like((seq, D), LOW)],
        [pl.BlockSpec((2 * TILE, HD), lambda r, m: (m[2 * r] // 2, 0))] * 4
        + [held((HD, D))] * 4
        + [block(D), held((4, D))],
        [block(D), block(D)],
        (*mixed, *outs, x, gains),
        grid=(seq // TILE // 2,),
        flops=2 * seq * D * H * HD,
        prefetch=(stored_map,),
    )


def column_cuts(main, width):
    return [(at, min(width, main - at)) for at in range(0, main, width)]


def gate_stage(pre, w, places, half, into=()):
    seq, part = pre.shape[0], w.cols // 2
    rows = 512
    first = half * (seq // 2 // rows)
    count = len(w.parts)

    def pieces(g, u):
        t = jnp.tanh(GELU_A * (g + GELU_B * (g * g * g)))
        a = 0.5 * g * (1.0 + t)
        slope = 0.5 * (1.0 + t) + (0.5 * g) * (1.0 - t * t) * (GELU_A * (1.0 + 3.0 * GELU_B * (g * g)))
        return a * u, u * slope, a

    def body(pl_ref, p_ref, *refs):
        hidden, ab, room, sems = refs[count:]
        w.load(pl_ref, refs[:count], room, sems)
        p = p_ref[...]

        def multiply(at, wide):
            return mm(p, room[:, at : at + wide]), mm(p, room[:, part + at : part + at + wide])

        def finish(at, wide, made):
            h, b, a = pieces(*made)
            hidden[:, at : at + wide] = h.astype(LOW)
            ab[:, at : at + wide] = b.astype(LOW)
            ab[:, part + at : part + at + wide] = a.astype(LOW)

        last = None
        for cut in column_cuts(part, 256):
            made = multiply(*cut)
            if last is not None:
                finish(*last)
            last = (*cut, made)
        finish(*last)

    def block(cols):
        return pl.BlockSpec((rows, cols), lambda r, m: (first + r, 0))

    return call(
        body,
        [like((seq, part), LOW), like((seq, 2 * part), LOW)],
        [block(D)] + w.specs(),
        [block(part), block(2 * part)],
        (pre, *w.parts),
        grid=(seq // 2 // rows,),
        flops=2 * seq * D * part,
        scratch=w.scratch(),
        into=into,
        prefetch=(places,),
    )


def down_stage(hidden, w, places, half):
    seq, part = hidden.shape
    rows = seq // 4
    count = len(w.parts)

    def body(pl_ref, h, *refs):
        even, odd, room, sems = refs[count:]
        w.load(pl_ref, refs[:count], room, sems)
        odd[...] = mm(h[rows:, :], room[...]).astype(LOW)
        even[...] = mm(h[:rows, :], room[...]).astype(LOW)

    return call(
        body,
        [like((rows, D), LOW)] * 2,
        [
            pl.BlockSpec(
                (2 * rows, part), lambda r, m: (half, 0), pipeline_mode=pl.Buffered(1)
            )
        ]
        + w.specs(),
        [held((rows, D))] * 2,
        (hidden, *w.parts),
        flops=4 * rows * D * part,
        scratch=w.scratch(),
        prefetch=(places,),
    )


def ffn_stage(parts, near, far, proj, x, cot, gains):
    rows = cot.shape[0]

    def body(p, n, f, proj_ref, x_ref, c_ref, g, out, grad, gain):
        y = p[...].astype(F32) + n[...].astype(F32) + f[...].astype(F32)
        pr = proj_ref[...]
        s = scale_of(y)
        r = x_ref[...].astype(F32) + pr * scale_of(pr) * g[1:2]
        out[...] = (r + y * s * g[3:4]).astype(LOW)
        dy = c_ref[...].astype(F32)
        grad[...] = norm_pull(y, s, g[3:4], dy).astype(LOW)
        part = jnp.sum(dy * y * s, axis=0, keepdims=True)

        @pl.when(pl.program_id(0) == 0)
        def _():
            gain[...] = part

        @pl.when(pl.program_id(0) > 0)
        def _():
            gain[...] += part

    block = pl.BlockSpec((TILE, D), lambda r: (r, 0))
    return call(
        body,
        [like((rows, D), LOW), like((rows, D), LOW), like((1, D), F32)],
        [block] * 6 + [held((4, D))],
        [block, block, held((1, D))],
        (parts, near, far, proj, x, cot, gains),
        grid=(rows // TILE,),
    )


def hidden_back(grad, w, ab, places, half, into=()):
    seq, part = ab.shape[0], ab.shape[1] // 2
    rows = 512
    first = half * (seq // 2 // rows)
    count = len(w.parts)

    def body(pl_ref, g_ref, ab_ref, *refs):
        out, room, sems = refs[count:]
        w.load(pl_ref, refs[:count], room, sems)
        g = g_ref[...]
        for at, wide in column_cuts(part, 256):
            hg = mm_nt(g, room[at : at + wide, :])
            for side in (at, part + at):
                out[:, side : side + wide] = (hg * ab_ref[:, side : side + wide].astype(F32)).astype(LOW)

    def block(cols):
        return pl.BlockSpec((rows, cols), lambda r, m: (first + r, 0))

    return call(
        body,
        [like((seq, 2 * part), LOW)],
        [pl.BlockSpec((rows, D), lambda r, m: (r, 0)), block(2 * part)] + w.specs(),
        [block(2 * part)],
        (grad, ab, *w.parts),
        grid=(seq // 2 // rows,),
        flops=seq * D * part,
        scratch=w.scratch(),
        into=into,
        prefetch=(places,),
    )[0]


def residual_back(gu, w, outs, proj, x, cot, gains, stored_map, places, half, into=()):
    seq, wide = gu.shape
    own = cot.shape[0] // TILE
    steps = seq // 2 // TILE
    first = half * steps
    count = len(w.parts)

    def body(_, pl_ref, gu_ref, w0, w1, w2, w3, proj_ref, x_ref, c_ref, g, *refs):
        rg, pg, even, odd, gain, room, sems, *made = refs[count:]
        w.load(pl_ref, refs[:count], room, sems)
        step = pl.program_id(0)

        def multiply(turn):
            made[turn][...] = mm_nt(gu_ref[...], room[...])

        def finish(turn):
            dy = made[turn][...]
            pr = proj_ref[...]
            sp = scale_of(pr)
            r = x_ref[...].astype(F32) + pr * sp * g[1:2]
            s = scale_of(r)
            dr = norm_pull(r, s, g[2:3], dy)
            if half == 0:
                dr = dr + jnp.where(step <= own, 1.0, 0.0) * c_ref[...].astype(F32)
            rg[...] = dr.astype(LOW)
            low = norm_pull(pr, sp, g[1:2], dr).astype(LOW)
            pg[...] = low
            even[0] = mm_nt(low, w0[...]).astype(LOW)
            odd[0] = mm_nt(low, w1[...]).astype(LOW)
            even[1] = mm_nt(low, w2[...]).astype(LOW)
            odd[1] = mm_nt(low, w3[...]).astype(LOW)
            before = jnp.where(step == 1, 0.0, gain[...])
            gain[0:1, :] = before[0:1] + jnp.sum(dr * pr * sp, axis=0, keepdims=True)
            gain[1:2, :] = before[1:2] + jnp.sum(dy * r * s, axis=0, keepdims=True)

        @pl.when(step == 0)
        def _():
            multiply(0)

        for turn in range(2):

            @pl.when((step > 0) & (step < steps) & (step % 2 == turn))
            def _():
                multiply(turn)
                finish(1 - turn)

        @pl.when(step == steps)
        def _():
            finish((steps - 1) % 2)

    def last(i):
        return jnp.maximum(i - 1, 0)

    def block(cols):
        return pl.BlockSpec((TILE, cols), lambda i, m, p: (first + last(i), 0))

    heads = pl.BlockSpec((2, TILE, HD), lambda i, m, p: (0, m[first + last(i)] % steps, 0))
    return call(
        body,
        [like((seq, D), LOW), like((seq, D), LOW)]
        + [like((2, seq // 2, HD), LOW)] * 2
        + [like((2, D), F32)],
        [pl.BlockSpec((TILE, wide), lambda i, m, p: (first + jnp.minimum(i, steps - 1), 0))]
        + [held((HD, D))] * 4
        + [block(D), block(D)]
        + [pl.BlockSpec((TILE, D), lambda i, m, p: (jnp.minimum(last(i), own - 1), 0)), held((4, D))]
        + w.specs(),
        [
            block(D),
            pl.BlockSpec((TILE, D), lambda i, m, p: (m[first + last(i)], 0)),
            heads,
            heads,
            held((2, D)),
        ],
        (gu, *outs, proj, x, cot, gains, *w.parts),
        grid=(steps + 1,),
        flops=seq * D * (wide + H * HD),
        scratch=w.scratch() + [pltpu.VMEM((TILE, D), F32)] * 2,
        into=into,
        prefetch=(stored_map, places),
    )


def input_back(qkv, w_in, x, rg, gain, pos_map, places):
    seq = x.shape[0]
    rows = 2 * TILE
    count = len(w_in.parts)

    def body(_, pl_ref, q0, q1, x_ref, rg_ref, g, *refs):
        even, odd, gain_out, w, sems = refs[count:]
        w_in.load(pl_ref, refs[:count], w, sems)
        step = pl.program_id(0)
        total = jnp.zeros((1, D), F32)
        made = []
        for i, q_ref in enumerate((q0, q1)):
            at = slice(i * TILE, (i + 1) * TILE)
            dy = mm_nt(q_ref[...], w[...])
            xf = x_ref[at, :].astype(F32)
            s = scale_of(xf)
            made.append((rg_ref[at, :].astype(F32) + norm_pull(xf, s, g[...], dy)).astype(LOW))
            total += jnp.sum(dy * xf * s, axis=0, keepdims=True)
        gain_out[...] = jnp.where(step == 0, 0.0, gain_out[...]) + total

        @pl.when(step % 2 == 0)
        def _():
            even[:TILE, :], even[TILE:, :] = made

        @pl.when(step % 2 == 1)
        def _():
            odd[:TILE, :], odd[TILE:, :] = made

    block = pl.BlockSpec((rows, D), lambda i, m, s: (i, 0))
    out = pl.BlockSpec((rows, D), lambda i, m, s: (i // 2, 0))
    return call(
        body,
        [like((seq // 2, D), LOW)] * 2 + [like((1, D), F32)],
        [
            pl.BlockSpec((TILE, 3 * HD), lambda i, m, s: (m[2 * i], 0)),
            pl.BlockSpec((TILE, 3 * HD), lambda i, m, s: (m[2 * i + 1], 0)),
            block,
            block,
            held((1, D)),
        ]
        + w_in.specs(),
        [out, out, held((1, D))],
        (qkv, qkv, x, rg, gain, *w_in.parts),
        grid=(seq // rows,),
        flops=2 * seq * D * 3 * HD,
        scratch=w_in.scratch(),
        prefetch=(pos_map, places),
    )


def local(
    tokens,
    cotangent,
    lengths,
    w_qkv,
    w_out,
    w_gate_up,
    w_down,
    gains,
    head_gains,
    first_qkv,
    first_out,
    first_gate_up,
    first_down,
    first_gains,
    first_head,
    second_qkv,
    second_out,
    second_gate_up,
    second_down,
    second_gains,
    second_head,
):
    low = jnp.bfloat16
    f32 = jnp.float32
    rows = tokens.shape[1]
    dp = lax.axis_size("dp")
    ctx = lax.axis_size("ctx")
    place = lax.axis_index("ctx")
    seq = rows * ctx
    in_rows = w_qkv.shape[0]
    out_rows = w_out.shape[0]
    ff_rows = w_down.shape[0]
    gain_cols = gains.shape[1]
    head_cols = head_gains.shape[1]
    qkv_cols = 3 * HD
    ring = Ring()

    q_cols = w_qkv[:, : H * HD].astype(low).reshape(in_rows, ctx, HD).transpose(1, 0, 2)
    kv_cols = jnp.broadcast_to(w_qkv[:, H * HD :].astype(low)[None], (ctx, in_rows, 2 * HD))
    extra = jnp.concatenate(
        [gains.astype(low).reshape(-1), head_gains.astype(low).reshape(-1)]
    )
    extra = jnp.pad(extra, (0, 4 * qkv_cols - extra.shape[0])).reshape(4, qkv_cols)
    small_sent = jnp.concatenate(
        [
            jnp.concatenate([q_cols, kv_cols], axis=2),
            jnp.broadcast_to(extra[None], (ctx, 4, qkv_cols)),
        ],
        axis=1,
    )
    to_user = [((dp * c + d), d * ctx + c) for d in range(dp) for c in range(ctx)]
    to_owner = [(b, a) for a, b in to_user]
    out_mine = lax.ppermute(w_out.astype(low), ("dp", "ctx"), to_user)
    half = out_rows // 2
    small = exchange(small_sent, "ctx")
    packed = pack_columns(tie(w_gate_up, small_sent), dp, ctx)
    own_rows = ctx * in_rows
    small_ring = Gather(
        ring,
        jnp.concatenate(
            [
                small[:, :in_rows].reshape(own_rows, qkv_cols),
                small[:, in_rows:].reshape(4 * ctx, qkv_cols),
                out_mine[:, :qkv_cols],
                jnp.concatenate([out_mine[:half, qkv_cols:], out_mine[half:, qkv_cols:]], axis=1),
            ]
        ),
    )
    down_block = jnp.pad(w_down.astype(low), ((0, padded(ff_rows) - ff_rows), (0, 0)))
    down_ring = Gather(ring, down_block)
    down_first = down_ring.advance()
    tokens_far = swap(tie(tokens[0], small), 2)
    tokens_near = swap(tie(tokens[0], small), 1)
    gate_up_cols = exchange(tie(packed, tokens_far), "ctx").reshape(own_rows, -1)
    first_len = lengths[0, 0]
    pos = tie(jnp.arange(seq, dtype=jnp.int32), packed)
    cos_t, sin_t = rope_tables(pos - jnp.where(pos < first_len, 0, first_len), HD)
    small_ring.advance(*down_first)
    small_ring.advance(cos_t, sin_t)
    tokens_last = swap(tie(tokens_far, *small_ring.held.values()), 1)
    tokens_all = jnp.concatenate([tokens[0], tokens_near, tokens_far, tokens_last])
    while small_ring.hop < ring.hops[0]:
        small_ring.advance()
    small_seen = list(small_ring.held.values())
    gate_ring = Gather(ring, gate_up_cols)
    gate_seen = gate_ring.advance(*small_seen, tokens_last)
    w_in = Blocks(small_ring, own_rows)
    places = ring.places
    gain_rows, head_rows, out_mine = unpack_small(
        small_ring, own_rows, dp, ctx, out_rows, gain_cols, head_cols
    )
    out_far, out_near = swap(out_mine, 2), swap(out_mine, 1)

    blocks = seq // TILE
    split = first_len // TILE
    base = jnp.where(split == LONG, jnp.array([0, LONG, 0]), jnp.array([SHORT, 0, 0]))
    base = (base + jnp.array([0, 0, 1]) * (place // 2)).astype(jnp.int32)
    tiles = jnp.arange(blocks, dtype=jnp.int32)
    stored_map = 2 * (place ^ (tiles // 2)) + tiles % 2
    owner = jnp.where(tiles < ctx, tiles, 2 * ctx - 1 - tiles)
    row_map = 2 * (place ^ owner) + (tiles >= ctx)
    pos_map = jnp.where(tiles % 2 == 0, stored_map // 2, 2 * ctx - 1 - stored_map // 2)

    q, k, v, raw, normed = input_stage(
        tokens_all, w_in, gain_rows[0:1], head_rows, cos_t, sin_t, row_map, places
    )
    down_second = down_ring.advance(q, *gate_seen)
    gate_second = gate_ring.advance(q)
    mixed, lse = attention(tie(q, *gate_seen, out_far, out_near), k, v, base)
    mixed = tie(mixed, *down_second)
    mixed_far, mixed_near = swap(mixed, 2), swap(mixed, 1)
    out_parts = [out_mine, out_near, out_far, swap(tie(out_far, mixed), 1)]
    down_ring.advance(mixed)
    gate_ring.advance(mixed)
    mixed_parts = [mixed, mixed_near, mixed_far, swap(tie(mixed_far, *gate_second), 1)]
    proj, pre_low = project(mixed_parts, out_parts, tokens_all, gain_rows, stored_map)
    while gate_ring.hop < ring.hops[0]:
        gate_ring.advance(pre_low)
        if down_ring.hop < ring.hops[0]:
            down_ring.advance(pre_low)
    down_ring.finish()
    full_gate_up = Blocks(gate_ring)
    full_down = Blocks(down_ring)
    buffers = gate_stage(pre_low, full_gate_up, places, 1)
    even, odd = down_stage(buffers[0], full_down, places, 1)
    summed = add_low(even, swap(odd, 1))
    far = swap(summed, 2)
    hidden_low, slopes = gate_stage(tie(pre_low, summed), full_gate_up, places, 0, buffers)
    even, odd = down_stage(tie(hidden_low, far), full_down, places, 0)
    near = swap(odd, 1)
    result, ffn_grad, gain_grad_d = ffn_stage(
        even, near, far, proj, tokens[0], cotangent[0], gain_rows
    )

    far = swap(ffn_grad, 2)
    ffn_here = jnp.concatenate([ffn_grad, swap(ffn_grad, 1)])
    residual = partial(
        residual_back,
        w=full_gate_up,
        outs=out_parts,
        proj=proj,
        x=tokens_all,
        cot=cotangent[0],
        gains=gain_rows,
        stored_map=stored_map,
        places=places,
    )
    gate_up_low = hidden_back(ffn_here, full_down, slopes, places, 0)
    far = tie(far, gate_up_low)
    ffn_there = jnp.concatenate([far, swap(far, 1)])
    gate_up_low = hidden_back(ffn_there, full_down, slopes, places, 1, (gate_up_low,))
    grad_gate_up = mm_tn(pre_low, gate_up_low).astype(low)
    gate_sum = Reduce(ring, grad_gate_up).send()
    resid_grad, proj_low, even, odd, gain_grad_here = residual(
        tie(gate_up_low, *gate_sum.tokens()), half=0
    )
    held_gate = gate_sum.absorb(resid_grad)
    near = swap(tie(odd, *held_gate), 1)
    parts_here = (even, near)
    summed = add_low(even[1], near[1])
    far_there = swap(summed, 2)
    gate_sum.send()
    ffn_low = jnp.concatenate([ffn_here, ffn_there])
    grad_down = mm_tn(hidden_low, tie(ffn_low, summed, *held_gate)).astype(low)
    down_sum = Reduce(ring, grad_down).send()
    resid_grad, proj_low, even, odd, gain_grad_there = residual(
        tie(gate_up_low, far_there, *down_sum.tokens()), half=1, into=(resid_grad, proj_low)
    )
    near = swap(tie(odd, *gate_sum.came.values(), *down_sum.came.values()), 1)
    summed = add_low(even[1], near[1])
    far_here = swap(summed, 2)
    held_gate = gate_sum.absorb(odd)
    held_down = down_sum.absorb(odd)
    gate_sum.send()
    down_sum.send()
    proj_low = tie(proj_low, *held_gate, *held_down)
    grad_out = [mm_tn(m, proj_low).astype(low) for m in mixed_parts]
    far_here = tie(far_here, *grad_out)
    grad_out = reduce_ctx(grad_out).astype(low)
    qkv_low, head_grads = attention_back(
        q,
        k,
        v,
        raw,
        lse,
        parts_here + (far_here,) + (even, near, far_there),
        head_rows,
        cos_t,
        sin_t,
        base,
    )
    grad_in = mm_tn(normed, qkv_low).astype(low)
    grad_out = grad_out.reshape(dp, out_rows, D)
    in_blocks = jnp.concatenate(
        [
            grad_in.reshape(dp, own_rows, qkv_cols),
            grad_out[:, :, :qkv_cols],
            jnp.concatenate(
                [grad_out[:, :half, qkv_cols:], grad_out[:, half:, qkv_cols:]], axis=2
            ),
        ],
        axis=1,
    )
    in_sum = Reduce(ring, in_blocks.reshape(-1, qkv_cols))
    held_gate = gate_sum.absorb(*in_sum.tokens())
    held_down = down_sum.absorb(*in_sum.tokens())
    in_sum.send()
    gate_sum.send()
    down_sum.send()
    held_in = in_sum.absorb(*held_gate, *held_down)
    in_sum.send()
    input_even, input_odd, gain_grad_a = input_back(
        tie(qkv_low, *held_in),
        w_in,
        tokens_all,
        resid_grad,
        gain_rows[0:1],
        pos_map,
        places,
    )
    gate_came = list(gate_sum.came.values())
    in_sum.absorb(input_odd)
    in_sum.send(*gate_came)
    gate_sum.absorb(input_odd)
    down_sum.absorb(input_odd)
    gate_up_own = gate_sum.finish().astype(low)
    gate_up_own = exchange(gate_up_own.reshape(ctx, in_rows, -1), "ctx")
    near = swap(tie(input_odd, *gate_came), 1)
    summed = add_low(input_even[rows:], near[rows:])
    gain_grad_bc = gain_grad_here + gain_grad_there
    while in_sum.hop > 1:
        in_sum.absorb()
        in_sum.send()

    in_own = in_sum.absorb()[0].astype(low)
    down_sum.send(in_own)
    down_sum.absorb()
    down_own = down_sum.finish()[:ff_rows]
    out_own = in_own[own_rows:]
    out_own = jnp.concatenate(
        [
            out_own[:out_rows],
            jnp.concatenate(
                [out_own[out_rows:, : D - qkv_cols], out_own[out_rows:, D - qkv_cols :]], axis=0
            ),
        ],
        axis=1,
    )
    out_own = lax.ppermute(out_own, ("dp", "ctx"), to_owner).astype(f32)
    in_own = exchange(
        tie(in_own[:own_rows], gate_up_own, down_own).reshape(ctx, in_rows, qkv_cols), "ctx"
    ).astype(f32)
    far = swap(tie(summed, gate_up_own, in_own), 2)
    input_grad = (
        input_even[:rows].astype(f32) + near[:rows].astype(f32) + far.astype(f32)
    )
    gate_up_own = unpack_columns(gate_up_own, dp, ctx, ff_rows)
    qkv_own = jnp.concatenate(
        [
            in_own[:, :, :HD].transpose(1, 0, 2).reshape(in_rows, H * HD),
            jnp.sum(in_own[:, :, HD:], axis=0),
        ],
        axis=1,
    )
    gain_grads = jnp.concatenate([gain_grad_a, gain_grad_bc, gain_grad_d], axis=0)
    local_squares = jnp.float32(0.0)
    for piece in (qkv_own, out_own, gate_up_own, down_own):
        local_squares = local_squares + jnp.sum(piece * piece)
    lines = jnp.concatenate([gain_grads.reshape(-1, 128), head_grads.reshape(-1, 128)])
    squares = jnp.pad(local_squares.reshape(1, 1), ((0, 7), (0, 127)))
    sums = sum_others(jnp.concatenate([lines, squares]))
    sums = sums + swap(tie(sums, far), 2)
    small_grads = sums[: lines.shape[0]]
    index = lax.axis_index("dp") * ctx + place
    gains_own = lax.dynamic_slice_in_dim(
        small_grads[: 4 * D // 128].reshape(4, D), index * gain_cols, gain_cols, axis=1
    )
    head_own = lax.dynamic_slice_in_dim(
        small_grads[4 * D // 128 :].reshape(2, HD), index * head_cols, head_cols, axis=1
    )
    reduced = (qkv_own, out_own, gate_up_own, down_own, gains_own, head_own)
    total_squares = sums[lines.shape[0], 0] + jnp.sum(small_grads * small_grads)
    grad_norm = jnp.sqrt(total_squares)
    factor = 1.0 / jnp.maximum(grad_norm, 1.0)
    weights = (w_qkv, w_out, w_gate_up, w_down, gains, head_gains)
    firsts = (first_qkv, first_out, first_gate_up, first_down, first_gains, first_head)
    seconds = (second_qkv, second_out, second_gate_up, second_down, second_gains, second_head)
    rates = (D ** (-0.5), (H * HD) ** (-0.5), D ** (-0.5), FF ** (-0.5), GAIN_RATE, GAIN_RATE)
    decays = (WEIGHT_DECAY, WEIGHT_DECAY, WEIGHT_DECAY, WEIGHT_DECAY, 0.0, 0.0)
    updates = [
        adam_update(
            weights[index],
            firsts[index],
            seconds[index],
            reduced[index] * factor,
            rates[index],
            decays[index],
        )
        for index in range(6)
    ]
    return (
        result[None],
        input_grad[None],
        updates[0][0],
        updates[1][0],
        updates[2][0],
        updates[3][0],
        updates[4][0],
        updates[5][0],
        updates[0][1],
        updates[1][1],
        updates[2][1],
        updates[3][1],
        updates[4][1],
        updates[5][1],
        updates[0][2],
        updates[1][2],
        updates[2][2],
        updates[3][2],
        updates[4][2],
        updates[5][2],
        grad_norm,
    )


def solution(mesh):
    in_specs = (
        P("dp", "ctx", None),
        P("dp", "ctx", None),
        P("dp", None),
        P(("dp", "ctx"), None),
        P(("dp", "ctx"), None),
        P(("dp", "ctx"), None),
        P(("dp", "ctx"), None),
        P(None, ("dp", "ctx")),
        P(None, ("dp", "ctx")),
        P(("dp", "ctx"), None),
        P(("dp", "ctx"), None),
        P(("dp", "ctx"), None),
        P(("dp", "ctx"), None),
        P(None, ("dp", "ctx")),
        P(None, ("dp", "ctx")),
        P(("dp", "ctx"), None),
        P(("dp", "ctx"), None),
        P(("dp", "ctx"), None),
        P(("dp", "ctx"), None),
        P(None, ("dp", "ctx")),
        P(None, ("dp", "ctx")),
    )
    out_specs = (
        P("dp", "ctx", None),
        P("dp", "ctx", None),
        P(("dp", "ctx"), None),
        P(("dp", "ctx"), None),
        P(("dp", "ctx"), None),
        P(("dp", "ctx"), None),
        P(None, ("dp", "ctx")),
        P(None, ("dp", "ctx")),
        P(("dp", "ctx"), None),
        P(("dp", "ctx"), None),
        P(("dp", "ctx"), None),
        P(("dp", "ctx"), None),
        P(None, ("dp", "ctx")),
        P(None, ("dp", "ctx")),
        P(("dp", "ctx"), None),
        P(("dp", "ctx"), None),
        P(("dp", "ctx"), None),
        P(("dp", "ctx"), None),
        P(None, ("dp", "ctx")),
        P(None, ("dp", "ctx")),
        P(),
    )
    return jax.shard_map(local, mesh=mesh, in_specs=in_specs, out_specs=out_specs, check_vma=False)
```

```python
from functools import partial

import jax
import jax.numpy as jnp
from jax import lax
from jax.experimental import pallas as pl
from jax.experimental.pallas import tpu as pltpu
from jax.sharding import PartitionSpec as P

D = 1152
H = 4
HD = 256
FF = 6912
STEP = 10

EPSILON = 1e-06
ROPE_BASE = 1000000.0
BETA_ONE = 0.9
BETA_TWO = 0.95
ADAM_EPSILON = 1e-08
WEIGHT_DECAY = 0.1
GAIN_RATE = 1.0


def rope_tables(offsets, width):
    half = width // 2
    freq = jnp.exp(-jnp.log(ROPE_BASE) * jnp.arange(half, dtype=jnp.float32) * (2.0 / width))
    angle = offsets.astype(jnp.float32)[:, None] * freq[None, :]
    return (jnp.cos(angle), jnp.sin(angle))


def adam_update(weight, first, second, grad, rate, decay):
    first_new = BETA_ONE * first + (1.0 - BETA_ONE) * grad
    second_new = BETA_TWO * second + (1.0 - BETA_TWO) * grad * grad
    first_hat = first_new / (1.0 - BETA_ONE**STEP)
    second_hat = second_new / (1.0 - BETA_TWO**STEP)
    updated = weight - rate * (first_hat / (jnp.sqrt(second_hat) + ADAM_EPSILON) + decay * weight)
    return (updated, first_new, second_new)


def exchange(parts, axis):
    return lax.all_to_all(parts, axis, split_axis=0, concat_axis=0, tiled=True)


def swap(value, bit):
    count = lax.axis_size("ctx")
    return lax.ppermute(value, "ctx", [(i, i ^ bit) for i in range(count)])


def swap_dp(value, bit):
    count = lax.axis_size("dp")
    return lax.ppermute(value, "dp", [(i, i ^ bit) for i in range(count)])


def gather_ctx(block):
    far = swap(block, 2)
    return [block, swap(block, 1), far, swap(far, 1)]


def add_low(a, b):
    return a + b


def reduce_ctx(blocks):
    near, far = jnp.concatenate([blocks[1], blocks[3]]), None
    near = swap(near, 1)
    size = blocks[0].shape[0]
    far = swap(add_low(blocks[2], near[size:]), 2)
    mine = blocks[0].astype(jnp.float32) + near[:size].astype(jnp.float32)
    return mine + far.astype(jnp.float32)


def reorder(value, bit, rows):
    parts = [value[j * rows : (j + 1) * rows] for j in range(value.shape[0] // rows)]
    return jnp.concatenate([parts[j ^ bit] for j in range(len(parts))])


def sum_others(value):
    value = value + swap(value, 1)
    bit = 1
    while bit < lax.axis_size("dp"):
        value = value + swap_dp(value, bit)
        bit *= 2
    return value


def tie(value, *tokens):
    return lax.optimization_barrier((value, *tokens))[0]


class Ring:
    def __init__(self):
        count = self.count = lax.axis_size("dp")
        self.ctx = lax.axis_size("ctx")
        self.order = list(range(0, count, 2)) + list(range(count - 1, 0, -2))
        self.hops = (count // 2, count - 1 - count // 2)
        table = [
            [self.order[(self.order.index(i) + sense * step) % count] for step in range(count)]
            for sense in (1, -1)
            for i in range(count)
        ]
        row = (lax.axis_index("ctx") % 2) * count + lax.axis_index("dp")
        self.places = lax.dynamic_slice(
            jnp.array(table, jnp.int32), (row, 0), (1, count), allow_negative_indices=False
        )[0]

    def send(self, value, way):
        pairs = []
        for place, source in enumerate(self.order):
            for c in range(self.ctx):
                target = self.order[(place + (way if c % 2 == 0 else -way)) % self.count]
                pairs.append((source * self.ctx + c, target * self.ctx + c))
        return lax.ppermute(value, ("dp", "ctx"), pairs)

    def ways(self, hop):
        return [way for way, last in zip((1, -1), self.hops) if hop <= last]


class Gather:
    def __init__(self, ring, block):
        self.ring, self.hop = ring, 0
        self.held = {1: block, -1: block}
        self.parts, self.steps = [block], [0]

    def advance(self, *tokens):
        self.hop += 1
        for way in self.ring.ways(self.hop):
            self.held[way] = self.ring.send(tie(self.held[way], *tokens), way)
            self.parts.append(self.held[way])
            self.steps.append(-way * self.hop % self.ring.count)
        return list(self.held.values())

    def finish(self):
        while self.hop < self.ring.hops[0]:
            self.advance()
        return self

    def whole(self):
        block = self.parts[0]
        rows = block.shape[0]
        found = jnp.zeros((rows * self.ring.count, block.shape[1]), block.dtype)
        starts = self.ring.places * rows
        for step, part in zip(self.steps, self.parts):
            found = lax.dynamic_update_slice(
                found, part, (starts[step], 0), allow_negative_indices=False
            )
        return found


class Reduce:
    def __init__(self, ring, whole):
        self.ring, self.source, self.hop = ring, whole, ring.hops[0]
        self.rows = whole.shape[0] // ring.count
        self.starts = ring.places * self.rows
        self.held = {way: self.piece(way * last) for way, last in zip((1, -1), ring.hops)}
        self.total = None

    def piece(self, step):
        return lax.dynamic_slice(
            self.source,
            (self.starts[step % self.ring.count], 0),
            (self.rows, self.source.shape[1]),
            allow_negative_indices=False,
        )

    def tokens(self):
        return list(self.held.values())

    def send(self, *tokens):
        self.came = {
            way: self.ring.send(tie(self.held[way], *tokens), way) for way in self.ring.ways(self.hop)
        }
        return self

    def absorb(self, *tokens):
        for way, came in self.came.items():
            came = tie(came, *tokens) if tokens else came
            if self.hop > 1:
                self.held[way] = add_low(came, self.piece(way * (self.hop - 1)))
            else:
                mine = self.piece(0) if self.total is None else self.total
                self.total = mine.astype(jnp.float32) + came.astype(jnp.float32)
        self.hop -= 1
        return self.tokens() if self.total is None else [self.total]

    def finish(self):
        while self.hop > 0:
            self.send().absorb()
        return self.total


LOW = jnp.bfloat16
F32 = jnp.float32
TILE = 256
LONG = 6
SHORT = 2
GELU_A = 0.7978845608028654
GELU_B = 0.044715
VMEM = 36 * 2**20


def mm(a, b):
    return jnp.dot(a, b, preferred_element_type=F32)


def mm_nt(a, b):
    return lax.dot_general(a, b, (((1,), (1,)), ((), ())), preferred_element_type=F32)


def mm_tn(a, b):
    return lax.dot_general(a, b, (((0,), (0,)), ((), ())), preferred_element_type=F32)


def call(body, out_shape, in_specs, out_specs, args, grid=(1,), flops=0, scratch=(), into=(), prefetch=()):
    given = len(prefetch)
    used = len(in_specs)

    def kernel(*refs):
        body(*refs[: given + used], *refs[given + used + len(into) :])

    nbytes = sum(a.size * a.dtype.itemsize for a in args)
    nbytes += sum(o.size * o.dtype.itemsize for o in jax.tree.leaves(out_shape))
    return pl.pallas_call(
        kernel,
        out_shape=out_shape,
        grid_spec=pltpu.PrefetchScalarGridSpec(
            num_scalar_prefetch=given,
            grid=grid,
            in_specs=list(in_specs) + [pl.BlockSpec(memory_space=pl.ANY)] * len(into),
            out_specs=out_specs,
            scratch_shapes=list(scratch),
        ),
        compiler_params=pltpu.CompilerParams(vmem_limit_bytes=VMEM),
        cost_estimate=pl.CostEstimate(flops=flops // 16, bytes_accessed=nbytes // 16, transcendentals=0),
        input_output_aliases={given + used + i: i for i in range(len(into))},
    )(*prefetch, *args, *into)


def held(shape):
    return pl.BlockSpec(shape, lambda *_: (0,) * len(shape), pipeline_mode=pl.Buffered(1))


def like(shape, dtype):
    return jax.ShapeDtypeStruct(shape, dtype)


def scale_of(v):
    return lax.rsqrt(jnp.mean(v * v, axis=-1, keepdims=True) + EPSILON)


def norm_pull(v, s, g, dy):
    w = dy * g
    return s * w - v * (s * s * s) * jnp.mean(w * v, axis=-1, keepdims=True)


def turn(v, cos_t, sin_t, sign):
    half = v.shape[-1] // 2
    a, b = v[:, :half], v[:, half:]
    return jnp.concatenate([a * cos_t - sign * (b * sin_t), b * cos_t + sign * (a * sin_t)], axis=-1)


def stored_block(p):
    return jnp.where(p < 4, 2 * p, 2 * (7 - p) + 1)


def padded(rows):
    return -(-rows // 16) * 16


def pack_columns(w_gate_up, dp, ctx):
    rows, wide = w_gate_up.shape
    ff = wide // 2
    step = ff // (dp * ctx)
    room = padded(step)
    part = dp * room

    def body(w, out):
        zeros = [jnp.zeros((rows, room - step), F32)] if room > step else []
        for c in range(ctx):
            for side in range(2):
                cut = []
                for d in range(dp):
                    at = side * ff + (d * ctx + c) * step
                    cut += [w[:, at : at + step]] + zeros
                out[c, :, side * part : (side + 1) * part] = jnp.concatenate(cut, axis=1).astype(LOW)

    return call(
        body,
        like((ctx, rows, 2 * part), LOW),
        [held((rows, wide))],
        held((ctx, rows, 2 * part)),
        (w_gate_up,),
    )


def unpack_columns(parts, dp, ctx, step):
    rows, wide = parts.shape[1], parts.shape[2]
    part = wide // 2
    room = part // dp
    ff = dp * ctx * step

    def body(p, out):
        for c in range(ctx):
            own = p[c].astype(F32)
            for side in range(2):
                for d in range(dp):
                    at = side * ff + (d * ctx + c) * step
                    start = side * part + d * room
                    out[:, at : at + step] = own[:, start : start + step]

    return call(
        body,
        like((rows, 2 * ff), F32),
        [held(parts.shape)],
        held((rows, 2 * ff)),
        (parts,),
    )


class Blocks:
    def __init__(self, gathered, rows=None):
        block, self.cols = gathered.parts[0].shape
        self.rows = rows = rows or block
        count = gathered.ring.count
        self.height = rows * count
        if rows % 16:
            whole = gathered.whole().reshape(count, block, self.cols)[:, :rows]
            self.parts, self.steps = [whole.reshape(self.height, self.cols)], [0]
            self.rows = self.height
        else:
            self.parts, self.steps = gathered.parts, gathered.steps

    def specs(self):
        return [pl.BlockSpec(memory_space=pl.ANY)] * len(self.parts)

    def scratch(self):
        return [
            pltpu.VMEM((self.height, self.cols), LOW),
            pltpu.SemaphoreType.DMA((len(self.parts),)),
        ]

    def load(self, places, refs, room, sems):
        @pl.when(pl.program_id(0) == 0)
        def _():
            copies = []
            for i, (step, ref) in enumerate(zip(self.steps, refs)):
                at = pl.multiple_of(places[step] * self.rows, 16) if len(refs) > 1 else 0
                copies.append(
                    pltpu.make_async_copy(
                        ref.at[pl.ds(0, self.rows), :], room.at[pl.ds(at, self.rows), :], sems.at[i]
                    )
                )
            for copy in copies:
                copy.start()
            for copy in copies:
                copy.wait()


def unpack_small(gathered, first, dp, ctx, out_rows, gain_cols, head_cols):
    block, wide = gathered.parts[0].shape
    rows = block - first
    direct = first % 16 == 0 and rows % 16 == 0
    if direct:
        parts, steps = gathered.parts, gathered.steps
    else:
        parts, steps = [gathered.whole().reshape(dp, block, wide)[:, first:]], [0]
    half = out_rows // 2
    count = len(parts)

    def body(places, *refs):
        gain, head, out, room, sems = refs[count:]
        copies = []
        for i, ref in enumerate(refs[:count]):
            if direct:
                source, target = ref.at[pl.ds(first, rows), :], room.at[places[steps[i]]]
            else:
                source, target = ref, room
            copies.append(pltpu.make_async_copy(source, target, sems.at[i]))
        for copy in copies:
            copy.start()
        for copy in copies:
            copy.wait()
        lines = []
        for d in range(dp):
            extra = room[d, : 4 * ctx, :].astype(F32)
            lines += [extra[4 * c : 4 * c + 1] for c in range(ctx)]
            at, own = d * out_rows, room[d, 4 * ctx :, :]
            out[at : at + out_rows, :wide] = own[:out_rows]
            out[at : at + half, wide:] = own[out_rows:, : D - wide]
            out[at + half : at + out_rows, wide:] = own[out_rows:, D - wide :]
        for g in range(4):
            cut = [line[:, g * gain_cols : (g + 1) * gain_cols] for line in lines]
            gain[g : g + 1, :] = jnp.concatenate(cut, axis=1)
        for g in range(2):
            at = 4 * gain_cols + g * head_cols
            cut = [line[:, at : at + head_cols] for line in lines]
            head[g : g + 1, :] = jnp.concatenate(cut, axis=1)

    return call(
        body,
        [like((4, D), F32), like((2, HD), F32), like((HD, D), LOW)],
        [pl.BlockSpec(memory_space=pl.ANY)] * count,
        [held((4, D)), held((2, HD)), held((HD, D))],
        tuple(parts),
        scratch=[pltpu.VMEM((dp, rows, wide), LOW), pltpu.SemaphoreType.DMA((count,))],
        prefetch=(gathered.ring.places,),
    )


def input_stage(x, w_in, gain, head_rows, cos_t, sin_t, row_map, places):
    seq = x.shape[0]
    count = len(w_in.parts)

    def body(_, pl_ref, x0, x1, g, hg, cos, sin, *refs):
        q, k, v, raw, n_ref, w, sems = refs[count:]
        w_in.load(pl_ref, refs[:count], w, sems)
        for i, x_ref in enumerate((x0, x1)):
            at = slice(i * TILE, (i + 1) * TILE)
            xf = x_ref[...].astype(F32)
            n = (xf * scale_of(xf) * g[...]).astype(LOW)
            n_ref[at, :] = n
            y = mm(n, w[...])
            qy, ky = y[:, :HD], y[:, HD : 2 * HD]
            raw[at, :] = y[:, : 2 * HD]
            c, s = cos[at, :], sin[at, :]
            q[at, :] = turn(qy * scale_of(qy) * hg[0:1], c, s, 1.0).astype(LOW)
            k[at, :] = turn(ky * scale_of(ky) * hg[1:2], c, s, 1.0).astype(LOW)
            v[at, :] = y[:, 2 * HD :].astype(LOW)

    def block(cols):
        return pl.BlockSpec((2 * TILE, cols), lambda p, m, s: (p, 0))

    return call(
        body,
        [like((seq, HD), LOW)] * 3 + [like((seq, 2 * HD), F32), like((seq, D), LOW)],
        [
            pl.BlockSpec((TILE, D), lambda p, m, s: (m[2 * p], 0)),
            pl.BlockSpec((TILE, D), lambda p, m, s: (m[2 * p + 1], 0)),
            held((1, D)),
            held((2, HD)),
            block(HD // 2),
            block(HD // 2),
        ]
        + w_in.specs(),
        [block(HD)] * 3 + [block(2 * HD), block(D)],
        (x, x, gain, head_rows, cos_t, sin_t, *w_in.parts),
        grid=(seq // TILE // 2,),
        flops=2 * seq * D * 3 * HD,
        scratch=w_in.scratch(),
        prefetch=(row_map, places),
    )


def scores_of(q, k, doc_step):
    s = mm_nt(q, k) * HD ** (-0.5)
    row = lax.broadcasted_iota(jnp.int32, s.shape, 0) + doc_step * TILE
    col = lax.broadcasted_iota(jnp.int32, s.shape, 1)
    return jnp.where(col <= row, s, -1e30)


def attention(q, k, v, base):
    seq = q.shape[0]

    def body(b, q_ref, k_ref, v_ref, mixed, lse):
        for doc, count in enumerate((LONG, SHORT)):
            first = b[doc]
            for i in range(count):
                p = first + i
                at = pl.ds(pl.multiple_of(p * TILE, TILE), TILE)
                keys = pl.ds(pl.multiple_of(first * TILE, TILE), (i + 1) * TILE)
                s = scores_of(q_ref[at, :], k_ref[keys, :], i)
                peak = jnp.max(s, axis=-1, keepdims=True)
                e = jnp.exp(s - peak)
                total = jnp.sum(e, axis=-1, keepdims=True)
                lse[at, :] = peak + jnp.log(total)
                probs = (e * (1.0 / total)).astype(LOW)
                to = pl.ds(pl.multiple_of(stored_block(p) * TILE, TILE), TILE)
                mixed[to, :] = mm(probs, v_ref[keys, :]).astype(LOW)

    return call(
        body,
        [like((seq, HD), LOW), like((seq, 1), F32)],
        [held((seq, HD))] * 3,
        [held((seq, HD)), held((seq, 1))],
        (q, k, v),
        flops=4 * 24 * TILE * TILE * HD,
        prefetch=(base,),
    )


def attention_back(q, k, v, raw, lse, grads, head_rows, cos_t, sin_t, base):
    seq = q.shape[0]
    chip = seq // 2

    def pull_head(v_raw, g, dy, cos, sin):
        dy = turn(dy, cos, sin, -1.0)
        s = scale_of(v_raw)
        return norm_pull(v_raw, s, g, dy), jnp.sum(dy * v_raw * s, axis=0, keepdims=True)

    def body(b, q_ref, k_ref, v_ref, raw_ref, l_ref, *refs):
        hg, cos, sin, out, head_out, dk, dv, mixed_grad = refs[6:]
        for i in range(2):
            mine, near, far = refs[3 * i : 3 * i + 3]
            rows = pl.ds(pl.multiple_of((b[2] if i == 0 else 1 - b[2]) * chip, chip), chip)
            mixed_grad[rows, :] = (
                mine[0].astype(F32) + near[0].astype(F32) + far[...].astype(F32)
            ).astype(LOW)
        dk[...] = jnp.zeros_like(dk)
        dv[...] = jnp.zeros_like(dv)
        head_q = jnp.zeros((1, HD), F32)
        for doc, count in enumerate((LONG, SHORT)):
            first = b[doc]
            for i in range(count):
                p = first + i
                at = pl.ds(pl.multiple_of(p * TILE, TILE), TILE)
                keys = pl.ds(pl.multiple_of(first * TILE, TILE), (i + 1) * TILE)
                src = pl.ds(pl.multiple_of(stored_block(p) * TILE, TILE), TILE)
                do = mixed_grad[src, :]
                qs = q_ref[at, :]
                probs = jnp.exp(scores_of(qs, k_ref[keys, :], i) - l_ref[at, :])
                dp = mm_nt(do, v_ref[keys, :])
                inner = jnp.sum(probs * dp, axis=-1, keepdims=True)
                ds = (probs * (dp - inner)).astype(LOW)
                dq = mm(ds, k_ref[keys, :]) * HD ** (-0.5)
                dk[keys, :] += mm_tn(ds, qs)
                dv[keys, :] += mm_tn(probs.astype(LOW), do)
                dq, part = pull_head(raw_ref[at, :HD], hg[0:1], dq, cos[at, :], sin[at, :])
                head_q += part
                out[at, :HD] = dq.astype(LOW)
        head_k = jnp.zeros((1, HD), F32)
        for p in range(seq // TILE):
            at = slice(p * TILE, (p + 1) * TILE)
            dkp, part = pull_head(
                raw_ref[at, HD:], hg[1:2], dk[at, :] * HD ** (-0.5), cos[at, :], sin[at, :]
            )
            head_k += part
            out[at, HD : 2 * HD] = dkp.astype(LOW)
            out[at, 2 * HD :] = dv[at, :].astype(LOW)
        head_out[0:1, :] = head_q
        head_out[1:2, :] = head_k

    pair = pl.BlockSpec((1, chip, HD), lambda *_: (0, 0, 0), pipeline_mode=pl.Buffered(1))
    return call(
        body,
        [like((seq, 3 * HD), LOW), like((2, HD), F32)],
        [held((seq, HD))] * 3
        + [held((seq, 2 * HD)), held((seq, 1))]
        + [pair, pair, held((chip, HD))] * 2
        + [held((2, HD))]
        + [held((seq, HD // 2))] * 2,
        [held((seq, 3 * HD)), held((2, HD))],
        (q, k, v, raw, lse, *grads, head_rows, cos_t, sin_t),
        flops=10 * 24 * TILE * TILE * HD,
        scratch=[pltpu.VMEM((seq, HD), F32)] * 2 + [pltpu.VMEM((seq, HD), LOW)],
        prefetch=(base,),
    )


def project(mixed, outs, x, gains, stored_map):
    seq = x.shape[0]

    def body(_, m0, m1, m2, m3, w0, w1, w2, w3, x_ref, g, proj, pre):
        for i in range(2):
            at = slice(i * TILE, (i + 1) * TILE)
            y = mm(m0[at, :], w0[...]) + mm(m1[at, :], w1[...])
            y = y + mm(m2[at, :], w2[...]) + mm(m3[at, :], w3[...])
            proj[at, :] = y
            r = x_ref[at, :].astype(F32) + y * scale_of(y) * g[1:2]
            pre[at, :] = (r * scale_of(r) * g[2:3]).astype(LOW)

    def block(cols):
        return pl.BlockSpec((2 * TILE, cols), lambda r, m: (r, 0))

    return call(
        body,
        [like((seq, D), F32), like((seq, D), LOW)],
        [pl.BlockSpec((2 * TILE, HD), lambda r, m: (m[2 * r] // 2, 0))] * 4
        + [held((HD, D))] * 4
        + [block(D), held((4, D))],
        [block(D), block(D)],
        (*mixed, *outs, x, gains),
        grid=(seq // TILE // 2,),
        flops=2 * seq * D * H * HD,
        prefetch=(stored_map,),
    )


def column_cuts(main, width):
    return [(at, min(width, main - at)) for at in range(0, main, width)]


def gate_stage(pre, w, places, half, into=()):
    seq, part = pre.shape[0], w.cols // 2
    rows = 512
    first = half * (seq // 2 // rows)
    count = len(w.parts)

    def pieces(g, u):
        t = jnp.tanh(GELU_A * (g + GELU_B * (g * g * g)))
        a = 0.5 * g * (1.0 + t)
        slope = 0.5 * (1.0 + t) + (0.5 * g) * (1.0 - t * t) * (GELU_A * (1.0 + 3.0 * GELU_B * (g * g)))
        return a * u, u * slope, a

    def body(pl_ref, p_ref, *refs):
        hidden, ab, room, sems = refs[count:]
        w.load(pl_ref, refs[:count], room, sems)
        p = p_ref[...]

        def multiply(at, wide):
            return mm(p, room[:, at : at + wide]), mm(p, room[:, part + at : part + at + wide])

        def finish(at, wide, made):
            h, b, a = pieces(*made)
            hidden[:, at : at + wide] = h.astype(LOW)
            ab[:, at : at + wide] = b.astype(LOW)
            ab[:, part + at : part + at + wide] = a.astype(LOW)

        last = None
        for cut in column_cuts(part, 256):
            made = multiply(*cut)
            if last is not None:
                finish(*last)
            last = (*cut, made)
        finish(*last)

    def block(cols):
        return pl.BlockSpec((rows, cols), lambda r, m: (first + r, 0))

    return call(
        body,
        [like((seq, part), LOW), like((seq, 2 * part), LOW)],
        [block(D)] + w.specs(),
        [block(part), block(2 * part)],
        (pre, *w.parts),
        grid=(seq // 2 // rows,),
        flops=2 * seq * D * part,
        scratch=w.scratch(),
        into=into,
        prefetch=(places,),
    )


def down_stage(hidden, w, places, half):
    seq, part = hidden.shape
    rows = seq // 4
    count = len(w.parts)

    def body(pl_ref, h, *refs):
        even, odd, room, sems = refs[count:]
        w.load(pl_ref, refs[:count], room, sems)
        odd[...] = mm(h[rows:, :], room[...]).astype(LOW)
        even[...] = mm(h[:rows, :], room[...]).astype(LOW)

    return call(
        body,
        [like((rows, D), LOW)] * 2,
        [
            pl.BlockSpec(
                (2 * rows, part), lambda r, m: (half, 0), pipeline_mode=pl.Buffered(1)
            )
        ]
        + w.specs(),
        [held((rows, D))] * 2,
        (hidden, *w.parts),
        flops=4 * rows * D * part,
        scratch=w.scratch(),
        prefetch=(places,),
    )


def ffn_stage(parts, near, far, proj, x, cot, gains):
    rows = cot.shape[0]

    def body(p, n, f, proj_ref, x_ref, c_ref, g, out, grad, gain):
        y = p[...].astype(F32) + n[...].astype(F32) + f[...].astype(F32)
        pr = proj_ref[...]
        s = scale_of(y)
        r = x_ref[...].astype(F32) + pr * scale_of(pr) * g[1:2]
        out[...] = (r + y * s * g[3:4]).astype(LOW)
        dy = c_ref[...].astype(F32)
        grad[...] = norm_pull(y, s, g[3:4], dy).astype(LOW)
        part = jnp.sum(dy * y * s, axis=0, keepdims=True)

        @pl.when(pl.program_id(0) == 0)
        def _():
            gain[...] = part

        @pl.when(pl.program_id(0) > 0)
        def _():
            gain[...] += part

    block = pl.BlockSpec((TILE, D), lambda r: (r, 0))
    return call(
        body,
        [like((rows, D), LOW), like((rows, D), LOW), like((1, D), F32)],
        [block] * 6 + [held((4, D))],
        [block, block, held((1, D))],
        (parts, near, far, proj, x, cot, gains),
        grid=(rows // TILE,),
    )


def hidden_back(grad, w, ab, places, half, into=()):
    seq, part = ab.shape[0], ab.shape[1] // 2
    rows = 512
    first = half * (seq // 2 // rows)
    count = len(w.parts)

    def body(pl_ref, g_ref, ab_ref, *refs):
        out, room, sems = refs[count:]
        w.load(pl_ref, refs[:count], room, sems)
        g = g_ref[...]
        for at, wide in column_cuts(part, 256):
            hg = mm_nt(g, room[at : at + wide, :])
            for side in (at, part + at):
                out[:, side : side + wide] = (hg * ab_ref[:, side : side + wide].astype(F32)).astype(LOW)

    def block(cols):
        return pl.BlockSpec((rows, cols), lambda r, m: (first + r, 0))

    return call(
        body,
        [like((seq, 2 * part), LOW)],
        [pl.BlockSpec((rows, D), lambda r, m: (r, 0)), block(2 * part)] + w.specs(),
        [block(2 * part)],
        (grad, ab, *w.parts),
        grid=(seq // 2 // rows,),
        flops=seq * D * part,
        scratch=w.scratch(),
        into=into,
        prefetch=(places,),
    )[0]


def residual_back(gu, w, outs, proj, x, cot, gains, stored_map, places, half, into=()):
    seq, wide = gu.shape
    own = cot.shape[0] // TILE
    steps = seq // 2 // TILE
    first = half * steps
    count = len(w.parts)

    def body(_, pl_ref, gu_ref, w0, w1, w2, w3, proj_ref, x_ref, c_ref, g, *refs):
        rg, pg, even, odd, gain, room, sems, *made = refs[count:]
        w.load(pl_ref, refs[:count], room, sems)
        step = pl.program_id(0)

        def multiply(turn):
            made[turn][...] = mm_nt(gu_ref[...], room[...])

        def finish(turn):
            dy = made[turn][...]
            pr = proj_ref[...]
            sp = scale_of(pr)
            r = x_ref[...].astype(F32) + pr * sp * g[1:2]
            s = scale_of(r)
            dr = norm_pull(r, s, g[2:3], dy)
            if half == 0:
                dr = dr + jnp.where(step <= own, 1.0, 0.0) * c_ref[...].astype(F32)
            rg[...] = dr.astype(LOW)
            low = norm_pull(pr, sp, g[1:2], dr).astype(LOW)
            pg[...] = low
            even[0] = mm_nt(low, w0[...]).astype(LOW)
            odd[0] = mm_nt(low, w1[...]).astype(LOW)
            even[1] = mm_nt(low, w2[...]).astype(LOW)
            odd[1] = mm_nt(low, w3[...]).astype(LOW)
            before = jnp.where(step == 1, 0.0, gain[...])
            gain[0:1, :] = before[0:1] + jnp.sum(dr * pr * sp, axis=0, keepdims=True)
            gain[1:2, :] = before[1:2] + jnp.sum(dy * r * s, axis=0, keepdims=True)

        @pl.when(step == 0)
        def _():
            multiply(0)

        for turn in range(2):

            @pl.when((step > 0) & (step < steps) & (step % 2 == turn))
            def _():
                multiply(turn)
                finish(1 - turn)

        @pl.when(step == steps)
        def _():
            finish((steps - 1) % 2)

    def last(i):
        return jnp.maximum(i - 1, 0)

    def block(cols):
        return pl.BlockSpec((TILE, cols), lambda i, m, p: (first + last(i), 0))

    heads = pl.BlockSpec((2, TILE, HD), lambda i, m, p: (0, m[first + last(i)] % steps, 0))
    return call(
        body,
        [like((seq, D), LOW), like((seq, D), LOW)]
        + [like((2, seq // 2, HD), LOW)] * 2
        + [like((2, D), F32)],
        [pl.BlockSpec((TILE, wide), lambda i, m, p: (first + jnp.minimum(i, steps - 1), 0))]
        + [held((HD, D))] * 4
        + [block(D), block(D)]
        + [pl.BlockSpec((TILE, D), lambda i, m, p: (jnp.minimum(last(i), own - 1), 0)), held((4, D))]
        + w.specs(),
        [
            block(D),
            pl.BlockSpec((TILE, D), lambda i, m, p: (m[first + last(i)], 0)),
            heads,
            heads,
            held((2, D)),
        ],
        (gu, *outs, proj, x, cot, gains, *w.parts),
        grid=(steps + 1,),
        flops=seq * D * (wide + H * HD),
        scratch=w.scratch() + [pltpu.VMEM((TILE, D), F32)] * 2,
        into=into,
        prefetch=(stored_map, places),
    )


def input_back(qkv, w_in, x, rg, gain, pos_map, places):
    seq = x.shape[0]
    rows = 2 * TILE
    count = len(w_in.parts)

    def body(_, pl_ref, q0, q1, x_ref, rg_ref, g, *refs):
        even, odd, gain_out, w, sems = refs[count:]
        w_in.load(pl_ref, refs[:count], w, sems)
        step = pl.program_id(0)
        total = jnp.zeros((1, D), F32)
        made = []
        for i, q_ref in enumerate((q0, q1)):
            at = slice(i * TILE, (i + 1) * TILE)
            dy = mm_nt(q_ref[...], w[...])
            xf = x_ref[at, :].astype(F32)
            s = scale_of(xf)
            made.append((rg_ref[at, :].astype(F32) + norm_pull(xf, s, g[...], dy)).astype(LOW))
            total += jnp.sum(dy * xf * s, axis=0, keepdims=True)
        gain_out[...] = jnp.where(step == 0, 0.0, gain_out[...]) + total

        @pl.when(step % 2 == 0)
        def _():
            even[:TILE, :], even[TILE:, :] = made

        @pl.when(step % 2 == 1)
        def _():
            odd[:TILE, :], odd[TILE:, :] = made

    block = pl.BlockSpec((rows, D), lambda i, m, s: (i, 0))
    out = pl.BlockSpec((rows, D), lambda i, m, s: (i // 2, 0))
    return call(
        body,
        [like((seq // 2, D), LOW)] * 2 + [like((1, D), F32)],
        [
            pl.BlockSpec((TILE, 3 * HD), lambda i, m, s: (m[2 * i], 0)),
            pl.BlockSpec((TILE, 3 * HD), lambda i, m, s: (m[2 * i + 1], 0)),
            block,
            block,
            held((1, D)),
        ]
        + w_in.specs(),
        [out, out, held((1, D))],
        (qkv, qkv, x, rg, gain, *w_in.parts),
        grid=(seq // rows,),
        flops=2 * seq * D * 3 * HD,
        scratch=w_in.scratch(),
        prefetch=(pos_map, places),
    )


def local(
    tokens,
    cotangent,
    lengths,
    w_qkv,
    w_out,
    w_gate_up,
    w_down,
    gains,
    head_gains,
    first_qkv,
    first_out,
    first_gate_up,
    first_down,
    first_gains,
    first_head,
    second_qkv,
    second_out,
    second_gate_up,
    second_down,
    second_gains,
    second_head,
):
    low = jnp.bfloat16
    f32 = jnp.float32
    rows = tokens.shape[1]
    dp = lax.axis_size("dp")
    ctx = lax.axis_size("ctx")
    place = lax.axis_index("ctx")
    seq = rows * ctx
    in_rows = w_qkv.shape[0]
    out_rows = w_out.shape[0]
    ff_rows = w_down.shape[0]
    gain_cols = gains.shape[1]
    head_cols = head_gains.shape[1]
    qkv_cols = 3 * HD
    ring = Ring()

    q_cols = w_qkv[:, : H * HD].astype(low).reshape(in_rows, ctx, HD).transpose(1, 0, 2)
    kv_cols = jnp.broadcast_to(w_qkv[:, H * HD :].astype(low)[None], (ctx, in_rows, 2 * HD))
    extra = jnp.concatenate(
        [gains.astype(low).reshape(-1), head_gains.astype(low).reshape(-1)]
    )
    extra = jnp.pad(extra, (0, 4 * qkv_cols - extra.shape[0])).reshape(4, qkv_cols)
    small_sent = jnp.concatenate(
        [
            jnp.concatenate([q_cols, kv_cols], axis=2),
            jnp.broadcast_to(extra[None], (ctx, 4, qkv_cols)),
        ],
        axis=1,
    )
    to_user = [((dp * c + d), d * ctx + c) for d in range(dp) for c in range(ctx)]
    to_owner = [(b, a) for a, b in to_user]
    out_mine = lax.ppermute(w_out.astype(low), ("dp", "ctx"), to_user)
    half = out_rows // 2
    small = exchange(small_sent, "ctx")
    packed = pack_columns(tie(w_gate_up, small_sent), dp, ctx)
    own_rows = ctx * in_rows
    small_ring = Gather(
        ring,
        jnp.concatenate(
            [
                small[:, :in_rows].reshape(own_rows, qkv_cols),
                small[:, in_rows:].reshape(4 * ctx, qkv_cols),
                out_mine[:, :qkv_cols],
                jnp.concatenate([out_mine[:half, qkv_cols:], out_mine[half:, qkv_cols:]], axis=1),
            ]
        ),
    )
    down_block = jnp.pad(w_down.astype(low), ((0, padded(ff_rows) - ff_rows), (0, 0)))
    down_ring = Gather(ring, down_block)
    down_first = down_ring.advance()
    tokens_far = swap(tie(tokens[0], small), 2)
    tokens_near = swap(tie(tokens[0], small), 1)
    gate_up_cols = exchange(tie(packed, tokens_far), "ctx").reshape(own_rows, -1)
    first_len = lengths[0, 0]
    pos = tie(jnp.arange(seq, dtype=jnp.int32), packed)
    cos_t, sin_t = rope_tables(pos - jnp.where(pos < first_len, 0, first_len), HD)
    small_ring.advance(*down_first)
    small_ring.advance(cos_t, sin_t)
    tokens_last = swap(tie(tokens_far, *small_ring.held.values()), 1)
    tokens_all = jnp.concatenate([tokens[0], tokens_near, tokens_far, tokens_last])
    while small_ring.hop < ring.hops[0]:
        small_ring.advance()
    small_seen = list(small_ring.held.values())
    gate_ring = Gather(ring, gate_up_cols)
    gate_seen = gate_ring.advance(*small_seen, tokens_last)
    w_in = Blocks(small_ring, own_rows)
    places = ring.places
    gain_rows, head_rows, out_mine = unpack_small(
        small_ring, own_rows, dp, ctx, out_rows, gain_cols, head_cols
    )
    out_far, out_near = swap(out_mine, 2), swap(out_mine, 1)

    blocks = seq // TILE
    split = first_len // TILE
    base = jnp.where(split == LONG, jnp.array([0, LONG, 0]), jnp.array([SHORT, 0, 0]))
    base = (base + jnp.array([0, 0, 1]) * (place // 2)).astype(jnp.int32)
    tiles = jnp.arange(blocks, dtype=jnp.int32)
    stored_map = 2 * (place ^ (tiles // 2)) + tiles % 2
    owner = jnp.where(tiles < ctx, tiles, 2 * ctx - 1 - tiles)
    row_map = 2 * (place ^ owner) + (tiles >= ctx)
    pos_map = jnp.where(tiles % 2 == 0, stored_map // 2, 2 * ctx - 1 - stored_map // 2)

    q, k, v, raw, normed = input_stage(
        tokens_all, w_in, gain_rows[0:1], head_rows, cos_t, sin_t, row_map, places
    )
    down_second = down_ring.advance(q, *gate_seen)
    gate_second = gate_ring.advance(q)
    mixed, lse = attention(tie(q, *gate_seen, out_far, out_near), k, v, base)
    mixed = tie(mixed, *down_second)
    mixed_far, mixed_near = swap(mixed, 2), swap(mixed, 1)
    out_parts = [out_mine, out_near, out_far, swap(tie(out_far, mixed), 1)]
    down_ring.advance(mixed)
    gate_ring.advance(mixed)
    mixed_parts = [mixed, mixed_near, mixed_far, swap(tie(mixed_far, *gate_second), 1)]
    proj, pre_low = project(mixed_parts, out_parts, tokens_all, gain_rows, stored_map)
    while gate_ring.hop < ring.hops[0]:
        gate_ring.advance(pre_low)
        if down_ring.hop < ring.hops[0]:
            down_ring.advance(pre_low)
    down_ring.finish()
    full_gate_up = Blocks(gate_ring)
    full_down = Blocks(down_ring)
    buffers = gate_stage(pre_low, full_gate_up, places, 1)
    even, odd = down_stage(buffers[0], full_down, places, 1)
    summed = add_low(even, swap(odd, 1))
    far = swap(summed, 2)
    hidden_low, slopes = gate_stage(tie(pre_low, summed), full_gate_up, places, 0, buffers)
    even, odd = down_stage(tie(hidden_low, far), full_down, places, 0)
    near = swap(odd, 1)
    result, ffn_grad, gain_grad_d = ffn_stage(
        even, near, far, proj, tokens[0], cotangent[0], gain_rows
    )

    far = swap(ffn_grad, 2)
    ffn_here = jnp.concatenate([ffn_grad, swap(ffn_grad, 1)])
    residual = partial(
        residual_back,
        w=full_gate_up,
        outs=out_parts,
        proj=proj,
        x=tokens_all,
        cot=cotangent[0],
        gains=gain_rows,
        stored_map=stored_map,
        places=places,
    )
    gate_up_low = hidden_back(ffn_here, full_down, slopes, places, 0)
    far = tie(far, gate_up_low)
    ffn_there = jnp.concatenate([far, swap(far, 1)])
    gate_up_low = hidden_back(ffn_there, full_down, slopes, places, 1, (gate_up_low,))
    grad_gate_up = mm_tn(pre_low, gate_up_low).astype(low)
    gate_sum = Reduce(ring, grad_gate_up).send()
    resid_grad, proj_low, even, odd, gain_grad_here = residual(
        tie(gate_up_low, *gate_sum.tokens()), half=0
    )
    held_gate = gate_sum.absorb(resid_grad)
    near = swap(tie(odd, *held_gate), 1)
    parts_here = (even, near)
    summed = add_low(even[1], near[1])
    far_there = swap(summed, 2)
    gate_sum.send()
    ffn_low = jnp.concatenate([ffn_here, ffn_there])
    grad_down = mm_tn(hidden_low, tie(ffn_low, summed, *held_gate)).astype(low)
    down_sum = Reduce(ring, grad_down).send()
    resid_grad, proj_low, even, odd, gain_grad_there = residual(
        tie(gate_up_low, far_there, *down_sum.tokens()), half=1, into=(resid_grad, proj_low)
    )
    near = swap(tie(odd, *gate_sum.came.values(), *down_sum.came.values()), 1)
    summed = add_low(even[1], near[1])
    far_here = swap(summed, 2)
    held_gate = gate_sum.absorb(odd)
    held_down = down_sum.absorb(odd)
    gate_sum.send()
    down_sum.send()
    proj_low = tie(proj_low, *held_gate, *held_down)
    grad_out = [mm_tn(m, proj_low).astype(low) for m in mixed_parts]
    far_here = tie(far_here, *grad_out)
    grad_out = reduce_ctx(grad_out).astype(low)
    qkv_low, head_grads = attention_back(
        q,
        k,
        v,
        raw,
        lse,
        parts_here + (far_here,) + (even, near, far_there),
        head_rows,
        cos_t,
        sin_t,
        base,
    )
    grad_in = mm_tn(normed, qkv_low).astype(low)
    grad_out = grad_out.reshape(dp, out_rows, D)
    in_blocks = jnp.concatenate(
        [
            grad_in.reshape(dp, own_rows, qkv_cols),
            grad_out[:, :, :qkv_cols],
            jnp.concatenate(
                [grad_out[:, :half, qkv_cols:], grad_out[:, half:, qkv_cols:]], axis=2
            ),
        ],
        axis=1,
    )
    in_sum = Reduce(ring, in_blocks.reshape(-1, qkv_cols))
    held_gate = gate_sum.absorb(*in_sum.tokens())
    held_down = down_sum.absorb(*in_sum.tokens())
    in_sum.send()
    gate_sum.send()
    down_sum.send()
    held_in = in_sum.absorb(*held_gate, *held_down)
    in_sum.send()
    input_even, input_odd, gain_grad_a = input_back(
        tie(qkv_low, *held_in),
        w_in,
        tokens_all,
        resid_grad,
        gain_rows[0:1],
        pos_map,
        places,
    )
    gate_came = list(gate_sum.came.values())
    in_sum.absorb(input_odd)
    in_sum.send(*gate_came)
    gate_sum.absorb(input_odd)
    down_sum.absorb(input_odd)
    gate_up_own = gate_sum.finish().astype(low)
    gate_up_own = exchange(gate_up_own.reshape(ctx, in_rows, -1), "ctx")
    near = swap(tie(input_odd, *gate_came), 1)
    summed = add_low(input_even[rows:], near[rows:])
    gain_grad_bc = gain_grad_here + gain_grad_there
    while in_sum.hop > 1:
        in_sum.absorb()
        in_sum.send()

    in_own = in_sum.absorb()[0].astype(low)
    down_sum.send(in_own)
    down_sum.absorb()
    down_own = down_sum.finish()[:ff_rows]
    out_own = in_own[own_rows:]
    out_own = jnp.concatenate(
        [
            out_own[:out_rows],
            jnp.concatenate(
                [out_own[out_rows:, : D - qkv_cols], out_own[out_rows:, D - qkv_cols :]], axis=0
            ),
        ],
        axis=1,
    )
    out_low = lax.ppermute(out_own, ("dp", "ctx"), to_owner)
    out_own = out_low.astype(f32)
    in_own = exchange(
        tie(in_own[:own_rows], gate_up_own, down_own, out_low, summed).reshape(
            ctx, in_rows, qkv_cols
        ),
        "ctx",
    ).astype(f32)
    far = swap(tie(summed, gate_up_own, in_own), 2)
    input_grad = (
        input_even[:rows].astype(f32) + near[:rows].astype(f32) + far.astype(f32)
    )
    gate_up_own = unpack_columns(gate_up_own, dp, ctx, ff_rows)
    qkv_own = jnp.concatenate(
        [
            in_own[:, :, :HD].transpose(1, 0, 2).reshape(in_rows, H * HD),
            jnp.sum(in_own[:, :, HD:], axis=0),
        ],
        axis=1,
    )
    gain_grads = jnp.concatenate([gain_grad_a, gain_grad_bc, gain_grad_d], axis=0)
    local_squares = jnp.float32(0.0)
    for piece in (qkv_own, out_own, gate_up_own, down_own):
        local_squares = local_squares + jnp.sum(piece * piece)
    lines = jnp.concatenate([gain_grads.reshape(-1, 128), head_grads.reshape(-1, 128)])
    squares = jnp.pad(local_squares.reshape(1, 1), ((0, 7), (0, 127)))
    sums = sum_others(jnp.concatenate([lines, squares]))
    sums = sums + swap(tie(sums, far), 2)
    small_grads = sums[: lines.shape[0]]
    index = lax.axis_index("dp") * ctx + place
    gains_own = lax.dynamic_slice_in_dim(
        small_grads[: 4 * D // 128].reshape(4, D), index * gain_cols, gain_cols, axis=1
    )
    head_own = lax.dynamic_slice_in_dim(
        small_grads[4 * D // 128 :].reshape(2, HD), index * head_cols, head_cols, axis=1
    )
    reduced = (qkv_own, out_own, gate_up_own, down_own, gains_own, head_own)
    total_squares = sums[lines.shape[0], 0] + jnp.sum(small_grads * small_grads)
    grad_norm = jnp.sqrt(total_squares)
    factor = 1.0 / jnp.maximum(grad_norm, 1.0)
    weights = (w_qkv, w_out, w_gate_up, w_down, gains, head_gains)
    firsts = (first_qkv, first_out, first_gate_up, first_down, first_gains, first_head)
    seconds = (second_qkv, second_out, second_gate_up, second_down, second_gains, second_head)
    rates = (D ** (-0.5), (H * HD) ** (-0.5), D ** (-0.5), FF ** (-0.5), GAIN_RATE, GAIN_RATE)
    decays = (WEIGHT_DECAY, WEIGHT_DECAY, WEIGHT_DECAY, WEIGHT_DECAY, 0.0, 0.0)
    updates = [
        adam_update(
            weights[index],
            firsts[index],
            seconds[index],
            reduced[index] * factor,
            rates[index],
            decays[index],
        )
        for index in range(6)
    ]
    return (
        result[None],
        input_grad[None],
        updates[0][0],
        updates[1][0],
        updates[2][0],
        updates[3][0],
        updates[4][0],
        updates[5][0],
        updates[0][1],
        updates[1][1],
        updates[2][1],
        updates[3][1],
        updates[4][1],
        updates[5][1],
        updates[0][2],
        updates[1][2],
        updates[2][2],
        updates[3][2],
        updates[4][2],
        updates[5][2],
        grad_norm,
    )


def solution(mesh):
    in_specs = (
        P("dp", "ctx", None),
        P("dp", "ctx", None),
        P("dp", None),
        P(("dp", "ctx"), None),
        P(("dp", "ctx"), None),
        P(("dp", "ctx"), None),
        P(("dp", "ctx"), None),
        P(None, ("dp", "ctx")),
        P(None, ("dp", "ctx")),
        P(("dp", "ctx"), None),
        P(("dp", "ctx"), None),
        P(("dp", "ctx"), None),
        P(("dp", "ctx"), None),
        P(None, ("dp", "ctx")),
        P(None, ("dp", "ctx")),
        P(("dp", "ctx"), None),
        P(("dp", "ctx"), None),
        P(("dp", "ctx"), None),
        P(("dp", "ctx"), None),
        P(None, ("dp", "ctx")),
        P(None, ("dp", "ctx")),
    )
    out_specs = (
        P("dp", "ctx", None),
        P("dp", "ctx", None),
        P(("dp", "ctx"), None),
        P(("dp", "ctx"), None),
        P(("dp", "ctx"), None),
        P(("dp", "ctx"), None),
        P(None, ("dp", "ctx")),
        P(None, ("dp", "ctx")),
        P(("dp", "ctx"), None),
        P(("dp", "ctx"), None),
        P(("dp", "ctx"), None),
        P(("dp", "ctx"), None),
        P(None, ("dp", "ctx")),
        P(None, ("dp", "ctx")),
        P(("dp", "ctx"), None),
        P(("dp", "ctx"), None),
        P(("dp", "ctx"), None),
        P(("dp", "ctx"), None),
        P(None, ("dp", "ctx")),
        P(None, ("dp", "ctx")),
        P(),
    )
    return jax.shard_map(local, mesh=mesh, in_specs=in_specs, out_specs=out_specs, check_vma=False)
```
